32 devices in a mesh: seg: 2 (over y), bundle: 16 (over z, x, core).
Axes of the slice: x: 2, y: 2, z: 4, core: 2. Of those that a mesh axis runs over, the one named last changes fastest.
Arguments:
- conc: float32 [64, 16, 1024], P('bundle', None, 'seg'), may hold values from -6 to 6
- slowness: float32 [64, 1024], P('bundle', 'seg'), may hold values from 0 to 3
- retard: float32 [16], replicated, may hold values from 0.05 to 30.72
- taps: float32 [16, 33], replicated, may hold values from -0.12 to 0.12
- inlet: float32 [64, 16], P('bundle'), may hold values from -6 to 6
- grid: float32 [16, 65536], P(None, ('seg', 'bundle')), may hold values from -6 to 6
- kappa: float32 [65536], P(('seg', 'bundle')), may hold values from 0.05 to 0.5
- owners: int32 [2, 64, 4, 1], P('seg', 'bundle'), may hold values from 0 to 15; in each aligned block of 16 rows (0 to 15, 16 to 31, ..., all dimensions but the last counted through in order) at most 2 rows name the same one
- cells: int32 [64, 1024], P('bundle', 'seg'), may hold values from 0 to 2047
Outputs:
- conc_out: float32 [64, 16, 1024], P('bundle', None, 'seg')
- grid_out: float32 [16, 65536], P(None, ('seg', 'bundle'))
The draws below stay inside these ranges and needn't reach their ends.
Inputs may be any that keep to these rules, and one draw needn't show every extreme that they name: `owners`: among the node blocks of one device (one segment of 4 streamlines), at most 2 name the same owner.
All inputs are finite; a program needn't handle non-finite values.
Results may differ from the reference program's by a relative error of at most 0.00022.
Values sent between devices are 32-bit elements; how exact they have to be, the bound alone decides.
No kernel may reach another device: no remote copies, remote signals or barrier semaphores. Data moves between devices by JAX's collectives and lax.ppermute only.
A program may use at most 128 MiB of HBM per device.

```python
import math
import jax
import jax.numpy as jnp
import numpy as np
from jax import lax

COMP = 16
TAPS = 33
STEPS = 4
LINES_DEV = 4
CELLS_DEV = 2048
NBD = 4
CAP = 2
STREAMLINE_COUNT = 64
NODES_PER_LINE = 1024
CELLS = 65536
N_SEG = 2
N_BUNDLE = 16


def draw_slowness(key, part):
    key = jax.random.fold_in(key, 11)
    streamline_key, roughness_key, location_key, pulse_key = jax.random.split(key, 4)
    streamline_factor = jax.random.uniform(streamline_key, (STREAMLINE_COUNT, 1), jnp.float32, 0.5, 2.0)
    roughness_noise = jax.random.uniform(roughness_key, (STREAMLINE_COUNT, NODES_PER_LINE), jnp.float32, 0.5, 1.5)
    base_profile = 1.0 / NODES_PER_LINE
    pulse_location = jax.random.randint(location_key, (STREAMLINE_COUNT, 3), 0, NODES_PER_LINE)
    node_position = jnp.arange(NODES_PER_LINE, dtype=jnp.int32)
    pulse_hits = jnp.any(node_position[None, None, :] == pulse_location[:, :, None], axis=1)
    pulse_input = jax.random.uniform(pulse_key, (STREAMLINE_COUNT, NODES_PER_LINE), jnp.float32, 0.8, 3.0)
    return jnp.where(pulse_hits, pulse_input, base_profile * streamline_factor * roughness_noise).astype(jnp.float32)


def place_ends(result, stream_key, low, high):
    index_at = [jax.random.randint(jax.random.fold_in(stream_key, axis), (), 0, length) for axis, length in enumerate(result.shape)]
    widest = result.shape.index(max(result.shape))
    next_to = index_at[:widest] + [(index_at[widest] + 1) % result.shape[widest]] + index_at[widest + 1:]
    return result.at[tuple(index_at)].set(low).at[tuple(next_to)].set(high)


def levels(stream_key, shape, pieces, smallest, largest):
    level = 1.0
    for axis_at, shards_of in pieces:
        steps = jax.random.uniform(jax.random.fold_in(jax.random.fold_in(stream_key, 6), axis_at), (shards_of,), jnp.float32, smallest / len(pieces), largest / len(pieces))
        level = level * jnp.repeat(jnp.exp(steps), shape[axis_at] // shards_of).reshape((-1,) + (1,) * (len(shape) - 1 - axis_at))
    return level


def routed_block(key, own, number, rows, count, top, limit, lean):
    order = jax.random.permutation(key, count)
    heavy_load, usual = shares(count, rows * top, limit, lean, True), shares(count, rows * top, limit, lean, False)
    places = jnp.arange(count)

    def named(lengths, rotation):
        used = int((lengths > 0).sum())
        fixed = max(1, used // 4)
        passed = fixed + (places - fixed + rotation * (used - fixed)) % max(1, count - fixed)
        return jnp.zeros((count,), jnp.int32).at[order[jnp.where(places < fixed, places, passed)]].set(jnp.asarray(lengths, jnp.int32))

    lengths = jnp.where(number % 4 == 0, named(heavy_load, number // 4), named(usual, number - number // 4 - 1))
    mixed = jax.random.permutation(jax.random.fold_in(own, 3), count)
    giver, sink = mixed[0:count // 2 * 2:2], mixed[1:count // 2 * 2:2]
    margin = jnp.minimum(lengths[giver] - 1, limit - lengths[sink]) // 2
    margin = jnp.where((giver == order[0]) | (sink == order[0]) | (lengths[sink] == 0), 0, jnp.maximum(margin, 0))
    passed = jax.random.randint(jax.random.fold_in(own, 4), (count // 2,), 0, 1 << 20) % (margin + 1)
    lengths = lengths.at[giver].add(-passed).at[sink].add(passed)
    items = jnp.searchsorted(jnp.cumsum(lengths), jnp.arange(rows * top), side="right").astype(jnp.int32)
    listing = items.reshape(top, rows).T
    listing = listing[jax.random.permutation(jax.random.fold_in(own, 1), rows)]
    rotation = jax.random.randint(jax.random.fold_in(own, 2), (rows, 1), 0, top)
    return jnp.take_along_axis(listing, (jnp.arange(top)[None, :] + rotation) % top, axis=1)


def shares(number_of, total, limit, slope, full):
    weights = [(1 << 20) // math.isqrt(standing ** slope) + 1 for standing in range(1, number_of + 1)]
    largest = limit if full else min(limit, max(-(-total // number_of), total * weights[0] // sum(weights)))
    least = 1 if total - largest >= number_of - 1 else 0
    holding, rest = [largest] + [least] * (number_of - 1), total - largest - least * (number_of - 1)
    while rest > 0:
        movable = [i for i in range(1, number_of) if holding[i] < largest] or [i for i in range(1, number_of) if holding[i] < limit]
        mass, left = sum([weights[i] for i in movable]), rest
        for i in movable:
            more = min(limit - holding[i], max(1, left * weights[i] // mass), rest)
            holding[i] = holding[i] + more
            rest = rest - more
    return np.array(holding)


def bell_draw(key, extent, scale, bound, cuts=(), kind=jnp.bfloat16):
    factor_of = levels(key, extent, cuts, -0.22, 0.18) if cuts else 1.0
    result = jax.random.normal(key, extent, jnp.float32) * scale * factor_of
    return jnp.minimum(jnp.maximum(result, -bound), bound).astype(kind)


def setup_inputs(seed: int = 0) -> dict:
    splits = jax.random.split(jax.random.key(seed), 10)
    conc = bell_draw(splits[0], (STREAMLINE_COUNT, COMP, NODES_PER_LINE), 1.0, 6.0, ((0, 16), (2, 2)), jnp.float32)
    slowness = draw_slowness(jax.random.fold_in(splits[9], 71), 0)
    retard = jnp.clip(jnp.exp(jax.random.uniform(splits[2], (COMP,), jnp.float32, math.log(0.05), math.log(30.72))), 0.05, 30.72)
    taps = bell_draw(splits[3], (COMP, TAPS), 0.04, 0.12, (), jnp.float32)
    inlet = bell_draw(splits[4], (STREAMLINE_COUNT, COMP), 1.0, 6.0, ((0, 16),), jnp.float32)
    grid = bell_draw(splits[5], (COMP, CELLS), 1.0, 6.0, ((1, 32),), jnp.float32)
    kappa = jnp.clip(jnp.exp(math.log(0.5) - 2.3025851 * jax.random.uniform(splits[6], (CELLS,), jnp.float32) ** levels(splits[6], (CELLS,), ((0, 32),), -0.2, 0.2)), 0.05, 0.5)
    owners_keys = jax.random.split(jax.random.fold_in(splits[7], 1), N_SEG * STREAMLINE_COUNT * NBD // (LINES_DEV * NBD))
    owners_turns = jax.random.permutation(jax.random.fold_in(splits[7], 3), N_SEG * STREAMLINE_COUNT * NBD // (LINES_DEV * NBD))
    owners = jax.vmap(lambda own, number: routed_block(jax.random.fold_in(splits[7], 2), own, number, LINES_DEV * NBD, N_BUNDLE, 1, CAP, 2))(owners_keys, owners_turns).reshape((N_SEG, STREAMLINE_COUNT, NBD, 1))
    cells = place_ends(jax.random.randint(splits[8], (STREAMLINE_COUNT, NODES_PER_LINE), 0, CELLS_DEV), jax.random.fold_in(splits[8], 1), 0, CELLS_DEV - 1).astype(jnp.int32)
    return {"conc": conc, "slowness": slowness, "retard": retard, "taps": taps, "inlet": inlet, "grid": grid, "kappa": kappa, "owners": owners, "cells": cells}


def combine(earlier, later):
    return (earlier[0] * later[0], later[0] * earlier[1] + later[1])


def reference(conc, slowness, retard, taps, inlet, grid, kappa, owners, cells):
    blocks = NODES_PER_LINE // 128
    retain = 1.0 / (1.0 + retard[None, :, None] * slowness[:, None, :])
    owner_line = jnp.transpose(owners[:, :, :, 0], (1, 0, 2)).reshape(STREAMLINE_COUNT, blocks)
    region = (jnp.arange(blocks, dtype=jnp.int32) // NBD)[None, :]
    base_profile = ((region * N_BUNDLE + owner_line) * CELLS_DEV).astype(jnp.int32)
    global_cell = (cells.reshape(STREAMLINE_COUNT, blocks, 128) + base_profile[:, :, None]).reshape(STREAMLINE_COUNT, NODES_PER_LINE)
    coupling = kappa[global_cell]
    flat_cells = global_cell.reshape(-1)
    half_width = TAPS // 2
    for step in range(STEPS):
        factor, offset = lax.associative_scan(combine, (retain, (1.0 - retain) * conc), axis=2)
        upwind = factor * inlet[:, :, None] + offset
        padded = jnp.pad(upwind, ((0, 0), (0, 0), (half_width, half_width)))
        spread = upwind
        for tap in range(TAPS):
            spread = spread + taps[None, :, tap, None] * padded[:, :, tap:tap + NODES_PER_LINE]
        looked = jnp.transpose(grid[:, global_cell], (1, 0, 2))
        flux = coupling[:, None, :] * (looked - spread)
        conc = spread + flux
        grid = grid.at[:, flat_cells].add(-0.25 * jnp.transpose(flux, (1, 0, 2)).reshape(COMP, STREAMLINE_COUNT * NODES_PER_LINE))
    return conc, grid
```

```python
import functools

import jax
import jax.numpy as jnp
from jax import lax
from jax.experimental import pallas as pl
from jax.experimental.pallas import tpu as pltpu
from jax.sharding import PartitionSpec as P

STEPS = 4
LANES = 128
HALF = 16
F32 = jnp.float32
BF16 = jnp.bfloat16

VMEM = pl.BlockSpec(memory_space=pltpu.VMEM)
SMEM = pl.BlockSpec(memory_space=pltpu.SMEM)


def call(kernel, outs, ins, out_specs=None, scratch=(), flops=100_000):
    args = [a for a, _ in ins]
    size = sum(a.size * 4 for a in args) + sum(o.size * 4 for o in outs)
    return pl.pallas_call(
        kernel,
        out_shape=outs,
        in_specs=[s for _, s in ins],
        out_specs=out_specs or [VMEM] * len(outs),
        scratch_shapes=list(scratch),
        cost_estimate=pl.CostEstimate(flops=flops, bytes_accessed=size, transcendentals=0),
        compiler_params=pltpu.CompilerParams(vmem_limit_bytes=40 * 1024 * 1024),
    )(*args)


def sds(shape, dtype=F32):
    return jax.ShapeDtypeStruct(shape, dtype)


def route_kernel(groups, cap, owners, cells, slot, send, count):
    blocks = slot.shape[0]
    owners_total = send.shape[0]
    send[...] = jnp.full(send.shape, -1, jnp.int32)
    for o in range(owners_total):
        count[o] = 0
    for b in range(blocks):
        line, group = b // groups, b % groups
        owner = owners[b]
        rank = count[owner]
        count[owner] = rank + 1
        slot[b] = owner * cap + rank
        send[owner, pl.ds(rank, 1), :] = cells[
            pl.ds(line, 1), group * LANES : (group + 1) * LANES
        ]


def where_slot(slot, b, cap):
    s = slot[b]
    return s // cap, s % cap


def block_scan(retain, value, lane):
    factor, offset = retain, (1.0 - retain) * value
    shift = 1
    while shift < LANES:
        inside = lane >= shift
        offset = offset + jnp.where(inside, factor * pltpu.roll(offset, shift, 1), 0.0)
        factor = jnp.where(inside, factor * pltpu.roll(factor, shift, 1), factor)
        shift *= 2
    return factor, offset


def last_lane(x):
    return jnp.broadcast_to(x[:, LANES - 1 : LANES], x.shape)


def scan_line(retains, values, lane):
    factors, offsets = [], []
    for retain, value in zip(retains, values):
        factor, offset = block_scan(retain, value, lane)
        if factors:
            offset = offset + factor * last_lane(offsets[-1])
            factor = factor * last_lane(factors[-1])
        factors.append(factor)
        offsets.append(offset)
    return factors, offsets


def column(ref_at, rows):
    row = lax.broadcasted_iota(jnp.int32, (rows, LANES), 0)
    out = jnp.zeros((rows, LANES), F32)
    for k in range(rows):
        out = jnp.where(row == k, ref_at(k), out)
    return out


def tile(ref, line, comps, group):
    return ref[pl.ds(line * comps, comps), group * LANES : (group + 1) * LANES]


def put(ref, line, comps, group, value):
    ref[pl.ds(line * comps, comps), group * LANES : (group + 1) * LANES] = value


def first_kernel(lines, comps, groups, conc, slowness, retard, retain, offset, factor, ends):
    lane = lax.broadcasted_iota(jnp.int32, (comps, LANES), 1)
    slow_by = column(lambda k: retard[k], comps)
    for line in range(lines):
        retains, values = [], []
        for group in range(groups):
            s = slowness[pl.ds(line, 1), group * LANES : (group + 1) * LANES]
            r = 1.0 / (1.0 + slow_by * s)
            put(retain, line, comps, group, r)
            retains.append(r)
            values.append(conc[line, :, group * LANES : (group + 1) * LANES])
        factors, offsets = scan_line(retains, values, lane)
        for group in range(groups):
            put(factor, line, comps, group, factors[group])
            put(offset, line, comps, group, offsets[group])
        ends[0, pl.ds(line * comps, comps), :] = jnp.where(lane < 64, offsets[0], offsets[-1])
        ends[1, pl.ds(line * comps, comps), :] = jnp.where(lane < 64, factors[0], factors[-1])


def spread_kernel(
    lines, comps, groups, cap, segs, has_gather,
    offset, factor, end_offset, end_factor, other_offset, other_factor, taps, inlet, slot, spread, send,
):
    taps_total = taps.shape[1]
    me = lax.axis_index("seg")
    lane = lax.broadcasted_iota(jnp.int32, (comps, LANES), 1)
    columns = [jnp.broadcast_to(taps[:, t : t + 1], (comps, LANES)) for t in range(taps_total)]
    for line in range(lines):
        rows = pl.ds(line * comps, comps)

        def part(s):
            if has_gather:
                return other_offset[s, rows, :], other_factor[s, rows, :]
            mine = me == s
            return (
                jnp.where(mine, end_offset[0, rows, :], other_offset[0, rows, :]),
                jnp.where(mine, end_factor[1, rows, :], other_factor[1, rows, :]),
            )

        flow = column(lambda k: inlet[line, k], comps)
        zero = jnp.zeros((comps, LANES), F32)
        left, right, inflow = zero, zero, zero
        for s in range(segs):
            inflow = jnp.where(me == s, flow, inflow)
            off, fac = part(s)
            edge = off + fac * flow
            left = jnp.where(me == s + 1, edge, left)
            right = jnp.where(me == s - 1, edge, right)
            flow = last_lane(edge)
        up = [left]
        for group in range(groups):
            up.append(tile(offset, line, comps, group) + tile(factor, line, comps, group) * inflow)
        up.append(right)
        for group in range(groups):
            before, here, after = up[group], up[group + 1], up[group + 2]
            total = here + columns[HALF] * here
            for d in range(1, HALF + 1):
                low = pltpu.roll(jnp.where(lane >= LANES - d, before, here), d, 1)
                high = pltpu.roll(jnp.where(lane < d, after, here), LANES - d, 1)
                total = total + columns[HALF - d] * low + columns[HALF + d] * high
            put(spread, line, comps, group, total)
            owner, rank = where_slot(slot, line * groups + group, cap)
            send[owner, pl.ds(pl.multiple_of(rank * comps, 8), comps), :] = total


def conc_kernel(lines, comps, groups, cap, first, last, spread, got, coupling, retain, slot, *outs):
    lane = lax.broadcasted_iota(jnp.int32, (comps, LANES), 1)
    outs = list(outs)
    coupling_out = outs.pop() if first else None
    for line in range(lines):
        values, retains = [], []
        for group in range(groups):
            b = line * groups + group
            owner, rank = where_slot(slot, b, cap)
            looked = got[owner, pl.ds(pl.multiple_of(rank * comps, 8), comps), :]
            if first:
                rate = got[owner, pl.ds(cap * comps + rank, 1), :]
                coupling_out[pl.ds(b, 1), :] = rate
            else:
                rate = coupling[pl.ds(b, 1), :]
            s = tile(spread, line, comps, group)
            value = s + rate * (looked - s)
            if last:
                outs[0][line, :, group * LANES : (group + 1) * LANES] = value
            values.append(value)
            if not last:
                retains.append(tile(retain, line, comps, group))
        if last:
            continue
        _, offsets = scan_line(retains, values, lane)
        for group in range(groups):
            put(outs[0], line, comps, group, offsets[group])
        outs[1][0, pl.ds(line * comps, comps), :] = jnp.where(lane < 64, offsets[0], offsets[-1])


def gather_cells(grid, cell, comps, high_total):
    low = jnp.broadcast_to(cell & (LANES - 1), (comps, LANES))
    high = jnp.broadcast_to(cell >> 7, (comps, LANES))
    out = jnp.zeros((comps, LANES), F32)
    for h in range(high_total):
        g = jnp.take_along_axis(
            grid[:, h * LANES : (h + 1) * LANES], low, axis=1, mode="promise_in_bounds"
        )
        out = jnp.where(high == h, g, out)
    return out


def look_first_kernel(cap, cells, grid, kappa, send, rates):
    comps = grid.shape[0]
    high_total = grid.shape[1] // LANES
    row = lax.broadcasted_iota(jnp.int32, (high_total, LANES), 0)

    def one(owner, carry):
        for rank in range(cap):
            cell = cells[owner, pl.ds(rank, 1), :]
            valid = cell >= 0
            cell = jnp.maximum(cell, 0)
            send[owner, rank * comps : (rank + 1) * comps, :] = gather_cells(
                grid, cell, comps, high_total
            )
            low = jnp.broadcast_to(cell & (LANES - 1), (high_total, LANES))
            k = jnp.take_along_axis(kappa[...], low, axis=1, mode="promise_in_bounds")
            rate = jnp.sum(jnp.where(row == (cell >> 7), k, 0.0), axis=0, keepdims=True)
            rate = jnp.where(valid, rate, 0.0)
            rates[owner, pl.ds(rank, 1), :] = rate
            send[owner, pl.ds(cap * comps + rank, 1), :] = rate
        return carry

    lax.fori_loop(0, cells.shape[0], one, 0, unroll=4)


def update_kernel(cap, chunk, last, cells, arrived, looked, rates, grid, *rest):
    if last:
        grid_out, masked, onehot = rest
    else:
        grid_out, send, masked, onehot = rest
    comps = grid.shape[0]
    high_total = grid.shape[1] // LANES
    owners_total = cells.shape[0]
    rows = high_total * comps
    lane_row = lax.broadcasted_iota(jnp.int32, (LANES, LANES), 0).astype(F32)
    total = None
    for start in range(0, owners_total, chunk):

        for i in range(chunk):
            owner = start + i
            for rank in range(cap):
                at = (i * cap + rank) * LANES
                cell = cells[owner, rank : rank + 1, :]
                valid = jnp.broadcast_to(cell, (comps, LANES)) >= 0
                cell = jnp.maximum(cell, 0)
                rate = rates[owner, rank : rank + 1, :]
                span = slice(rank * comps, (rank + 1) * comps)
                flux = jnp.where(valid, rate * (looked[owner, span, :] - arrived[owner, span, :]), 0.0)
                coarse = flux.astype(BF16)
                fine = (flux - coarse.astype(F32)).astype(BF16)
                high = jnp.broadcast_to((cell >> 7).astype(F32), (comps, LANES)).astype(BF16)
                for h in range(high_total):
                    hit = high == jnp.asarray(h, BF16)
                    masked[h * comps : (h + 1) * comps, at : at + LANES] = jnp.where(
                        hit, coarse, jnp.zeros_like(coarse)
                    )
                    masked[rows + h * comps : rows + (h + 1) * comps, at : at + LANES] = jnp.where(
                        hit, fine, jnp.zeros_like(fine)
                    )
                low = (cell & (LANES - 1)).astype(F32)
                onehot[:, at : at + LANES] = jnp.where(lane_row == low, 1.0, 0.0).astype(BF16)
        part = lax.dot_general(
            masked[...], onehot[...], (((1,), (1,)), ((), ())), preferred_element_type=F32
        )
        total = part if total is None else total + part
    for h in range(high_total):
        span = slice(h * LANES, (h + 1) * LANES)
        at = slice(h * comps, (h + 1) * comps)
        at2 = slice(rows + h * comps, rows + (h + 1) * comps)
        grid_out[:, span] = grid[:, span] - 0.25 * (total[at, :] + total[at2, :])
    if last:
        return

    def one(owner, carry):
        for rank in range(cap):
            cell = jnp.maximum(cells[owner, pl.ds(rank, 1), :], 0)
            send[owner, rank * comps : (rank + 1) * comps, :] = gather_cells(
                grid_out, cell, comps, high_total
            )
        return carry

    lax.fori_loop(0, owners_total, one, 0, unroll=4)


def swap(x, segs):
    if segs == 2:
        return lax.ppermute(x, "seg", [(0, 1), (1, 0)])
    return lax.all_gather(x, "seg")


def exchange(x):
    return lax.all_to_all(x, "bundle", split_axis=0, concat_axis=0, tiled=True)


def per_device(conc, slowness, retard, taps, inlet, grid, kappa, owners, cells):
    lines, comps, nodes = conc.shape
    groups = nodes // LANES
    blocks = lines * groups
    segs = lax.axis_size("seg")
    owners_total = lax.axis_size("bundle")
    cap = max(2, 2 * blocks // owners_total)
    rows = lines * comps
    cell_count = grid.shape[1]
    chunk = 16 if owners_total % 16 == 0 else owners_total

    slot, cell_send = call(
        functools.partial(route_kernel, groups, cap),
        [sds((blocks,), jnp.int32), sds((owners_total, cap, LANES), jnp.int32)],
        [(owners.reshape(blocks), SMEM), (cells, VMEM)],
        out_specs=[SMEM, VMEM],
        scratch=[pltpu.SMEM((owners_total,), jnp.int32)],
    )
    cell_recv = exchange(cell_send)

    retain, offset, factor, ends = call(
        functools.partial(first_kernel, lines, comps, groups),
        [sds((rows, nodes))] * 3 + [sds((2, rows, LANES))],
        [(conc, VMEM), (slowness, VMEM), (retard, SMEM)],
    )
    first_ends = ends
    other = swap(ends, segs)
    if segs == 2:
        other_offset = other_factor = other
    else:
        other_offset, other_factor = other[:, 0], other[:, 1]

    looked, rates = call(
        functools.partial(look_first_kernel, cap),
        [sds((owners_total, cap * comps + 8 * (-(-cap // 8)), LANES)), sds((owners_total, cap, LANES))],
        [(cell_recv, VMEM), (grid, VMEM), (kappa.reshape(cell_count // LANES, LANES), VMEM)],
    )
    coupling = None
    for step in range(STEPS):
        last = step == STEPS - 1
        spread, send = call(
            functools.partial(spread_kernel, lines, comps, groups, cap, segs, segs != 2),
            [sds((rows, nodes)), sds((owners_total, cap * comps, LANES))],
            [
                (offset, VMEM), (factor, VMEM), (ends, VMEM), (first_ends, VMEM),
                (other_offset, VMEM), (other_factor, VMEM), (taps, VMEM), (inlet, SMEM), (slot, SMEM),
            ],
        )
        arrived = exchange(send)
        got = exchange(looked)
        outs = [sds(conc.shape)] if last else [sds((rows, nodes)), sds((1, rows, LANES))]
        if step == 0:
            outs.append(sds((blocks, LANES)))
        result = call(
            functools.partial(conc_kernel, lines, comps, groups, cap, step == 0, last),
            outs,
            [
                (spread, VMEM), (got, VMEM), (slowness if step == 0 else coupling, VMEM),
                (retain, VMEM), (slot, SMEM),
            ],
        )
        if step == 0:
            coupling = result[-1]
        if last:
            conc_out = result[0]
        else:
            offset, ends = result[0], result[1]
            got_ends = swap(ends, segs)
            other_offset = got_ends if segs == 2 else got_ends[:, 0]
        outs = [sds(grid.shape)]
        if not last:
            outs.append(sds((owners_total, cap * comps, LANES)))
        result = call(
            functools.partial(update_kernel, cap, chunk, last),
            outs,
            [(cell_recv, VMEM), (arrived, VMEM), (looked, VMEM), (rates, VMEM), (grid, VMEM)],
            scratch=[
                pltpu.VMEM((2 * (cell_count // LANES) * comps, chunk * cap * LANES), BF16),
                pltpu.VMEM((LANES, chunk * cap * LANES), BF16),
            ],
        )
        grid = result[0]
        if not last:
            looked = result[1]
    return (conc_out, grid)


def solution(mesh):
    return jax.shard_map(
        per_device,
        mesh=mesh,
        in_specs=(
            P("bundle", None, "seg"),
            P("bundle", "seg"),
            P(),
            P(),
            P("bundle", None),
            P(None, ("seg", "bundle")),
            P(("seg", "bundle")),
            P("seg", "bundle", None, None),
            P("bundle", "seg"),
        ),
        out_specs=(P("bundle", None, "seg"), P(None, ("seg", "bundle"))),
        check_vma=False,
    )
```

```python
import functools

import jax
import jax.numpy as jnp
from jax import lax
from jax.experimental import pallas as pl
from jax.experimental.pallas import tpu as pltpu
from jax.sharding import PartitionSpec as P

STEPS = 4
LANES = 128
HALF = 16
RADIX = 4
F32 = jnp.float32
BF16 = jnp.bfloat16

VMEM = pl.BlockSpec(memory_space=pltpu.VMEM)
SMEM = pl.BlockSpec(memory_space=pltpu.SMEM)
ANY = pl.BlockSpec(memory_space=pl.ANY)


def call(kernel, outs, ins, out_specs=None, scratch=(), flops=100_000, aliases=None):
    args = [a for a, _ in ins]
    size = sum(a.size * 4 for a in args) + sum(o.size * 4 for o in outs)
    return pl.pallas_call(
        kernel,
        out_shape=outs,
        in_specs=[s for _, s in ins],
        out_specs=out_specs or [VMEM] * len(outs),
        scratch_shapes=list(scratch),
        input_output_aliases=aliases or {},
        cost_estimate=pl.CostEstimate(flops=flops, bytes_accessed=size, transcendentals=0),
        compiler_params=pltpu.CompilerParams(vmem_limit_bytes=40 * 1024 * 1024),
    )(*args)


def sds(shape, dtype=F32):
    return jax.ShapeDtypeStruct(shape, dtype)


def route_kernel(groups, cap, owners, cells, slot, send, count):
    blocks = slot.shape[0]
    owners_total = send.shape[0]
    send[...] = jnp.full(send.shape, -1, jnp.int32)
    for o in range(owners_total):
        count[o] = 0
    for b in range(blocks):
        line, group = b // groups, b % groups
        owner = owners[0, line, 0, group]
        rank = count[owner]
        count[owner] = rank + 1
        slot[b] = owner * cap + rank
        send[owner, pl.ds(rank, 1), :] = cells[
            pl.ds(line, 1), group * LANES : (group + 1) * LANES
        ]


def where_slot(slot, b, cap):
    s = slot[b]
    return s // cap, s % cap


def last_lane(x):
    return jnp.broadcast_to(x[:, LANES - 1 : LANES], x.shape)


def column(ref_at, rows):
    row = lax.broadcasted_iota(jnp.int32, (rows, LANES), 0)
    out = jnp.zeros((rows, LANES), F32)
    for k in range(rows):
        out = jnp.where(row == k, ref_at(k), out)
    return out


def tile(ref, line, comps, group):
    return ref[pl.ds(line * comps, comps), group * LANES : (group + 1) * LANES]


def put(ref, line, comps, group, value):
    ref[pl.ds(line * comps, comps), group * LANES : (group + 1) * LANES] = value


def level_rows(levels, level, line, comps, group):
    return levels[level, pl.ds(line * comps, comps), group * LANES : (group + 1) * LANES]


LEVELS = 7


def scan_line(levels, retain, values, line, comps, groups):
    offsets = []
    for group in range(groups):
        offset = (1.0 - tile(retain, line, comps, group)) * values[group]
        for level in range(LEVELS):
            offset = offset + level_rows(levels, level, line, comps, group) * pltpu.roll(
                offset, 1 << level, 1
            )
        offsets.append(offset)
    carry = last_lane(offsets[0])
    done = [offsets[0]]
    for group in range(1, groups):
        done.append(offsets[group] + level_rows(levels, LEVELS, line, comps, group) * carry)
        if group < groups - 1:
            carry = (
                last_lane(offsets[group])
                + level_rows(levels, LEVELS + 1, line, comps, group) * carry
            )
    return done


def tap_columns(taps, comps):
    return [jnp.broadcast_to(taps[:, t : t + 1], (comps, LANES)) for t in range(taps.shape[1])]


def correlate(tiles, columns, lane):
    count = len(tiles)
    shifted = [tiles]
    for b in range(1, RADIX):
        row = []
        for j in range(count):
            x = tiles[j]
            y = jnp.where(lane < b, tiles[j + 1] if j + 1 < count else 0.0, x)
            row.append(pltpu.roll(y, LANES - b, 1))
        shifted.append(row)
    early = [None] + [
        jnp.where(lane >= LANES - b, pltpu.roll(tiles[0], LANES - b, 1), 0.0) for b in range(1, RADIX)
    ]

    def mix(a, values):
        total = None
        for b in range(RADIX):
            t = RADIX * a + b + HALF
            if t < len(columns) and values[b] is not None:
                term = columns[t] * values[b]
                total = term if total is None else total + term
        return total

    spans = range(-(HALF // RADIX), HALF // RADIX + 1)
    outs = [None] * count
    for a in spans:
        parts = [mix(a, [shifted[b][j] for b in range(RADIX)]) for j in range(count)]
        for j in range(count):
            if a == 0:
                y = parts[j]
            elif a > 0:
                after = parts[j + 1] if j + 1 < count else 0.0
                y = pltpu.roll(jnp.where(lane < RADIX * a, after, parts[j]), LANES - RADIX * a, 1)
            else:
                before = parts[j - 1] if j else mix(a, early)
                y = pltpu.roll(
                    jnp.where(lane >= LANES + RADIX * a, before, parts[j]), -RADIX * a, 1
                )
            outs[j] = y if outs[j] is None else outs[j] + y
    return outs


def correlate_ring(x, columns):
    shifted = [x] + [pltpu.roll(x, LANES - b, 1) for b in range(1, RADIX)]
    out = None
    for a in range(-(HALF // RADIX), HALF // RADIX + 1):
        total = None
        for b in range(RADIX):
            t = RADIX * a + b + HALF
            if t < len(columns):
                term = columns[t] * shifted[b]
                total = term if total is None else total + term
        if a:
            total = pltpu.roll(total, (-RADIX * a) % LANES, 1)
        out = total if out is None else out + total
    return out


def first_kernel(
    lines, comps, groups, conc, slowness, retard, order, retain, levels, offset, factor, ends
):
    lane = lax.broadcasted_iota(jnp.int32, (comps, LANES), 1)
    slow_by = column(lambda k: retard[k], comps)
    for line in range(lines):
        values, whole = [], []
        for group in range(groups):
            s = slowness[pl.ds(line, 1), group * LANES : (group + 1) * LANES]
            r = 1.0 / (1.0 + slow_by * s)
            put(retain, line, comps, group, r)
            rows = pl.ds(line * comps, comps)
            span = slice(group * LANES, (group + 1) * LANES)
            f = r
            for level in range(LEVELS):
                inside = lane >= (1 << level)
                levels[level, rows, span] = jnp.where(inside, f, 0.0)
                f = jnp.where(inside, f * pltpu.roll(f, 1 << level, 1), f)
            levels[LEVELS, rows, span] = f
            end = last_lane(f)
            levels[LEVELS + 1, rows, span] = end
            if group:
                f = f * carry
                carry = carry * end
            else:
                carry = end
            put(factor, line, comps, group, f)
            whole.append(f)
            values.append(conc[line, :, span])
        offsets = scan_line(levels, retain, values, line, comps, groups)
        for group in range(groups):
            put(offset, line, comps, group, offsets[group])
        ends[0, pl.ds(line * comps, comps), :] = jnp.where(lane < 64, offsets[0], offsets[-1])
        ends[1, pl.ds(line * comps, comps), :] = jnp.where(lane < 64, whole[0], whole[-1])


def taps_kernel(lines, comps, groups, sources, taps, *refs):
    lane = lax.broadcasted_iota(jnp.int32, (comps, LANES), 1)
    columns = tap_columns(taps, comps)
    for source, out in zip(refs[:sources], refs[sources:]):
        for line in range(lines):
            tiles = [tile(source, line, comps, group) for group in range(groups)]
            sums = correlate(tiles, columns, lane)
            for group in range(groups):
                put(out, line, comps, group, tiles[group] + sums[group])


def finish_kernel(
    lines, comps, groups, cap, segs, has_gather, aliased,
    local, carried, end_offset, end_factor, other_offset, other_factor, taps, inlet, slot, *rest,
):
    if aliased:
        rest = rest[1:]
    spread, send, done = rest
    me = lax.axis_index("seg")
    lane = lax.broadcasted_iota(jnp.int32, (comps, LANES), 1)
    columns = tap_columns(taps, comps)
    copies = []
    for line in range(lines):
        rows = pl.ds(line * comps, comps)

        def part(s):
            if has_gather:
                return other_offset[s, rows, :], other_factor[s, rows, :]
            mine = me == s
            return (
                jnp.where(mine, end_offset[0, rows, :], other_offset[0, rows, :]),
                jnp.where(mine, end_factor[1, rows, :], other_factor[1, rows, :]),
            )

        flow = column(lambda k: inlet[line, k], comps)
        zero = jnp.zeros((comps, LANES), F32)
        left, right, inflow = zero, zero, zero
        for s in range(segs):
            inflow = jnp.where(me == s, flow, inflow)
            off, fac = part(s)
            edge = off + fac * flow
            left = jnp.where(me == s + 1, edge, left)
            right = jnp.where(me == s - 1, edge, right)
            if s < segs - 1:
                flow = last_lane(edge)
        ring = jnp.where(lane >= LANES - HALF, left, 0.0)
        ring = jnp.where((lane >= 48) & (lane < 48 + HALF), pltpu.roll(right, 48, 1), ring)
        ring = correlate_ring(ring, columns)
        for group in range(groups):
            total = tile(local, line, comps, group) + tile(carried, line, comps, group) * inflow
            if group == 0:
                total = total + jnp.where(lane < HALF, ring, 0.0)
            if group == groups - 1:
                total = total + jnp.where(lane >= LANES - HALF, pltpu.roll(ring, 80, 1), 0.0)
            put(spread, line, comps, group, total)
            b = line * groups + group
            owner, rank = where_slot(slot, b, cap)
            copy = pltpu.make_async_copy(
                spread.at[pl.ds(line * comps, comps), group * LANES : (group + 1) * LANES],
                send.at[owner, pl.ds(pl.multiple_of((cap + rank) * comps, 8), comps), :],
                done.at[b],
            )
            copy.start()
            copies.append(copy)
    for copy in copies:
        copy.wait()


def conc_kernel(lines, comps, groups, cap, first, last, spread, got, coupling, retain, levels, slot, *outs):
    lane = lax.broadcasted_iota(jnp.int32, (comps, LANES), 1)
    outs = list(outs)
    coupling_out = outs.pop() if first else None
    for line in range(lines):
        values = []
        for group in range(groups):
            b = line * groups + group
            owner, rank = where_slot(slot, b, cap)
            looked = got[owner, pl.ds(pl.multiple_of(rank * comps, 8), comps), :]
            if first:
                rate = got[owner, pl.ds(2 * cap * comps + rank, 1), :]
                coupling_out[pl.ds(b, 1), :] = rate
            else:
                rate = coupling[pl.ds(b, 1), :]
            s = tile(spread, line, comps, group)
            value = s + rate * (looked - s)
            if last:
                outs[0][line, :, group * LANES : (group + 1) * LANES] = value
            values.append(value)
        if last:
            continue
        offsets = scan_line(levels, retain, values, line, comps, groups)
        for group in range(groups):
            put(outs[0], line, comps, group, offsets[group])
        outs[1][0, pl.ds(line * comps, comps), :] = jnp.where(lane < 64, offsets[0], offsets[-1])


def gather_cells(grid, cell, comps, high_total):
    low = jnp.broadcast_to(cell & (LANES - 1), (comps, LANES))
    high = jnp.broadcast_to(cell >> 7, (comps, LANES))
    out = jnp.zeros((comps, LANES), F32)
    for h in range(high_total):
        g = jnp.take_along_axis(
            grid[:, h * LANES : (h + 1) * LANES], low, axis=1, mode="promise_in_bounds"
        )
        out = jnp.where(high == h, g, out)
    return out


def look_first_kernel(cap, cells, grid, kappa, send_in, looked, rates, send, extra, done):
    comps = grid.shape[0]
    high_total = grid.shape[1] // LANES
    row = lax.broadcasted_iota(jnp.int32, (high_total, LANES), 0)

    def one(owner, carry):
        for rank in range(cap):
            cell = cells[owner, pl.ds(rank, 1), :]
            valid = cell >= 0
            cell = jnp.maximum(cell, 0)
            looked[owner, rank * comps : (rank + 1) * comps, :] = gather_cells(
                grid, cell, comps, high_total
            )
            low = jnp.broadcast_to(cell & (LANES - 1), (high_total, LANES))
            k = jnp.take_along_axis(kappa[...], low, axis=1, mode="promise_in_bounds")
            rate = jnp.sum(jnp.where(row == (cell >> 7), k, 0.0), axis=0, keepdims=True)
            rate = jnp.where(valid, rate, 0.0)
            rates[owner, pl.ds(rank, 1), :] = rate
            extra[owner, pl.ds(rank, 1), :] = rate
        return carry

    lax.fori_loop(0, cells.shape[0], one, 0, unroll=4)
    width = cap * comps
    copies = [
        pltpu.make_async_copy(looked, send.at[:, 0:width, :], done.at[0]),
        pltpu.make_async_copy(extra, send.at[:, 2 * width : 2 * width + extra.shape[1], :], done.at[1]),
    ]
    for copy in copies:
        copy.start()
    for copy in copies:
        copy.wait()


def onehot_kernel(cap, cells, onehot):
    wide = onehot.shape[1]
    row = lax.broadcasted_iota(jnp.int32, (wide, LANES), 0)

    def one(owner, carry):
        for rank in range(cap):
            cell = cells[owner, pl.ds(rank, 1), :]
            hit = jnp.where(row == (cell & (wide - 1)), 1.0, 0.0).astype(F32)
            at = pl.multiple_of((owner * cap + rank) * LANES, LANES)
            onehot[pl.ds(at, LANES), :] = hit.T.astype(BF16)
        return carry

    lax.fori_loop(0, cells.shape[0], one, 0)


def update_kernel(cap, chunk, last, cells, got, looked, rates, onehot, grid, *rest):
    if last:
        grid_out, masked = rest
    else:
        grid_out, looked_out, send, masked, done = rest
    comps = grid.shape[0]
    wide = onehot.shape[1]
    bits = wide.bit_length() - 1
    high_total = grid.shape[1] // wide
    owners_total = cells.shape[0]
    rows = high_total * comps
    width = chunk * cap * LANES
    total = None
    for start in range(0, owners_total, chunk):
        turn = (start // chunk) % masked.shape[0]
        for i in range(chunk):
            owner = start + i
            for rank in range(cap):
                at = (i * cap + rank) * LANES
                cell = cells[owner, rank : rank + 1, :]
                valid = jnp.broadcast_to(cell, (comps, LANES)) >= 0
                cell = jnp.maximum(cell, 0)
                rate = rates[owner, rank : rank + 1, :]
                span = slice(rank * comps, (rank + 1) * comps)
                came = slice((cap + rank) * comps, (cap + rank + 1) * comps)
                flux = jnp.where(valid, rate * (looked[owner, span, :] - got[owner, came, :]), 0.0)
                coarse = flux.astype(BF16)
                fine = (flux - coarse.astype(F32)).astype(BF16)
                high = jnp.broadcast_to((cell >> bits).astype(F32), (comps, LANES)).astype(BF16)
                for h in range(high_total):
                    hit = high == jnp.asarray(h, BF16)
                    masked[turn, h * comps : (h + 1) * comps, at : at + LANES] = jnp.where(
                        hit, coarse, jnp.zeros_like(coarse)
                    )
                    masked[turn, rows + h * comps : rows + (h + 1) * comps, at : at + LANES] = (
                        jnp.where(hit, fine, jnp.zeros_like(fine))
                    )
        first = start * cap * LANES
        part = jnp.dot(
            masked[turn], onehot[first : first + width, :], preferred_element_type=F32
        )
        total = part if total is None else total + part
    for h in range(high_total):
        span = slice(h * wide, (h + 1) * wide)
        at = slice(h * comps, (h + 1) * comps)
        at2 = slice(rows + h * comps, rows + (h + 1) * comps)
        grid_out[:, span] = grid[:, span] - 0.25 * (total[at, :] + total[at2, :])
    if last:
        return

    def one(owner, carry):
        for rank in range(cap):
            cell = jnp.maximum(cells[owner, pl.ds(rank, 1), :], 0)
            looked_out[owner, rank * comps : (rank + 1) * comps, :] = gather_cells(
                grid_out, cell, comps, grid.shape[1] // LANES
            )
        return carry

    lax.fori_loop(0, owners_total, one, 0, unroll=4)
    copy = pltpu.make_async_copy(looked_out, send.at[:, 0 : cap * comps, :], done.at[0])
    copy.start()
    copy.wait()


def swap(x, segs):
    if segs == 2:
        return lax.ppermute(x, "seg", [(0, 1), (1, 0)])
    return lax.all_gather(x, "seg")


def exchange(x):
    return lax.all_to_all(x, "bundle", split_axis=0, concat_axis=0, tiled=True)


def per_device(conc, slowness, retard, taps, inlet, grid, kappa, owners, cells):
    lines, comps, nodes = conc.shape
    groups = nodes // LANES
    blocks = lines * groups
    segs = lax.axis_size("seg")
    owners_total = lax.axis_size("bundle")
    cap = max(2, 2 * blocks // owners_total)
    rows = lines * comps
    cell_count = grid.shape[1]
    chunk = 4 if owners_total % 4 == 0 else owners_total
    half = cap * comps
    extra = 8 * (-(-cap // 8))

    slot, cell_send = call(
        functools.partial(route_kernel, groups, cap),
        [sds((blocks,), jnp.int32), sds((owners_total, cap, LANES), jnp.int32)],
        [(jnp.swapaxes(owners, 2, 3), SMEM), (cells, VMEM)],
        out_specs=[SMEM, VMEM],
        scratch=[pltpu.SMEM((owners_total,), jnp.int32)],
    )
    cell_recv = exchange(cell_send)

    retain, levels, offset, factor, ends = call(
        functools.partial(first_kernel, lines, comps, groups),
        [
            sds((rows, nodes)), sds((LEVELS + 2, rows, nodes)), sds((rows, nodes)),
            sds((rows, nodes)), sds((2, rows, LANES)),
        ],
        [(conc, VMEM), (slowness, VMEM), (retard, SMEM), (slot, SMEM)],
    )
    first_ends = ends
    other = swap(ends, segs)
    if segs == 2:
        other_offset = other_factor = other
    else:
        other_offset, other_factor = other[:, 0], other[:, 1]
    local, carried = call(
        functools.partial(taps_kernel, lines, comps, groups, 2),
        [sds((rows, nodes))] * 2,
        [(taps, VMEM), (offset, VMEM), (factor, VMEM)],
    )

    def finish(send, size):
        ins = [
            (local, VMEM), (carried, VMEM), (ends, VMEM), (first_ends, VMEM),
            (other_offset, VMEM), (other_factor, VMEM), (taps, VMEM), (inlet, SMEM), (slot, SMEM),
        ]
        aliases = {}
        if send is not None:
            aliases = {len(ins): 1}
            ins.append((send, ANY))
        return call(
            functools.partial(
                finish_kernel, lines, comps, groups, cap, segs, segs != 2, send is not None
            ),
            [sds((rows, nodes)), sds((owners_total, size, LANES))],
            ins,
            out_specs=[VMEM, ANY],
            scratch=[pltpu.SemaphoreType.DMA((blocks,))],
            aliases=aliases,
        )

    spread, send = finish(None, 2 * half + extra)
    looked, rates, send = call(
        functools.partial(look_first_kernel, cap),
        [
            sds((owners_total, half, LANES)), sds((owners_total, cap, LANES)),
            sds((owners_total, 2 * half + extra, LANES)),
        ],
        [
            (cell_recv, VMEM), (grid, VMEM),
            (kappa.reshape(cell_count // LANES, LANES), VMEM), (send, ANY),
        ],
        out_specs=[VMEM, VMEM, ANY],
        scratch=[pltpu.VMEM((owners_total, extra, LANES), F32), pltpu.SemaphoreType.DMA((2,))],
        aliases={3: 2},
    )
    wide = 256 if cell_count % 256 == 0 else LANES
    (onehot,) = call(
        functools.partial(onehot_kernel, cap),
        [sds((owners_total * cap * LANES, wide), BF16)],
        [(cell_recv, VMEM)],
    )
    coupling = slowness
    for step in range(STEPS):
        last = step == STEPS - 1
        got = exchange(send)
        outs = [sds(conc.shape)] if last else [sds((rows, nodes)), sds((1, rows, LANES))]
        if step == 0:
            outs.append(sds((blocks, LANES)))
        result = call(
            functools.partial(conc_kernel, lines, comps, groups, cap, step == 0, last),
            outs,
            [
                (spread, VMEM), (got, VMEM), (coupling, VMEM), (retain, VMEM), (levels, VMEM),
                (slot, SMEM),
            ],
        )
        if step == 0:
            coupling = result[-1]
        if last:
            conc_out = result[0]
        else:
            offset, ends = result[0], result[1]
            got_ends = swap(ends, segs)
            other_offset = got_ends if segs == 2 else got_ends[:, 0]
        outs, specs = [sds(grid.shape)], [VMEM]
        scratch = [pltpu.VMEM((min(4, owners_total // chunk), 2 * (cell_count // wide) * comps, chunk * cap * LANES), BF16)]
        if not last:
            outs += [sds((owners_total, half, LANES)), sds((owners_total, 2 * half, LANES))]
            specs += [VMEM, ANY]
            scratch.append(pltpu.SemaphoreType.DMA((1,)))
        result = call(
            functools.partial(update_kernel, cap, chunk, last),
            outs,
            [
                (cell_recv, VMEM), (got, VMEM), (looked, VMEM), (rates, VMEM), (onehot, VMEM),
                (grid, VMEM),
            ],
            out_specs=specs,
            scratch=scratch,
        )
        grid = result[0]
        if not last:
            looked, send = result[1], result[2]
            (local,) = call(
                functools.partial(taps_kernel, lines, comps, groups, 1),
                [sds((rows, nodes))],
                [(taps, VMEM), (offset, VMEM)],
            )
            spread, send = finish(send, 2 * half)
    return (conc_out, grid)


def solution(mesh):
    return jax.shard_map(
        per_device,
        mesh=mesh,
        in_specs=(
            P("bundle", None, "seg"),
            P("bundle", "seg"),
            P(),
            P(),
            P("bundle", None),
            P(None, ("seg", "bundle")),
            P(("seg", "bundle")),
            P("seg", "bundle", None, None),
            P("bundle", "seg"),
        ),
        out_specs=(P("bundle", None, "seg"), P(None, ("seg", "bundle"))),
        check_vma=False,
    )
```

```python
import functools

import jax
import jax.numpy as jnp
from jax import lax
from jax.experimental import pallas as pl
from jax.experimental.pallas import tpu as pltpu
from jax.sharding import PartitionSpec as P

STEPS = 4
LANES = 128
HALF = 16
RADIX = 4
F32 = jnp.float32
BF16 = jnp.bfloat16

VMEM = pl.BlockSpec(memory_space=pltpu.VMEM)
SMEM = pl.BlockSpec(memory_space=pltpu.SMEM)
ANY = pl.BlockSpec(memory_space=pl.ANY)


def call(kernel, outs, ins, out_specs=None, scratch=()):
    args = [a for a, _ in ins]
    return pl.pallas_call(
        kernel,
        out_shape=outs,
        in_specs=[s for _, s in ins],
        out_specs=out_specs or [VMEM] * len(outs),
        scratch_shapes=list(scratch),
        cost_estimate=pl.CostEstimate(flops=1, bytes_accessed=1, transcendentals=0),
        compiler_params=pltpu.CompilerParams(vmem_limit_bytes=40 * 1024 * 1024),
    )(*args)


def sds(shape, dtype=F32):
    return jax.ShapeDtypeStruct(shape, dtype)


def route_kernel(groups, cap, owners, cells, slot, send, count):
    blocks = slot.shape[0]
    owners_total = send.shape[0]
    send[...] = jnp.full(send.shape, -1, jnp.int32)
    for o in range(owners_total):
        count[o] = 0
    for b in range(blocks):
        line, group = b // groups, b % groups
        owner = owners[0, line, 0, group]
        rank = count[owner]
        count[owner] = rank + 1
        slot[b] = owner * cap + rank
        send[owner, pl.ds(rank, 1), :] = cells[
            pl.ds(line, 1), group * LANES : (group + 1) * LANES
        ]


def where_slot(slot, b, cap):
    s = slot[b]
    return s // cap, s % cap


def last_lane(x):
    return jnp.broadcast_to(x[:, LANES - 1 : LANES], x.shape)


def column(row, rows):
    square = (rows, rows)
    here = lax.broadcasted_iota(jnp.int32, square, 0) == lax.broadcasted_iota(jnp.int32, square, 1)
    values = jnp.sum(jnp.where(here, jnp.broadcast_to(row, square), 0.0), axis=1, keepdims=True)
    return jnp.broadcast_to(values, (rows, LANES))


def tile(ref, line, comps, group):
    return ref[pl.ds(line * comps, comps), group * LANES : (group + 1) * LANES]


def put(ref, line, comps, group, value):
    ref[pl.ds(line * comps, comps), group * LANES : (group + 1) * LANES] = value


def level_rows(levels, level, line, comps, group):
    return levels[level, pl.ds(line * comps, comps), group * LANES : (group + 1) * LANES]


LEVELS = 7


def scan_line(levels, retain, values, line, comps, groups):
    offsets = []
    for group in range(groups):
        offset = (1.0 - tile(retain, line, comps, group)) * values[group]
        for level in range(LEVELS):
            offset = offset + level_rows(levels, level, line, comps, group) * pltpu.roll(
                offset, 1 << level, 1
            )
        offsets.append(offset)
    carry = last_lane(offsets[0])
    done = [offsets[0]]
    for group in range(1, groups):
        done.append(offsets[group] + level_rows(levels, LEVELS, line, comps, group) * carry)
        if group < groups - 1:
            carry = (
                last_lane(offsets[group])
                + level_rows(levels, LEVELS + 1, line, comps, group) * carry
            )
    return done


def tap_columns(wide_taps):
    return [wide_taps[t] for t in range(wide_taps.shape[0])]


def correlate(tiles, columns, lane):
    count = len(tiles)
    shifted = [tiles]
    for b in range(1, RADIX):
        row = []
        for j in range(count):
            x = tiles[j]
            y = jnp.where(lane < b, tiles[j + 1] if j + 1 < count else 0.0, x)
            row.append(pltpu.roll(y, LANES - b, 1))
        shifted.append(row)
    early = [None] + [
        jnp.where(lane >= LANES - b, pltpu.roll(tiles[0], LANES - b, 1), 0.0) for b in range(1, RADIX)
    ]

    def mix(a, values):
        total = None
        for b in range(RADIX):
            t = RADIX * a + b + HALF
            if t < len(columns) and values[b] is not None:
                term = columns[t] * values[b]
                total = term if total is None else total + term
        return total

    spans = range(-(HALF // RADIX), HALF // RADIX + 1)
    outs = [None] * count
    for a in spans:
        parts = [mix(a, [shifted[b][j] for b in range(RADIX)]) for j in range(count)]
        for j in range(count):
            if a == 0:
                y = parts[j]
            elif a > 0:
                after = parts[j + 1] if j + 1 < count else 0.0
                y = pltpu.roll(jnp.where(lane < RADIX * a, after, parts[j]), LANES - RADIX * a, 1)
            else:
                before = parts[j - 1] if j else mix(a, early)
                y = pltpu.roll(
                    jnp.where(lane >= LANES + RADIX * a, before, parts[j]), -RADIX * a, 1
                )
            outs[j] = y if outs[j] is None else outs[j] + y
    return outs


def correlate_ring(x, columns):
    shifted = [x] + [pltpu.roll(x, LANES - b, 1) for b in range(1, RADIX)]
    out = None
    for a in range(-(HALF // RADIX), HALF // RADIX + 1):
        total = None
        for b in range(RADIX):
            t = RADIX * a + b + HALF
            if t < len(columns):
                term = columns[t] * shifted[b]
                total = term if total is None else total + term
        if a:
            total = pltpu.roll(total, (-RADIX * a) % LANES, 1)
        out = total if out is None else out + total
    return out


def first_kernel(
    lines, comps, groups, conc, slowness, retard, taps, inlet, order,
    retain, levels, offset, factor, ends, wide_taps, wide_inlet,
):
    lane = lax.broadcasted_iota(jnp.int32, (comps, LANES), 1)
    slow_by = column(retard[...], comps)
    for t in range(taps.shape[1]):
        wide_taps[t] = jnp.broadcast_to(taps[:, t : t + 1], (comps, LANES))
    for line in range(lines):
        wide_inlet[pl.ds(line * comps, comps), :] = column(inlet[line : line + 1, :], comps)
    for line in range(lines):
        values, whole = [], []
        for group in range(groups):
            s = slowness[pl.ds(line, 1), group * LANES : (group + 1) * LANES]
            r = 1.0 / (1.0 + slow_by * s)
            put(retain, line, comps, group, r)
            rows = pl.ds(line * comps, comps)
            span = slice(group * LANES, (group + 1) * LANES)
            f = r
            for level in range(LEVELS):
                inside = lane >= (1 << level)
                levels[level, rows, span] = jnp.where(inside, f, 0.0)
                f = jnp.where(inside, f * pltpu.roll(f, 1 << level, 1), f)
            levels[LEVELS, rows, span] = f
            end = last_lane(f)
            levels[LEVELS + 1, rows, span] = end
            if group:
                f = f * carry
                carry = carry * end
            else:
                carry = end
            put(factor, line, comps, group, f)
            whole.append(f)
            values.append(conc[line, :, span])
        offsets = scan_line(levels, retain, values, line, comps, groups)
        for group in range(groups):
            put(offset, line, comps, group, offsets[group])
        ends[0, pl.ds(line * comps, comps), :] = jnp.where(lane < 64, offsets[0], offsets[-1])
        ends[1, pl.ds(line * comps, comps), :] = jnp.where(lane < 64, whole[0], whole[-1])


def taps_kernel(lines, comps, groups, sources, taps, *refs):
    lane = lax.broadcasted_iota(jnp.int32, (comps, LANES), 1)
    columns = tap_columns(taps)
    for source, out in zip(refs[:sources], refs[sources:]):
        for line in range(lines):
            tiles = [tile(source, line, comps, group) for group in range(groups)]
            sums = correlate(tiles, columns, lane)
            for group in range(groups):
                put(out, line, comps, group, tiles[group] + sums[group])


def place(send, slot, b, cap, comps, value):
    owner, rank = where_slot(slot, b, cap)
    send[owner, pl.ds(pl.multiple_of((cap + rank) * comps, 8), comps), :] = value


def finish_kernel(
    lines, comps, groups, cap, segs, has_gather, first,
    local, carried, end_offset, end_factor, other_offset, other_factor, taps, inlet, *rest,
):
    if first:
        (spread,) = rest
    else:
        slot_in, looked, spread, send, slot, done = rest
        copy = pltpu.make_async_copy(slot_in, slot, done)
        copy.start()
    me = lax.axis_index("seg")
    lane = lax.broadcasted_iota(jnp.int32, (comps, LANES), 1)
    columns = tap_columns(taps)
    for line in range(lines):
        rows = pl.ds(line * comps, comps)

        def part(s):
            if has_gather:
                return other_offset[s, rows, :], other_factor[s, rows, :]
            mine = me == s
            return (
                jnp.where(mine, end_offset[0, rows, :], other_offset[0, rows, :]),
                jnp.where(mine, end_factor[1, rows, :], other_factor[1, rows, :]),
            )

        flow = inlet[rows, :]
        zero = jnp.zeros((comps, LANES), F32)
        left, right, inflow = zero, zero, zero
        for s in range(segs):
            inflow = jnp.where(me == s, flow, inflow)
            off, fac = part(s)
            edge = off + fac * flow
            left = jnp.where(me == s + 1, edge, left)
            right = jnp.where(me == s - 1, edge, right)
            if s < segs - 1:
                flow = last_lane(edge)
        ring = jnp.where(lane >= LANES - HALF, left, 0.0)
        ring = jnp.where((lane >= 48) & (lane < 48 + HALF), pltpu.roll(right, 48, 1), ring)
        ring = correlate_ring(ring, columns)
        for group in range(groups):
            total = tile(local, line, comps, group) + tile(carried, line, comps, group) * inflow
            if group == 0:
                total = total + jnp.where(lane < HALF, ring, 0.0)
            if group == groups - 1:
                total = total + jnp.where(lane >= LANES - HALF, pltpu.roll(ring, 80, 1), 0.0)
            put(spread, line, comps, group, total)
    if first:
        return
    send[:, 0 : cap * comps, :] = looked[...]
    copy.wait()
    for b in range(lines * groups):
        place(send, slot, b, cap, comps, tile(spread, b // groups, comps, b % groups))


def conc_kernel(lines, comps, groups, cap, first, last, spread, got, coupling, retain, levels, slot, *outs):
    lane = lax.broadcasted_iota(jnp.int32, (comps, LANES), 1)
    outs = list(outs)
    coupling_out = outs.pop() if first else None
    for line in range(lines):
        values = []
        for group in range(groups):
            b = line * groups + group
            owner, rank = where_slot(slot, b, cap)
            looked = got[owner, pl.ds(pl.multiple_of(rank * comps, 8), comps), :]
            if first:
                rate = got[owner, pl.ds(2 * cap * comps + rank, 1), :]
                coupling_out[pl.ds(b, 1), :] = rate
            else:
                rate = coupling[pl.ds(b, 1), :]
            s = tile(spread, line, comps, group)
            value = s + rate * (looked - s)
            if last:
                outs[0][line, :, group * LANES : (group + 1) * LANES] = value
            values.append(value)
        if last:
            continue
        offsets = scan_line(levels, retain, values, line, comps, groups)
        for group in range(groups):
            put(outs[0], line, comps, group, offsets[group])
        outs[1][0, pl.ds(line * comps, comps), :] = jnp.where(lane < 64, offsets[0], offsets[-1])


def gather_cells(grid, cell, comps, high_total):
    low = jnp.broadcast_to(cell & (LANES - 1), (comps, LANES))
    high = jnp.broadcast_to(cell >> 7, (comps, LANES))
    out = jnp.zeros((comps, LANES), F32)
    for h in range(high_total):
        g = jnp.take_along_axis(
            grid[:, h * LANES : (h + 1) * LANES], low, axis=1, mode="promise_in_bounds"
        )
        out = jnp.where(high == h, g, out)
    return out


def look_first_kernel(groups, cap, cells, grid, kappa, spread, slot, rates, send):
    comps = grid.shape[0]
    high_total = grid.shape[1] // LANES
    row = lax.broadcasted_iota(jnp.int32, (high_total, LANES), 0)

    def one(owner, carry):
        for rank in range(cap):
            cell = cells[owner, pl.ds(rank, 1), :]
            valid = cell >= 0
            cell = jnp.maximum(cell, 0)
            send[owner, rank * comps : (rank + 1) * comps, :] = gather_cells(
                grid, cell, comps, high_total
            )
            low = jnp.broadcast_to(cell & (LANES - 1), (high_total, LANES))
            k = jnp.take_along_axis(kappa[...], low, axis=1, mode="promise_in_bounds")
            rate = jnp.sum(jnp.where(row == (cell >> 7), k, 0.0), axis=0, keepdims=True)
            rate = jnp.where(valid, rate, 0.0)
            rates[owner, pl.ds(rank, 1), :] = rate
            send[owner, pl.ds(2 * cap * comps + rank, 1), :] = rate
        return carry

    lax.fori_loop(0, cells.shape[0], one, 0, unroll=4)
    for b in range(slot.shape[0]):
        place(send, slot, b, cap, comps, tile(spread, b // groups, comps, b % groups))


def onehot_kernel(cap, cells, onehot):
    wide = onehot.shape[1]
    row = lax.broadcasted_iota(jnp.int32, (wide, LANES), 0)

    def one(owner, carry):
        for rank in range(cap):
            cell = cells[owner, pl.ds(rank, 1), :]
            hit = jnp.where(row == (cell & (wide - 1)), 1.0, 0.0).astype(F32)
            at = pl.multiple_of((owner * cap + rank) * LANES, LANES)
            onehot[pl.ds(at, LANES), :] = hit.T.astype(BF16)
        return carry

    lax.fori_loop(0, cells.shape[0], one, 0)


def update_kernel(cap, chunk, last, cells, got, looked, rates, onehot, grid, *rest):
    if last:
        grid_out, masked = rest
    else:
        grid_out, looked_out, masked = rest
    comps = grid.shape[0]
    wide = onehot.shape[1]
    bits = wide.bit_length() - 1
    high_total = grid.shape[1] // wide
    owners_total = cells.shape[0]
    rows = high_total * comps
    width = chunk * cap * LANES
    total = None
    for start in range(0, owners_total, chunk):
        turn = (start // chunk) % masked.shape[0]
        for i in range(chunk):
            owner = start + i
            for rank in range(cap):
                at = (i * cap + rank) * LANES
                cell = cells[owner, rank : rank + 1, :]
                valid = jnp.broadcast_to(cell, (comps, LANES)) >= 0
                cell = jnp.maximum(cell, 0)
                rate = rates[owner, rank : rank + 1, :]
                span = slice(rank * comps, (rank + 1) * comps)
                came = slice((cap + rank) * comps, (cap + rank + 1) * comps)
                flux = jnp.where(valid, rate * (looked[owner, span, :] - got[owner, came, :]), 0.0)
                coarse = flux.astype(BF16)
                fine = (flux - coarse.astype(F32)).astype(BF16)
                high = jnp.broadcast_to((cell >> bits).astype(F32), (comps, LANES)).astype(BF16)
                for h in range(high_total):
                    hit = high == jnp.asarray(h, BF16)
                    masked[turn, h * comps : (h + 1) * comps, at : at + LANES] = jnp.where(
                        hit, coarse, jnp.zeros_like(coarse)
                    )
                    masked[turn, rows + h * comps : rows + (h + 1) * comps, at : at + LANES] = (
                        jnp.where(hit, fine, jnp.zeros_like(fine))
                    )
        first = start * cap * LANES
        part = jnp.dot(
            masked[turn], onehot[first : first + width, :], preferred_element_type=F32
        )
        total = part if total is None else total + part
    for h in range(high_total):
        span = slice(h * wide, (h + 1) * wide)
        at = slice(h * comps, (h + 1) * comps)
        at2 = slice(rows + h * comps, rows + (h + 1) * comps)
        grid_out[:, span] = grid[:, span] - 0.25 * (total[at, :] + total[at2, :])
    if last:
        return

    def one(owner, carry):
        for rank in range(cap):
            cell = jnp.maximum(cells[owner, pl.ds(rank, 1), :], 0)
            looked_out[owner, rank * comps : (rank + 1) * comps, :] = gather_cells(
                grid_out, cell, comps, grid.shape[1] // LANES
            )
        return carry

    lax.fori_loop(0, owners_total, one, 0, unroll=4)


def swap(x, segs):
    if segs == 2:
        return lax.ppermute(x, "seg", [(0, 1), (1, 0)])
    return lax.all_gather(x, "seg")


def exchange(x):
    return lax.all_to_all(x, "bundle", split_axis=0, concat_axis=0, tiled=True)


def per_device(conc, slowness, retard, taps, inlet, grid, kappa, owners, cells):
    lines, comps, nodes = conc.shape
    groups = nodes // LANES
    blocks = lines * groups
    segs = lax.axis_size("seg")
    owners_total = lax.axis_size("bundle")
    cap = max(2, 2 * blocks // owners_total)
    rows = lines * comps
    cell_count = grid.shape[1]
    chunk = 4 if owners_total % 4 == 0 else owners_total
    half = cap * comps
    extra = 8 * (-(-cap // 8))

    slot, cell_send = call(
        functools.partial(route_kernel, groups, cap),
        [sds((blocks,), jnp.int32), sds((owners_total, 8 * (-(-cap // 8)), LANES), jnp.int32)],
        [(jnp.swapaxes(owners, 2, 3), SMEM), (cells, VMEM)],
        out_specs=[SMEM, VMEM],
        scratch=[pltpu.SMEM((owners_total,), jnp.int32)],
    )
    cell_recv = exchange(cell_send)

    retain, levels, offset, factor, ends, taps, inlet = call(
        functools.partial(first_kernel, lines, comps, groups),
        [
            sds((rows, nodes)), sds((LEVELS + 2, rows, nodes)), sds((rows, nodes)),
            sds((rows, nodes)), sds((2, rows, LANES)), sds((taps.shape[1], comps, LANES)),
            sds((rows, LANES)),
        ],
        [
            (conc, VMEM), (slowness, VMEM), (retard.reshape(1, comps), VMEM), (taps, VMEM),
            (inlet, VMEM), (slot, ANY),
        ],
    )
    first_ends = ends
    other = swap(ends, segs)
    if segs == 2:
        other_offset = other_factor = other
    else:
        other_offset, other_factor = other[:, 0], other[:, 1]
    local, carried = call(
        functools.partial(taps_kernel, lines, comps, groups, 2),
        [sds((rows, nodes))] * 2,
        [(taps, VMEM), (offset, VMEM), (factor, VMEM)],
    )

    def finish(looked):
        first = looked is None
        ins = [
            (local, VMEM), (carried, VMEM), (ends, VMEM), (first_ends, VMEM),
            (other_offset, VMEM), (other_factor, VMEM), (taps, VMEM), (inlet, VMEM),
        ]
        outs, scratch = [sds((rows, nodes))], []
        if not first:
            ins += [(slot, VMEM), (looked, VMEM)]
            outs.append(sds((owners_total, 2 * half, LANES)))
            scratch = [pltpu.SMEM((blocks,), jnp.int32), pltpu.SemaphoreType.DMA]
        return call(
            functools.partial(finish_kernel, lines, comps, groups, cap, segs, segs != 2, first),
            outs, ins, scratch=scratch,
        )

    (spread,) = finish(None)
    rates, send = call(
        functools.partial(look_first_kernel, groups, cap),
        [
            sds((owners_total, cap, LANES)), sds((owners_total, 2 * half + extra, LANES)),
        ],
        [
            (cell_recv, VMEM), (grid, VMEM), (kappa.reshape(cell_count // LANES, LANES), VMEM),
            (spread, VMEM), (slot, SMEM),
        ],
    )
    looked = send
    wide = 256 if cell_count % 256 == 0 else LANES
    (onehot,) = call(
        functools.partial(onehot_kernel, cap),
        [sds((owners_total * cap * LANES, wide), BF16)],
        [(cell_recv, VMEM)],
    )
    coupling = slowness
    for step in range(STEPS):
        last = step == STEPS - 1
        got = exchange(send)
        outs = [sds(conc.shape)] if last else [sds((rows, nodes)), sds((1, rows, LANES))]
        if step == 0:
            outs.append(sds((blocks, LANES)))
        result = call(
            functools.partial(conc_kernel, lines, comps, groups, cap, step == 0, last),
            outs,
            [
                (spread, VMEM), (got, VMEM), (coupling, VMEM), (retain, VMEM), (levels, VMEM),
                (slot, SMEM),
            ],
        )
        if step == 0:
            coupling = result[-1]
        if last:
            conc_out = result[0]
        else:
            offset, ends = result[0], result[1]
            got_ends = swap(ends, segs)
            other_offset = got_ends if segs == 2 else got_ends[:, 0]
        outs = [sds(grid.shape)]
        if not last:
            outs.append(sds((owners_total, half, LANES)))
        result = call(
            functools.partial(update_kernel, cap, chunk, last),
            outs,
            [
                (cell_recv, VMEM), (got, VMEM), (looked, VMEM), (rates, VMEM), (onehot, VMEM),
                (grid, VMEM),
            ],
            scratch=[
                pltpu.VMEM(
                    (
                        min(4, owners_total // chunk),
                        2 * (cell_count // wide) * comps,
                        chunk * cap * LANES,
                    ),
                    BF16,
                )
            ],
        )
        grid = result[0]
        if not last:
            looked = result[1]
            (local,) = call(
                functools.partial(taps_kernel, lines, comps, groups, 1),
                [sds((rows, nodes))],
                [(taps, VMEM), (offset, VMEM)],
            )
            spread, send = finish(looked)
    return (conc_out, grid)


def solution(mesh):
    return jax.shard_map(
        per_device,
        mesh=mesh,
        in_specs=(
            P("bundle", None, "seg"),
            P("bundle", "seg"),
            P(),
            P(),
            P("bundle", None),
            P(None, ("seg", "bundle")),
            P(("seg", "bundle")),
            P("seg", "bundle", None, None),
            P("bundle", "seg"),
        ),
        out_specs=(P("bundle", None, "seg"), P(None, ("seg", "bundle"))),
        check_vma=False,
    )
```

```python
import functools

import jax
import jax.numpy as jnp
from jax import lax
from jax.experimental import pallas as pl
from jax.experimental.pallas import tpu as pltpu
from jax.sharding import PartitionSpec as P

STEPS = 4
LANES = 128
HALF = 16
RADIX = 4
F32 = jnp.float32
BF16 = jnp.bfloat16

VMEM = pl.BlockSpec(memory_space=pltpu.VMEM)
SMEM = pl.BlockSpec(memory_space=pltpu.SMEM)
ANY = pl.BlockSpec(memory_space=pl.ANY)


def call(kernel, outs, ins, out_specs=None, scratch=(), flops=1e8):
    args = [a for a, _ in ins]
    return pl.pallas_call(
        kernel,
        out_shape=outs,
        in_specs=[s for _, s in ins],
        out_specs=out_specs or [VMEM] * len(outs),
        scratch_shapes=list(scratch),
        cost_estimate=pl.CostEstimate(flops=int(flops), bytes_accessed=1, transcendentals=0),
        compiler_params=pltpu.CompilerParams(vmem_limit_bytes=40 * 1024 * 1024),
    )(*args)


def sds(shape, dtype=F32):
    return jax.ShapeDtypeStruct(shape, dtype)


def route_kernel(groups, cap, owners, cells, slot, send, count):
    blocks = slot.shape[0]
    owners_total = send.shape[0]
    send[...] = jnp.full(send.shape, -1, jnp.int32)
    for o in range(owners_total):
        count[o] = 0
    for b in range(blocks):
        line, group = b // groups, b % groups
        owner = owners[0, line, 0, group]
        rank = count[owner]
        count[owner] = rank + 1
        slot[b : b + 1, :] = jnp.full((1, LANES), owner * cap + rank, jnp.int32)
        send[owner, pl.ds(rank, 1), :] = cells[
            pl.ds(line, 1), group * LANES : (group + 1) * LANES
        ]


def where_slot(slot, b, cap):
    s = slot[b, 0]
    return s // cap, s % cap


def last_lane(x):
    return jnp.broadcast_to(x[:, LANES - 1 : LANES], x.shape)


def column(row, rows):
    square = (rows, rows)
    here = lax.broadcasted_iota(jnp.int32, square, 0) == lax.broadcasted_iota(jnp.int32, square, 1)
    values = jnp.sum(jnp.where(here, jnp.broadcast_to(row, square), 0.0), axis=1, keepdims=True)
    return jnp.broadcast_to(values, (rows, LANES))


def tile(ref, line, comps, group):
    return ref[pl.ds(line * comps, comps), group * LANES : (group + 1) * LANES]


def put(ref, line, comps, group, value):
    ref[pl.ds(line * comps, comps), group * LANES : (group + 1) * LANES] = value


def level_rows(levels, level, line, comps, group):
    return levels[level, pl.ds(line * comps, comps), group * LANES : (group + 1) * LANES]


LEVELS = 7


def scan_line(levels, retain, values, line, comps, groups):
    offsets = []
    for group in range(groups):
        offset = (1.0 - tile(retain, line, comps, group)) * values[group]
        for level in range(LEVELS):
            offset = offset + level_rows(levels, level, line, comps, group) * pltpu.roll(
                offset, 1 << level, 1
            )
        offsets.append(offset)
    carry = last_lane(offsets[0])
    done = [offsets[0]]
    for group in range(1, groups):
        done.append(offsets[group] + level_rows(levels, LEVELS, line, comps, group) * carry)
        if group < groups - 1:
            carry = (
                last_lane(offsets[group])
                + level_rows(levels, LEVELS + 1, line, comps, group) * carry
            )
    return done


def tap_columns(wide_taps):
    return [wide_taps[t] for t in range(wide_taps.shape[0])]


def correlate(tiles, columns, lane):
    count = len(tiles)
    shifted = [tiles]
    for b in range(1, RADIX):
        row = []
        for j in range(count):
            x = tiles[j]
            y = jnp.where(lane < b, tiles[j + 1] if j + 1 < count else 0.0, x)
            row.append(pltpu.roll(y, LANES - b, 1))
        shifted.append(row)
    early = [None] + [
        jnp.where(lane >= LANES - b, pltpu.roll(tiles[0], LANES - b, 1), 0.0) for b in range(1, RADIX)
    ]

    def mix(a, values):
        total = None
        for b in range(RADIX):
            t = RADIX * a + b + HALF
            if t < len(columns) and values[b] is not None:
                term = columns[t] * values[b]
                total = term if total is None else total + term
        return total

    spans = range(-(HALF // RADIX), HALF // RADIX + 1)
    outs = [None] * count
    for a in spans:
        parts = [mix(a, [shifted[b][j] for b in range(RADIX)]) for j in range(count)]
        for j in range(count):
            if a == 0:
                y = parts[j]
            elif a > 0:
                after = parts[j + 1] if j + 1 < count else 0.0
                y = pltpu.roll(jnp.where(lane < RADIX * a, after, parts[j]), LANES - RADIX * a, 1)
            else:
                before = parts[j - 1] if j else mix(a, early)
                y = pltpu.roll(
                    jnp.where(lane >= LANES + RADIX * a, before, parts[j]), -RADIX * a, 1
                )
            outs[j] = y if outs[j] is None else outs[j] + y
    return outs


def correlate_ring(x, columns):
    shifted = [x] + [pltpu.roll(x, LANES - b, 1) for b in range(1, RADIX)]
    out = None
    for a in range(-(HALF // RADIX), HALF // RADIX + 1):
        total = None
        for b in range(RADIX):
            t = RADIX * a + b + HALF
            if t < len(columns):
                term = columns[t] * shifted[b]
                total = term if total is None else total + term
        if a:
            total = pltpu.roll(total, (-RADIX * a) % LANES, 1)
        out = total if out is None else out + total
    return out


def pack_ends(line, lane, first, last):
    at = 2 * HALF * line
    both = jnp.where(lane < LANES // 2, first, last)
    both = pltpu.roll(both, (HALF + at) % LANES, 1)
    return both, (lane >= at) & (lane < at + 2 * HALF)


def unpack_ends(line, packed):
    return pltpu.roll(packed, (-(HALF + 2 * HALF * line)) % LANES, 1)


def first_kernel(
    lines, comps, groups, conc, slowness, retard, taps, inlet, order,
    retain, levels, offset, factor, ends, wide_taps, wide_inlet,
):
    lane = lax.broadcasted_iota(jnp.int32, (comps, LANES), 1)
    slow_by = column(retard[...], comps)
    packed = [jnp.zeros((comps, LANES), F32)] * 2
    for t in range(taps.shape[1]):
        wide_taps[t] = jnp.broadcast_to(taps[:, t : t + 1], (comps, LANES))
    for line in range(lines):
        wide_inlet[pl.ds(line * comps, comps), :] = column(inlet[line : line + 1, :], comps)
    for line in range(lines):
        values, whole = [], []
        for group in range(groups):
            s = slowness[pl.ds(line, 1), group * LANES : (group + 1) * LANES]
            r = 1.0 / (1.0 + slow_by * s)
            put(retain, line, comps, group, r)
            rows = pl.ds(line * comps, comps)
            span = slice(group * LANES, (group + 1) * LANES)
            f = r
            for level in range(LEVELS):
                inside = lane >= (1 << level)
                levels[level, rows, span] = jnp.where(inside, f, 0.0)
                f = jnp.where(inside, f * pltpu.roll(f, 1 << level, 1), f)
            levels[LEVELS, rows, span] = f
            end = last_lane(f)
            levels[LEVELS + 1, rows, span] = end
            if group:
                f = f * carry
                carry = carry * end
            else:
                carry = end
            put(factor, line, comps, group, f)
            whole.append(f)
            values.append(conc[line, :, span])
        offsets = scan_line(levels, retain, values, line, comps, groups)
        for group in range(groups):
            put(offset, line, comps, group, offsets[group])
        part, inside = pack_ends(line, lane, offsets[0], offsets[-1])
        packed[0] = jnp.where(inside, part, packed[0])
        part, inside = pack_ends(line, lane, whole[0], whole[-1])
        packed[1] = jnp.where(inside, part, packed[1])
    ends[0] = packed[0]
    ends[1] = packed[1]


def taps_kernel(lines, comps, groups, sources, taps, *refs):
    lane = lax.broadcasted_iota(jnp.int32, (comps, LANES), 1)
    columns = tap_columns(taps)
    for source, out in zip(refs[:sources], refs[sources:]):
        for line in range(lines):
            tiles = [tile(source, line, comps, group) for group in range(groups)]
            sums = correlate(tiles, columns, lane)
            for group in range(groups):
                put(out, line, comps, group, tiles[group] + sums[group])


def place(send, slot, b, cap, comps, value):
    owner, rank = where_slot(slot, b, cap)
    send[owner, pl.ds(pl.multiple_of((cap + rank) * comps, 8), comps), :] = value


def finish_kernel(
    lines, comps, groups, cap, segs, has_gather, first,
    local, carried, end_offset, end_factor, other_offset, other_factor, taps, inlet, *rest,
):
    if first:
        (spread,) = rest
    else:
        slot, looked, spread, send = rest
    me = lax.axis_index("seg")
    lane = lax.broadcasted_iota(jnp.int32, (comps, LANES), 1)
    columns = tap_columns(taps)
    for line in range(lines):
        rows = pl.ds(line * comps, comps)

        def part(s):
            if has_gather:
                pair = other_offset[s], other_factor[s]
            else:
                mine = me == s
                pair = (
                    jnp.where(mine, end_offset[0], other_offset[0]),
                    jnp.where(mine, end_factor[1], other_factor[1]),
                )
            return [unpack_ends(line, x) for x in pair]

        flow = inlet[rows, :]
        zero = jnp.zeros((comps, LANES), F32)
        left, right, inflow = zero, zero, zero
        for s in range(segs):
            inflow = jnp.where(me == s, flow, inflow)
            off, fac = part(s)
            edge = off + fac * flow
            left = jnp.where(me == s + 1, edge, left)
            right = jnp.where(me == s - 1, edge, right)
            if s < segs - 1:
                flow = last_lane(edge)
        ring = jnp.where(lane >= LANES - HALF, left, 0.0)
        ring = jnp.where((lane >= 48) & (lane < 48 + HALF), pltpu.roll(right, 48, 1), ring)
        ring = correlate_ring(ring, columns)
        for group in range(groups):
            total = tile(local, line, comps, group) + tile(carried, line, comps, group) * inflow
            if group == 0:
                total = total + jnp.where(lane < HALF, ring, 0.0)
            if group == groups - 1:
                total = total + jnp.where(lane >= LANES - HALF, pltpu.roll(ring, 80, 1), 0.0)
            put(spread, line, comps, group, total)
    if first:
        return
    send[:, 0 : cap * comps, :] = looked[...]
    for b in range(lines * groups):
        place(send, slot, b, cap, comps, tile(spread, b // groups, comps, b % groups))


def conc_kernel(lines, comps, groups, cap, first, last, spread, got, coupling, retain, levels, slot, *outs):
    lane = lax.broadcasted_iota(jnp.int32, (comps, LANES), 1)
    outs = list(outs)
    coupling_out = outs.pop() if first else None
    packed = jnp.zeros((comps, LANES), F32)
    for line in range(lines):
        values = []
        for group in range(groups):
            b = line * groups + group
            owner, rank = where_slot(slot, b, cap)
            looked = got[owner, pl.ds(pl.multiple_of(rank * comps, 8), comps), :]
            if first:
                rate = got[owner, pl.ds(2 * cap * comps + rank, 1), :]
                coupling_out[pl.ds(b, 1), :] = rate
            else:
                rate = coupling[pl.ds(b, 1), :]
            s = tile(spread, line, comps, group)
            value = s + rate * (looked - s)
            if last:
                outs[0][line, :, group * LANES : (group + 1) * LANES] = value
            values.append(value)
        if last:
            continue
        offsets = scan_line(levels, retain, values, line, comps, groups)
        for group in range(groups):
            put(outs[0], line, comps, group, offsets[group])
        part, inside = pack_ends(line, lane, offsets[0], offsets[-1])
        packed = jnp.where(inside, part, packed)
    if not last:
        outs[1][0] = packed


def gather_cells(grid, cell, comps, high_total):
    low = jnp.broadcast_to(cell & (LANES - 1), (comps, LANES))
    high = jnp.broadcast_to(cell >> 7, (comps, LANES))
    out = jnp.zeros((comps, LANES), F32)
    for h in range(high_total):
        g = jnp.take_along_axis(
            grid[:, h * LANES : (h + 1) * LANES], low, axis=1, mode="promise_in_bounds"
        )
        out = jnp.where(high == h, g, out)
    return out


def look_first_kernel(groups, cap, cells, grid, kappa, spread, slot, rates, send):
    comps = grid.shape[0]
    high_total = grid.shape[1] // LANES
    row = lax.broadcasted_iota(jnp.int32, (high_total, LANES), 0)

    for owner in range(cells.shape[0]):
        for rank in range(cap):
            cell = cells[owner, rank : rank + 1, :]
            valid = cell >= 0
            cell = jnp.maximum(cell, 0)
            send[owner, rank * comps : (rank + 1) * comps, :] = gather_cells(
                grid, cell, comps, high_total
            )
            low = jnp.broadcast_to(cell & (LANES - 1), (high_total, LANES))
            k = jnp.take_along_axis(kappa[...], low, axis=1, mode="promise_in_bounds")
            rate = jnp.sum(jnp.where(row == (cell >> 7), k, 0.0), axis=0, keepdims=True)
            rate = jnp.where(valid, rate, 0.0)
            rates[owner, rank : rank + 1, :] = rate
            at = 2 * cap * comps + rank
            send[owner, at : at + 1, :] = rate
    for b in range(slot.shape[0]):
        place(send, slot, b, cap, comps, tile(spread, b // groups, comps, b % groups))


def onehot_kernel(cap, cells, order, onehot):
    wide = onehot.shape[0]
    row = lax.broadcasted_iota(jnp.int32, (wide, LANES), 0)
    for owner in range(cells.shape[0]):
        for rank in range(cap):
            cell = cells[owner, rank : rank + 1, :]
            at = (owner * cap + rank) * LANES
            onehot[:, at : at + LANES] = jnp.where(row == (cell & (wide - 1)), 1.0, 0.0).astype(BF16)


def in_two(x):
    coarse = x.astype(BF16)
    return coarse, (x - coarse.astype(F32)).astype(BF16)


def update_kernel(cap, chunk, last, cells, got, looked, rates, onehot, grid, *rest):
    if last:
        grid_out, masked = rest
    else:
        grid_out, looked_out, masked, stack = rest
    comps = grid.shape[0]
    wide = onehot.shape[0]
    bits = wide.bit_length() - 1
    high_total = grid.shape[1] // wide
    owners_total = cells.shape[0]
    rows = high_total * comps
    width = chunk * cap * LANES
    total = None
    for start in range(0, owners_total, chunk):
        turn = (start // chunk) % masked.shape[0]
        for i in range(chunk):
            owner = start + i
            for rank in range(cap):
                at = (i * cap + rank) * LANES
                cell = cells[owner, rank : rank + 1, :]
                valid = jnp.broadcast_to(cell, (comps, LANES)) >= 0
                cell = jnp.maximum(cell, 0)
                rate = rates[owner, rank : rank + 1, :]
                span = slice(rank * comps, (rank + 1) * comps)
                came = slice((cap + rank) * comps, (cap + rank + 1) * comps)
                flux = jnp.where(valid, rate * (looked[owner, span, :] - got[owner, came, :]), 0.0)
                coarse, fine = in_two(flux)
                high = jnp.broadcast_to((cell >> bits).astype(F32), (comps, LANES)).astype(BF16)
                for h in range(high_total):
                    hit = high == jnp.asarray(h, BF16)
                    masked[turn, h * comps : (h + 1) * comps, at : at + LANES] = jnp.where(
                        hit, coarse, jnp.zeros_like(coarse)
                    )
                    masked[turn, rows + h * comps : rows + (h + 1) * comps, at : at + LANES] = (
                        jnp.where(hit, fine, jnp.zeros_like(fine))
                    )
        first = start * cap * LANES
        part = lax.dot_general(
            masked[turn], onehot[:, first : first + width], (((1,), (1,)), ((), ())),
            preferred_element_type=F32,
        )
        total = part if total is None else total + part
    for h in range(high_total):
        span = slice(h * wide, (h + 1) * wide)
        at = slice(h * comps, (h + 1) * comps)
        at2 = slice(rows + h * comps, rows + (h + 1) * comps)
        grid_out[:, span] = grid[:, span] - 0.25 * (total[at, :] + total[at2, :])
    if last:
        return

    for h in range(high_total):
        coarse, fine = in_two(grid_out[:, h * wide : (h + 1) * wide])
        stack[h * comps : (h + 1) * comps, :] = coarse
        stack[rows + h * comps : rows + (h + 1) * comps, :] = fine
    for first in range(0, owners_total * cap, 4):
        part = jnp.dot(
            stack[...], onehot[:, first * LANES : (first + 4) * LANES], preferred_element_type=F32
        )
        for i in range(4):
            owner, rank = (first + i) // cap, (first + i) % cap
            cell = jnp.maximum(cells[owner, rank : rank + 1, :], 0)
            high = jnp.broadcast_to(cell >> bits, (comps, LANES))
            span = slice(i * LANES, (i + 1) * LANES)
            found = jnp.zeros((comps, LANES), F32)
            for h in range(high_total):
                at = slice(h * comps, (h + 1) * comps)
                at2 = slice(rows + h * comps, rows + (h + 1) * comps)
                found = jnp.where(high == h, part[at, span] + part[at2, span], found)
            looked_out[owner, rank * comps : (rank + 1) * comps, :] = found


def swap(x, segs):
    if segs == 2:
        return lax.ppermute(x, "seg", [(0, 1), (1, 0)])
    return lax.all_gather(x, "seg")


def exchange(x):
    return lax.all_to_all(x, "bundle", split_axis=0, concat_axis=0, tiled=True)


def per_device(conc, slowness, retard, taps, inlet, grid, kappa, owners, cells):
    lines, comps, nodes = conc.shape
    groups = nodes // LANES
    blocks = lines * groups
    segs = lax.axis_size("seg")
    owners_total = lax.axis_size("bundle")
    cap = max(2, 2 * blocks // owners_total)
    rows = lines * comps
    cell_count = grid.shape[1]
    chunk = 4 if owners_total % 4 == 0 else owners_total
    half = cap * comps
    extra = 8 * (-(-cap // 8))

    slot, cell_send = call(
        functools.partial(route_kernel, groups, cap),
        [sds((blocks, LANES), jnp.int32), sds((owners_total, 8 * (-(-cap // 8)), LANES), jnp.int32)],
        [(jnp.swapaxes(owners, 2, 3), VMEM), (cells, VMEM)],
        scratch=[pltpu.SMEM((owners_total,), jnp.int32)],
        flops=1e9,
    )
    cell_recv = exchange(cell_send)

    retain, levels, offset, factor, ends, taps, inlet = call(
        functools.partial(first_kernel, lines, comps, groups),
        [
            sds((rows, nodes)), sds((LEVELS + 2, rows, nodes)), sds((rows, nodes)),
            sds((rows, nodes)), sds((2, comps, LANES)), sds((taps.shape[1], comps, LANES)),
            sds((rows, LANES)),
        ],
        [
            (conc, VMEM), (slowness, VMEM), (retard.reshape(1, comps), VMEM), (taps, VMEM),
            (inlet, VMEM), (slot, ANY),
        ],
    )
    first_ends = ends
    other = swap(ends, segs)
    if segs == 2:
        other_offset = other_factor = other
    else:
        other_offset, other_factor = other[:, 0], other[:, 1]
    local, carried = call(
        functools.partial(taps_kernel, lines, comps, groups, 2),
        [sds((rows, nodes))] * 2,
        [(taps, VMEM), (offset, VMEM), (factor, VMEM)],
    )

    def finish(looked):
        first = looked is None
        ins = [
            (local, VMEM), (carried, VMEM), (ends, VMEM), (first_ends, VMEM),
            (other_offset, VMEM), (other_factor, VMEM), (taps, VMEM), (inlet, VMEM),
        ]
        outs = [sds((rows, nodes))]
        if not first:
            ins += [(slot, VMEM), (looked, VMEM)]
            outs.append(sds((owners_total, 2 * half, LANES)))
        return call(
            functools.partial(finish_kernel, lines, comps, groups, cap, segs, segs != 2, first),
            outs, ins,
        )

    (spread,) = finish(None)
    rates, send = call(
        functools.partial(look_first_kernel, groups, cap),
        [
            sds((owners_total, cap, LANES)), sds((owners_total, 2 * half + extra, LANES)),
        ],
        [
            (cell_recv, VMEM), (grid, VMEM), (kappa.reshape(cell_count // LANES, LANES), VMEM),
            (spread, VMEM), (slot, VMEM),
        ],
    )
    looked = send
    wide = 256 if cell_count % 256 == 0 else LANES
    coupling = slowness
    for step in range(STEPS):
        last = step == STEPS - 1
        got = exchange(send)
        outs = [sds(conc.shape)] if last else [sds((rows, nodes)), sds((1, comps, LANES))]
        if step == 0:
            outs.append(sds((blocks, LANES)))
        result = call(
            functools.partial(conc_kernel, lines, comps, groups, cap, step == 0, last),
            outs,
            [
                (spread, VMEM), (got, VMEM), (coupling, VMEM), (retain, VMEM), (levels, VMEM),
                (slot, VMEM),
            ],
        )
        if step == 0:
            coupling = result[-1]
        if last:
            conc_out = result[0]
        else:
            offset, ends = result[0], result[1]
            got_ends = swap(ends, segs)
            other_offset = got_ends if segs == 2 else got_ends[:, 0]
        if step == 0:
            (onehot,) = call(
                functools.partial(onehot_kernel, cap),
                [sds((wide, owners_total * cap * LANES), BF16)],
                [(cell_recv, VMEM), (ends, ANY)],
            )
        outs = [sds(grid.shape)]
        if not last:
            outs.append(sds((owners_total, half, LANES)))
        result = call(
            functools.partial(update_kernel, cap, chunk, last),
            outs,
            [
                (cell_recv, VMEM), (got, VMEM), (looked, VMEM), (rates, VMEM), (onehot, VMEM),
                (grid, VMEM),
            ],
            scratch=[
                pltpu.VMEM(
                    (
                        min(4, owners_total // chunk),
                        2 * (cell_count // wide) * comps,
                        chunk * cap * LANES,
                    ),
                    BF16,
                )
            ]
            + ([] if last else [pltpu.VMEM((2 * (cell_count // wide) * comps, wide), BF16)]),
        )
        grid = result[0]
        if not last:
            looked = result[1]
            (local,) = call(
                functools.partial(taps_kernel, lines, comps, groups, 1),
                [sds((rows, nodes))],
                [(taps, VMEM), (offset, VMEM)],
            )
            spread, send = finish(looked)
    return (conc_out, grid)


def solution(mesh):
    return jax.shard_map(
        per_device,
        mesh=mesh,
        in_specs=(
            P("bundle", None, "seg"),
            P("bundle", "seg"),
            P(),
            P(),
            P("bundle", None),
            P(None, ("seg", "bundle")),
            P(("seg", "bundle")),
            P("seg", "bundle", None, None),
            P("bundle", "seg"),
        ),
        out_specs=(P("bundle", None, "seg"), P(None, ("seg", "bundle"))),
        check_vma=False,
    )
```

```python
import functools

import jax
import jax.numpy as jnp
from jax import lax
from jax.experimental import pallas as pl
from jax.experimental.pallas import tpu as pltpu
from jax.sharding import PartitionSpec as P

STEPS = 4
LANES = 128
HALF = 16
RADIX = 4
F32 = jnp.float32
BF16 = jnp.bfloat16

VMEM = pl.BlockSpec(memory_space=pltpu.VMEM)
SMEM = pl.BlockSpec(memory_space=pltpu.SMEM)
ANY = pl.BlockSpec(memory_space=pl.ANY)


def call(kernel, outs, ins, out_specs=None, scratch=(), flops=1):
    args = [a for a, _ in ins]
    return pl.pallas_call(
        kernel,
        out_shape=outs,
        in_specs=[s for _, s in ins],
        out_specs=out_specs or [VMEM] * len(outs),
        scratch_shapes=list(scratch),
        cost_estimate=pl.CostEstimate(flops=int(flops), bytes_accessed=1, transcendentals=0),
        compiler_params=pltpu.CompilerParams(vmem_limit_bytes=40 * 1024 * 1024),
    )(*args)


def sds(shape, dtype=F32):
    return jax.ShapeDtypeStruct(shape, dtype)


def route_kernel(groups, cap, owners, cells, slot, send, count):
    blocks = slot.shape[0]
    owners_total = send.shape[0]
    send[...] = jnp.full(send.shape, -1, jnp.int32)
    for o in range(owners_total):
        count[o] = 0
    for b in range(blocks):
        line, group = b // groups, b % groups
        owner = owners[0, line, 0, group]
        rank = count[owner]
        count[owner] = rank + 1
        slot[b : b + 1, :] = jnp.full((1, LANES), owner * cap + rank, jnp.int32)
        send[owner, pl.ds(rank, 1), :] = cells[
            pl.ds(line, 1), group * LANES : (group + 1) * LANES
        ]


def where_slot(slot, b, cap):
    s = slot[b, 0]
    return s // cap, s % cap


def last_lane(x):
    return jnp.broadcast_to(x[:, LANES - 1 : LANES], x.shape)


def column(row, rows):
    square = (rows, rows)
    here = lax.broadcasted_iota(jnp.int32, square, 0) == lax.broadcasted_iota(jnp.int32, square, 1)
    values = jnp.sum(jnp.where(here, jnp.broadcast_to(row, square), 0.0), axis=1, keepdims=True)
    return jnp.broadcast_to(values, (rows, LANES))


def tile(ref, line, comps, group):
    return ref[pl.ds(line * comps, comps), group * LANES : (group + 1) * LANES]


def put(ref, line, comps, group, value):
    ref[pl.ds(line * comps, comps), group * LANES : (group + 1) * LANES] = value


def level_rows(levels, level, line, comps, group):
    return levels[level, pl.ds(line * comps, comps), group * LANES : (group + 1) * LANES]


LEVELS = 7


def scan_line(levels, retain, values, line, comps, groups):
    offsets = []
    for group in range(groups):
        offset = (1.0 - tile(retain, line, comps, group)) * values[group]
        for level in range(LEVELS):
            offset = offset + level_rows(levels, level, line, comps, group) * pltpu.roll(
                offset, 1 << level, 1
            )
        offsets.append(offset)
    carry = last_lane(offsets[0])
    done = [offsets[0]]
    for group in range(1, groups):
        done.append(offsets[group] + level_rows(levels, LEVELS, line, comps, group) * carry)
        if group < groups - 1:
            carry = (
                last_lane(offsets[group])
                + level_rows(levels, LEVELS + 1, line, comps, group) * carry
            )
    return done


def tap_columns(wide_taps):
    return [wide_taps[t] for t in range(wide_taps.shape[0])]


def correlate(tiles, columns, lane):
    count = len(tiles)
    shifted = [tiles]
    for b in range(1, RADIX):
        row = []
        for j in range(count):
            x = tiles[j]
            y = jnp.where(lane < b, tiles[j + 1] if j + 1 < count else 0.0, x)
            row.append(pltpu.roll(y, LANES - b, 1))
        shifted.append(row)
    early = [None] + [
        jnp.where(lane >= LANES - b, pltpu.roll(tiles[0], LANES - b, 1), 0.0) for b in range(1, RADIX)
    ]

    def mix(a, values):
        total = None
        for b in range(RADIX):
            t = RADIX * a + b + HALF
            if t < len(columns) and values[b] is not None:
                term = columns[t] * values[b]
                total = term if total is None else total + term
        return total

    spans = range(-(HALF // RADIX), HALF // RADIX + 1)
    outs = [None] * count
    for a in spans:
        parts = [mix(a, [shifted[b][j] for b in range(RADIX)]) for j in range(count)]
        for j in range(count):
            if a == 0:
                y = parts[j]
            elif a > 0:
                after = parts[j + 1] if j + 1 < count else 0.0
                y = pltpu.roll(jnp.where(lane < RADIX * a, after, parts[j]), LANES - RADIX * a, 1)
            else:
                before = parts[j - 1] if j else mix(a, early)
                y = pltpu.roll(
                    jnp.where(lane >= LANES + RADIX * a, before, parts[j]), -RADIX * a, 1
                )
            outs[j] = y if outs[j] is None else outs[j] + y
    return outs


def correlate_ring(x, columns):
    shifted = [x] + [pltpu.roll(x, LANES - b, 1) for b in range(1, RADIX)]
    out = None
    for a in range(-(HALF // RADIX), HALF // RADIX + 1):
        total = None
        for b in range(RADIX):
            t = RADIX * a + b + HALF
            if t < len(columns):
                term = columns[t] * shifted[b]
                total = term if total is None else total + term
        if a:
            total = pltpu.roll(total, (-RADIX * a) % LANES, 1)
        out = total if out is None else out + total
    return out


def pack_ends(line, lane, first, last):
    at = 2 * HALF * line
    both = jnp.where(lane < LANES // 2, first, last)
    both = pltpu.roll(both, (HALF + at) % LANES, 1)
    return both, (lane >= at) & (lane < at + 2 * HALF)


def unpack_ends(line, packed):
    return pltpu.roll(packed, (-(HALF + 2 * HALF * line)) % LANES, 1)


def first_kernel(
    lines, comps, groups, conc, slowness, retard, taps, inlet, order,
    retain, levels, offset, factor, ends, wide_taps, wide_inlet,
):
    lane = lax.broadcasted_iota(jnp.int32, (comps, LANES), 1)
    slow_by = column(retard[...], comps)
    packed = [jnp.zeros((comps, LANES), F32)] * 2
    for t in range(taps.shape[1]):
        wide_taps[t] = jnp.broadcast_to(taps[:, t : t + 1], (comps, LANES))
    for line in range(lines):
        wide_inlet[pl.ds(line * comps, comps), :] = column(inlet[line : line + 1, :], comps)
    for line in range(lines):
        values, whole = [], []
        for group in range(groups):
            s = slowness[pl.ds(line, 1), group * LANES : (group + 1) * LANES]
            r = 1.0 / (1.0 + slow_by * s)
            put(retain, line, comps, group, r)
            rows = pl.ds(line * comps, comps)
            span = slice(group * LANES, (group + 1) * LANES)
            f = r
            for level in range(LEVELS):
                inside = lane >= (1 << level)
                levels[level, rows, span] = jnp.where(inside, f, 0.0)
                f = jnp.where(inside, f * pltpu.roll(f, 1 << level, 1), f)
            levels[LEVELS, rows, span] = f
            end = last_lane(f)
            levels[LEVELS + 1, rows, span] = end
            if group:
                f = f * carry
                carry = carry * end
            else:
                carry = end
            put(factor, line, comps, group, f)
            whole.append(f)
            values.append(conc[line, :, span])
        offsets = scan_line(levels, retain, values, line, comps, groups)
        for group in range(groups):
            put(offset, line, comps, group, offsets[group])
        part, inside = pack_ends(line, lane, offsets[0], offsets[-1])
        packed[0] = jnp.where(inside, part, packed[0])
        part, inside = pack_ends(line, lane, whole[0], whole[-1])
        packed[1] = jnp.where(inside, part, packed[1])
    ends[0] = packed[0]
    ends[1] = packed[1]


def taps_kernel(lines, comps, groups, sources, taps, *refs):
    lane = lax.broadcasted_iota(jnp.int32, (comps, LANES), 1)
    columns = tap_columns(taps)
    for source, out in zip(refs[:sources], refs[sources:]):
        for line in range(lines):
            tiles = [tile(source, line, comps, group) for group in range(groups)]
            sums = correlate(tiles, columns, lane)
            for group in range(groups):
                put(out, line, comps, group, tiles[group] + sums[group])


def place(send, slot, b, cap, comps, value):
    owner, rank = where_slot(slot, b, cap)
    send[owner, pl.ds(pl.multiple_of((cap + rank) * comps, 8), comps), :] = value


def finish_kernel(
    lines, comps, groups, cap, segs, has_gather, first,
    local, carried, end_offset, end_factor, other_offset, other_factor, taps, inlet, *rest,
):
    if first:
        (spread,) = rest
    else:
        slot, looked, spread, send = rest
    me = lax.axis_index("seg")
    lane = lax.broadcasted_iota(jnp.int32, (comps, LANES), 1)
    columns = tap_columns(taps)
    for line in range(lines):
        rows = pl.ds(line * comps, comps)

        def part(s):
            if has_gather:
                pair = other_offset[s], other_factor[s]
            else:
                mine = me == s
                pair = (
                    jnp.where(mine, end_offset[0], other_offset[0]),
                    jnp.where(mine, end_factor[1], other_factor[1]),
                )
            return [unpack_ends(line, x) for x in pair]

        flow = inlet[rows, :]
        zero = jnp.zeros((comps, LANES), F32)
        left, right, inflow = zero, zero, zero
        for s in range(segs):
            inflow = jnp.where(me == s, flow, inflow)
            off, fac = part(s)
            edge = off + fac * flow
            left = jnp.where(me == s + 1, edge, left)
            right = jnp.where(me == s - 1, edge, right)
            if s < segs - 1:
                flow = last_lane(edge)
        ring = jnp.where(lane >= LANES - HALF, left, 0.0)
        ring = jnp.where((lane >= 48) & (lane < 48 + HALF), pltpu.roll(right, 48, 1), ring)
        ring = correlate_ring(ring, columns)
        for group in range(groups):
            total = tile(local, line, comps, group) + tile(carried, line, comps, group) * inflow
            if group == 0:
                total = total + jnp.where(lane < HALF, ring, 0.0)
            if group == groups - 1:
                total = total + jnp.where(lane >= LANES - HALF, pltpu.roll(ring, 80, 1), 0.0)
            put(spread, line, comps, group, total)
    if first:
        return
    send[:, 0 : cap * comps, :] = looked[...]
    for b in range(lines * groups):
        place(send, slot, b, cap, comps, tile(spread, b // groups, comps, b % groups))


def conc_kernel(lines, comps, groups, cap, first, last, spread, got, coupling, retain, levels, slot, *outs):
    lane = lax.broadcasted_iota(jnp.int32, (comps, LANES), 1)
    outs = list(outs)
    coupling_out = outs.pop() if first else None
    packed = jnp.zeros((comps, LANES), F32)
    for line in range(lines):
        values = []
        for group in range(groups):
            b = line * groups + group
            owner, rank = where_slot(slot, b, cap)
            looked = got[owner, pl.ds(pl.multiple_of(rank * comps, 8), comps), :]
            if first:
                rate = got[owner, pl.ds(2 * cap * comps + rank, 1), :]
                coupling_out[pl.ds(b, 1), :] = rate
            else:
                rate = coupling[pl.ds(b, 1), :]
            s = tile(spread, line, comps, group)
            value = s + rate * (looked - s)
            if last:
                outs[0][line, :, group * LANES : (group + 1) * LANES] = value
            values.append(value)
        if last:
            continue
        offsets = scan_line(levels, retain, values, line, comps, groups)
        for group in range(groups):
            put(outs[0], line, comps, group, offsets[group])
        part, inside = pack_ends(line, lane, offsets[0], offsets[-1])
        packed = jnp.where(inside, part, packed)
    if not last:
        outs[1][0] = packed


def gather_cells(grid, cell, comps, high_total):
    low = jnp.broadcast_to(cell & (LANES - 1), (comps, LANES))
    high = jnp.broadcast_to(cell >> 7, (comps, LANES))
    out = jnp.zeros((comps, LANES), F32)
    for h in range(high_total):
        g = jnp.take_along_axis(
            grid[:, h * LANES : (h + 1) * LANES], low, axis=1, mode="promise_in_bounds"
        )
        out = jnp.where(high == h, g, out)
    return out


def look_first_kernel(groups, cap, cells, grid, kappa, spread, slot, rates, send):
    comps = grid.shape[0]
    high_total = grid.shape[1] // LANES
    row = lax.broadcasted_iota(jnp.int32, (high_total, LANES), 0)

    for owner in range(cells.shape[0]):
        for rank in range(cap):
            cell = cells[owner, rank : rank + 1, :]
            valid = cell >= 0
            cell = jnp.maximum(cell, 0)
            send[owner, rank * comps : (rank + 1) * comps, :] = gather_cells(
                grid, cell, comps, high_total
            )
            low = jnp.broadcast_to(cell & (LANES - 1), (high_total, LANES))
            k = jnp.take_along_axis(kappa[...], low, axis=1, mode="promise_in_bounds")
            rate = jnp.sum(jnp.where(row == (cell >> 7), k, 0.0), axis=0, keepdims=True)
            rate = jnp.where(valid, rate, 0.0)
            rates[owner, rank : rank + 1, :] = rate
            at = 2 * cap * comps + rank
            send[owner, at : at + 1, :] = rate
    for b in range(slot.shape[0]):
        place(send, slot, b, cap, comps, tile(spread, b // groups, comps, b % groups))


def onehot_kernel(cap, cells, order, onehot):
    wide = onehot.shape[0]
    row = lax.broadcasted_iota(jnp.int32, (wide, LANES), 0)
    for owner in range(cells.shape[0]):
        for rank in range(cap):
            cell = cells[owner, rank : rank + 1, :]
            at = (owner * cap + rank) * LANES
            onehot[:, at : at + LANES] = jnp.where(row == (cell & (wide - 1)), 1.0, 0.0).astype(BF16)


def in_two(x):
    coarse = x.astype(BF16)
    return coarse, (x - coarse.astype(F32)).astype(BF16)


def update_kernel(cap, chunk, cells, got, looked, rates, onehot, grid, grid_out, masked):
    comps = grid.shape[0]
    wide = onehot.shape[0]
    bits = wide.bit_length() - 1
    high_total = grid.shape[1] // wide
    owners_total = cells.shape[0]
    rows = high_total * comps
    width = chunk * cap * LANES
    total = None
    for start in range(0, owners_total, chunk):
        turn = (start // chunk) % masked.shape[0]
        for i in range(chunk):
            owner = start + i
            for rank in range(cap):
                at = (i * cap + rank) * LANES
                cell = cells[owner, rank : rank + 1, :]
                valid = jnp.broadcast_to(cell, (comps, LANES)) >= 0
                cell = jnp.maximum(cell, 0)
                rate = rates[owner, rank : rank + 1, :]
                span = slice(rank * comps, (rank + 1) * comps)
                came = slice((cap + rank) * comps, (cap + rank + 1) * comps)
                flux = jnp.where(valid, rate * (looked[owner, span, :] - got[owner, came, :]), 0.0)
                coarse, fine = in_two(flux)
                high = jnp.broadcast_to((cell >> bits).astype(F32), (comps, LANES)).astype(BF16)
                for h in range(high_total):
                    hit = high == jnp.asarray(h, BF16)
                    masked[turn, h * comps : (h + 1) * comps, at : at + LANES] = jnp.where(
                        hit, coarse, jnp.zeros_like(coarse)
                    )
                    masked[turn, rows + h * comps : rows + (h + 1) * comps, at : at + LANES] = (
                        jnp.where(hit, fine, jnp.zeros_like(fine))
                    )
        first = start * cap * LANES
        part = lax.dot_general(
            masked[turn], onehot[:, first : first + width], (((1,), (1,)), ((), ())),
            preferred_element_type=F32,
        )
        total = part if total is None else total + part
    for h in range(high_total):
        span = slice(h * wide, (h + 1) * wide)
        at = slice(h * comps, (h + 1) * comps)
        at2 = slice(rows + h * comps, rows + (h + 1) * comps)
        grid_out[:, span] = grid[:, span] - 0.25 * (total[at, :] + total[at2, :])


def look_kernel(cap, cells, onehot, grid, looked, stack):
    comps = grid.shape[0]
    wide = onehot.shape[0]
    bits = wide.bit_length() - 1
    high_total = grid.shape[1] // wide
    owners_total = cells.shape[0]
    rows = high_total * comps
    for h in range(high_total):
        coarse, fine = in_two(grid[:, h * wide : (h + 1) * wide])
        stack[h * comps : (h + 1) * comps, :] = coarse
        stack[rows + h * comps : rows + (h + 1) * comps, :] = fine
    for first in range(0, owners_total * cap, 4):
        part = jnp.dot(
            stack[...], onehot[:, first * LANES : (first + 4) * LANES], preferred_element_type=F32
        )
        for i in range(4):
            owner, rank = (first + i) // cap, (first + i) % cap
            cell = jnp.maximum(cells[owner, rank : rank + 1, :], 0)
            high = jnp.broadcast_to(cell >> bits, (comps, LANES))
            span = slice(i * LANES, (i + 1) * LANES)
            found = jnp.zeros((comps, LANES), F32)
            for h in range(high_total):
                at = slice(h * comps, (h + 1) * comps)
                at2 = slice(rows + h * comps, rows + (h + 1) * comps)
                found = jnp.where(high == h, part[at, span] + part[at2, span], found)
            looked[owner, rank * comps : (rank + 1) * comps, :] = found


def swap(x, segs):
    if segs == 2:
        return lax.ppermute(x, "seg", [(0, 1), (1, 0)])
    return lax.all_gather(x, "seg")


def exchange(x):
    return lax.all_to_all(x, "bundle", split_axis=0, concat_axis=0, tiled=True)


def per_device(conc, slowness, retard, taps, inlet, grid, kappa, owners, cells):
    lines, comps, nodes = conc.shape
    groups = nodes // LANES
    blocks = lines * groups
    segs = lax.axis_size("seg")
    owners_total = lax.axis_size("bundle")
    cap = max(2, 2 * blocks // owners_total)
    rows = lines * comps
    cell_count = grid.shape[1]
    chunk = 4 if owners_total % 4 == 0 else owners_total
    half = cap * comps
    extra = 8 * (-(-cap // 8))

    slot, cell_send = call(
        functools.partial(route_kernel, groups, cap),
        [sds((blocks, LANES), jnp.int32), sds((owners_total, cap, LANES), jnp.int32)],
        [(jnp.swapaxes(owners, 2, 3), VMEM), (cells, VMEM)],
        scratch=[pltpu.SMEM((owners_total,), jnp.int32)],
        flops=1e9,
    )
    cell_recv = exchange(cell_send)

    retain, levels, offset, factor, ends, taps, inlet = call(
        functools.partial(first_kernel, lines, comps, groups),
        [
            sds((rows, nodes)), sds((LEVELS + 2, rows, nodes)), sds((rows, nodes)),
            sds((rows, nodes)), sds((2, comps, LANES)), sds((taps.shape[1], comps, LANES)),
            sds((rows, LANES)),
        ],
        [
            (conc, VMEM), (slowness, VMEM), (retard.reshape(1, comps), VMEM), (taps, VMEM),
            (inlet, VMEM), (slot, ANY),
        ],
        flops=1e8,
    )
    first_ends = ends
    other = swap(ends, segs)
    if segs == 2:
        other_offset = other_factor = other
    else:
        other_offset, other_factor = other[:, 0], other[:, 1]
    local, carried = call(
        functools.partial(taps_kernel, lines, comps, groups, 2),
        [sds((rows, nodes))] * 2,
        [(taps, VMEM), (offset, VMEM), (factor, VMEM)],
        flops=1e8,
    )

    def finish(looked):
        first = looked is None
        ins = [
            (local, VMEM), (carried, VMEM), (ends, VMEM), (first_ends, VMEM),
            (other_offset, VMEM), (other_factor, VMEM), (taps, VMEM), (inlet, VMEM),
        ]
        outs = [sds((rows, nodes))]
        if not first:
            ins += [(slot, VMEM), (looked, VMEM)]
            outs.append(sds((owners_total, 2 * half, LANES)))
        return call(
            functools.partial(finish_kernel, lines, comps, groups, cap, segs, segs != 2, first),
            outs, ins, flops=1e8 if first else 1,
        )

    (spread,) = finish(None)
    rates, send = call(
        functools.partial(look_first_kernel, groups, cap),
        [
            sds((owners_total, cap, LANES)), sds((owners_total, 2 * half + extra, LANES)),
        ],
        [
            (cell_recv, VMEM), (grid, VMEM), (kappa.reshape(cell_count // LANES, LANES), VMEM),
            (spread, VMEM), (slot, VMEM),
        ],
        flops=1e8,
    )
    looked = send
    wide = 256 if cell_count % 256 == 0 else LANES
    coupling = slowness
    for step in range(STEPS):
        last = step == STEPS - 1
        got = exchange(send)
        outs = [sds(conc.shape)] if last else [sds((rows, nodes)), sds((1, comps, LANES))]
        if step == 0:
            outs.append(sds((blocks, LANES)))
        result = call(
            functools.partial(conc_kernel, lines, comps, groups, cap, step == 0, last),
            outs,
            [
                (spread, VMEM), (got, VMEM), (coupling, VMEM), (retain, VMEM), (levels, VMEM),
                (slot, VMEM),
            ],
        )
        if step == 0:
            coupling = result[-1]
        if last:
            conc_out = result[0]
        else:
            offset, ends = result[0], result[1]
            got_ends = swap(ends, segs)
            other_offset = got_ends if segs == 2 else got_ends[:, 0]
        if step == 0:
            (onehot,) = call(
                functools.partial(onehot_kernel, cap),
                [sds((wide, owners_total * cap * LANES), BF16)],
                [(cell_recv, VMEM), (ends, ANY)],
            )
        (grid,) = call(
            functools.partial(update_kernel, cap, chunk),
            [sds(grid.shape)],
            [
                (cell_recv, VMEM), (got, VMEM), (looked, VMEM), (rates, VMEM), (onehot, VMEM),
                (grid, VMEM),
            ],
            scratch=[
                pltpu.VMEM(
                    (
                        min(4, owners_total // chunk),
                        2 * (cell_count // wide) * comps,
                        chunk * cap * LANES,
                    ),
                    BF16,
                )
            ],
        )
        if not last:
            (looked,) = call(
                functools.partial(look_kernel, cap),
                [sds((owners_total, half, LANES))],
                [(cell_recv, VMEM), (onehot, VMEM), (grid, VMEM)],
                scratch=[pltpu.VMEM((2 * (cell_count // wide) * comps, wide), BF16)],
            )
            (local,) = call(
                functools.partial(taps_kernel, lines, comps, groups, 1),
                [sds((rows, nodes))],
                [(taps, VMEM), (offset, VMEM)],
            )
            spread, send = finish(looked)
    return (conc_out, grid)


def solution(mesh):
    return jax.shard_map(
        per_device,
        mesh=mesh,
        in_specs=(
            P("bundle", None, "seg"),
            P("bundle", "seg"),
            P(),
            P(),
            P("bundle", None),
            P(None, ("seg", "bundle")),
            P(("seg", "bundle")),
            P("seg", "bundle", None, None),
            P("bundle", "seg"),
        ),
        out_specs=(P("bundle", None, "seg"), P(None, ("seg", "bundle"))),
        check_vma=False,
    )
```

```python
import functools

import jax
import jax.numpy as jnp
from jax import lax
from jax.experimental import pallas as pl
from jax.experimental.pallas import tpu as pltpu
from jax.sharding import PartitionSpec as P

STEPS = 4
LANES = 128
HALF = 16
RADIX = 4
F32 = jnp.float32
BF16 = jnp.bfloat16

VMEM = pl.BlockSpec(memory_space=pltpu.VMEM)
SMEM = pl.BlockSpec(memory_space=pltpu.SMEM)
ANY = pl.BlockSpec(memory_space=pl.ANY)


def call(kernel, outs, ins, out_specs=None, scratch=(), flops=1, grant=40):
    args = [a for a, _ in ins]
    return pl.pallas_call(
        kernel,
        out_shape=outs,
        in_specs=[s for _, s in ins],
        out_specs=out_specs or [VMEM] * len(outs),
        scratch_shapes=list(scratch),
        cost_estimate=pl.CostEstimate(flops=int(flops), bytes_accessed=1, transcendentals=0),
        compiler_params=pltpu.CompilerParams(vmem_limit_bytes=grant * 1024 * 1024),
    )(*args)


def sds(shape, dtype=F32):
    return jax.ShapeDtypeStruct(shape, dtype)


def slots(owners, count, owners_total, lines, groups):
    for o in range(owners_total):
        count[o] = 0
    out = []
    for line in range(lines):
        for group in range(groups):
            owner = owners[0, line, 0, group]
            rank = count[owner]
            count[owner] = rank + 1
            out.append((owner, rank))
    return out


def route_kernel(groups, owners_in, cells_in, send, owners, cells, count, done):
    copies = [
        pltpu.make_async_copy(owners_in, owners, done.at[0]),
        pltpu.make_async_copy(cells_in, cells, done.at[1]),
    ]
    for copy in copies:
        copy.start()
    send[...] = jnp.full(send.shape, -1, jnp.int32)
    for copy in copies:
        copy.wait()
    for b, (owner, rank) in enumerate(slots(owners, count, send.shape[0], cells.shape[0], groups)):
        line, group = b // groups, b % groups
        send[owner, pl.ds(rank, 1), :] = cells[
            pl.ds(line, 1), group * LANES : (group + 1) * LANES
        ]


def where_slot(slot, b, cap):
    s = slot[b, 0]
    return s // cap, s % cap


def last_lane(x):
    return jnp.broadcast_to(x[:, LANES - 1 : LANES], x.shape)


def column(row, rows):
    square = (rows, rows)
    here = lax.broadcasted_iota(jnp.int32, square, 0) == lax.broadcasted_iota(jnp.int32, square, 1)
    values = jnp.sum(jnp.where(here, jnp.broadcast_to(row, square), 0.0), axis=1, keepdims=True)
    return jnp.broadcast_to(values, (rows, LANES))


def tile(ref, line, comps, group):
    return ref[pl.ds(line * comps, comps), group * LANES : (group + 1) * LANES]


def put(ref, line, comps, group, value):
    ref[pl.ds(line * comps, comps), group * LANES : (group + 1) * LANES] = value


def level_rows(levels, level, line, comps, group):
    return levels[level, pl.ds(line * comps, comps), group * LANES : (group + 1) * LANES]


LEVELS = 7


def scan_lines(levels, retain, values, lines, comps, groups):
    blocks = [(line, group) for line in range(lines) for group in range(groups)]
    offsets = [
        (1.0 - tile(retain, line, comps, group)) * values[line * groups + group]
        for line, group in blocks
    ]
    for level in range(LEVELS):
        offsets = [
            offset
            + level_rows(levels, level, line, comps, group) * pltpu.roll(offset, 1 << level, 1)
            for offset, (line, group) in zip(offsets, blocks)
        ]
    out = []
    for line in range(lines):
        own = offsets[line * groups : (line + 1) * groups]
        carry = last_lane(own[0])
        done = [own[0]]
        for group in range(1, groups):
            done.append(own[group] + level_rows(levels, LEVELS, line, comps, group) * carry)
            if group < groups - 1:
                carry = (
                    last_lane(own[group])
                    + level_rows(levels, LEVELS + 1, line, comps, group) * carry
                )
        out.append(done)
    return out


def tap_columns(wide_taps):
    return [wide_taps[t] for t in range(wide_taps.shape[0])]


def correlate(tiles, columns, lane):
    count = len(tiles)
    shifted = [tiles]
    for b in range(1, RADIX):
        row = []
        for j in range(count):
            x = tiles[j]
            y = jnp.where(lane < b, tiles[j + 1] if j + 1 < count else 0.0, x)
            row.append(pltpu.roll(y, LANES - b, 1))
        shifted.append(row)
    early = [None] + [
        jnp.where(lane >= LANES - b, pltpu.roll(tiles[0], LANES - b, 1), 0.0) for b in range(1, RADIX)
    ]

    def mix(a, values):
        total = None
        for b in range(RADIX):
            t = RADIX * a + b + HALF
            if t < len(columns) and values[b] is not None:
                term = columns[t] * values[b]
                total = term if total is None else total + term
        return total

    spans = range(-(HALF // RADIX), HALF // RADIX + 1)
    outs = [None] * count
    for a in spans:
        parts = [mix(a, [shifted[b][j] for b in range(RADIX)]) for j in range(count)]
        for j in range(count):
            if a == 0:
                y = parts[j]
            elif a > 0:
                after = parts[j + 1] if j + 1 < count else 0.0
                y = pltpu.roll(jnp.where(lane < RADIX * a, after, parts[j]), LANES - RADIX * a, 1)
            else:
                before = parts[j - 1] if j else mix(a, early)
                y = pltpu.roll(
                    jnp.where(lane >= LANES + RADIX * a, before, parts[j]), -RADIX * a, 1
                )
            outs[j] = y if outs[j] is None else outs[j] + y
    return outs


def correlate_ring(x, columns):
    shifted = [x] + [pltpu.roll(x, LANES - b, 1) for b in range(1, RADIX)]
    out = None
    for a in range(-(HALF // RADIX), HALF // RADIX + 1):
        total = None
        for b in range(RADIX):
            t = RADIX * a + b + HALF
            if t < len(columns):
                term = columns[t] * shifted[b]
                total = term if total is None else total + term
        if a:
            total = pltpu.roll(total, (-RADIX * a) % LANES, 1)
        out = total if out is None else out + total
    return out


def pack_ends(line, lane, first, last):
    at = 2 * HALF * line
    both = jnp.where(lane < LANES // 2, first, last)
    both = pltpu.roll(both, (HALF + at) % LANES, 1)
    return both, (lane >= at) & (lane < at + 2 * HALF)


def unpack_ends(line, packed):
    return pltpu.roll(packed, (-(HALF + 2 * HALF * line)) % LANES, 1)


def first_kernel(
    lines, comps, groups, cap, owners_total, conc, slowness, retard, taps, inlet, owners,
    retain, levels, offset, factor, ends, wide_taps, wide_inlet, slot, count,
):
    for b, (owner, rank) in enumerate(slots(owners, count, owners_total, lines, groups)):
        slot[b : b + 1, :] = jnp.full((1, LANES), owner * cap + rank, jnp.int32)
    lane = lax.broadcasted_iota(jnp.int32, (comps, LANES), 1)
    slow_by = column(retard[...], comps)
    packed = [jnp.zeros((comps, LANES), F32)] * 2
    for t in range(taps.shape[1]):
        wide_taps[t] = jnp.broadcast_to(taps[:, t : t + 1], (comps, LANES))
    for line in range(lines):
        wide_inlet[pl.ds(line * comps, comps), :] = column(inlet[line : line + 1, :], comps)
    values, wholes = [], []
    for line in range(lines):
        whole = []
        for group in range(groups):
            s = slowness[pl.ds(line, 1), group * LANES : (group + 1) * LANES]
            r = 1.0 / (1.0 + slow_by * s)
            put(retain, line, comps, group, r)
            rows = pl.ds(line * comps, comps)
            span = slice(group * LANES, (group + 1) * LANES)
            f = r
            for level in range(LEVELS):
                inside = lane >= (1 << level)
                levels[level, rows, span] = jnp.where(inside, f, 0.0)
                f = jnp.where(inside, f * pltpu.roll(f, 1 << level, 1), f)
            levels[LEVELS, rows, span] = f
            end = last_lane(f)
            levels[LEVELS + 1, rows, span] = end
            if group:
                f = f * carry
                carry = carry * end
            else:
                carry = end
            put(factor, line, comps, group, f)
            whole.append(f)
            values.append(conc[line, :, span])
        wholes.append(whole)
    for line, offsets in enumerate(scan_lines(levels, retain, values, lines, comps, groups)):
        whole = wholes[line]
        for group in range(groups):
            put(offset, line, comps, group, offsets[group])
        part, inside = pack_ends(line, lane, offsets[0], offsets[-1])
        packed[0] = jnp.where(inside, part, packed[0])
        part, inside = pack_ends(line, lane, whole[0], whole[-1])
        packed[1] = jnp.where(inside, part, packed[1])
    ends[0] = packed[0]
    ends[1] = packed[1]


def taps_kernel(lines, comps, groups, sources, taps, *refs):
    lane = lax.broadcasted_iota(jnp.int32, (comps, LANES), 1)
    columns = tap_columns(taps)
    for source, out in zip(refs[:sources], refs[sources:]):
        for line in range(lines):
            tiles = [tile(source, line, comps, group) for group in range(groups)]
            sums = correlate(tiles, columns, lane)
            for group in range(groups):
                put(out, line, comps, group, tiles[group] + sums[group])


def place(send, slot, b, cap, comps, value):
    owner, rank = where_slot(slot, b, cap)
    send[owner, pl.ds(pl.multiple_of((cap + rank) * comps, 8), comps), :] = value


def finish_kernel(
    lines, comps, groups, cap, segs, has_gather, first,
    local, carried, end_offset, end_factor, other_offset, other_factor, taps, inlet, *rest,
):
    if first:
        (spread,) = rest
    else:
        slot, looked, spread, send = rest
    me = lax.axis_index("seg")
    lane = lax.broadcasted_iota(jnp.int32, (comps, LANES), 1)
    columns = tap_columns(taps)
    for line in range(lines):
        rows = pl.ds(line * comps, comps)

        def part(s):
            if has_gather:
                pair = other_offset[s], other_factor[s]
            else:
                mine = me == s
                pair = (
                    jnp.where(mine, end_offset[0], other_offset[0]),
                    jnp.where(mine, end_factor[1], other_factor[1]),
                )
            return [unpack_ends(line, x) for x in pair]

        flow = inlet[rows, :]
        zero = jnp.zeros((comps, LANES), F32)
        left, right, inflow = zero, zero, zero
        for s in range(segs):
            inflow = jnp.where(me == s, flow, inflow)
            off, fac = part(s)
            edge = off + fac * flow
            left = jnp.where(me == s + 1, edge, left)
            right = jnp.where(me == s - 1, edge, right)
            if s < segs - 1:
                flow = last_lane(edge)
        ring = jnp.where(lane >= LANES - HALF, left, 0.0)
        ring = jnp.where((lane >= 48) & (lane < 48 + HALF), pltpu.roll(right, 48, 1), ring)
        ring = correlate_ring(ring, columns)
        for group in range(groups):
            total = tile(local, line, comps, group) + tile(carried, line, comps, group) * inflow
            if group == 0:
                total = total + jnp.where(lane < HALF, ring, 0.0)
            if group == groups - 1:
                total = total + jnp.where(lane >= LANES - HALF, pltpu.roll(ring, 80, 1), 0.0)
            put(spread, line, comps, group, total)
    if first:
        return
    send[:, 0 : cap * comps, :] = looked[...]
    for b in range(lines * groups):
        place(send, slot, b, cap, comps, tile(spread, b // groups, comps, b % groups))


def conc_kernel(lines, comps, groups, cap, first, spread, got, coupling, retain, levels, slot, *outs):
    lane = lax.broadcasted_iota(jnp.int32, (comps, LANES), 1)
    values = []
    for b in range(lines * groups):
        line, group = b // groups, b % groups
        owner, rank = where_slot(slot, b, cap)
        looked = got[owner, pl.ds(pl.multiple_of(rank * comps, 8), comps), :]
        if first:
            rate = got[owner, pl.ds(2 * cap * comps + rank, 1), :]
            outs[2][b : b + 1, :] = rate
        else:
            rate = coupling[b : b + 1, :]
        s = tile(spread, line, comps, group)
        values.append(s + rate * (looked - s))
    packed = jnp.zeros((comps, LANES), F32)
    for line, offsets in enumerate(scan_lines(levels, retain, values, lines, comps, groups)):
        for group in range(groups):
            put(outs[0], line, comps, group, offsets[group])
        part, inside = pack_ends(line, lane, offsets[0], offsets[-1])
        packed = jnp.where(inside, part, packed)
    outs[1][0] = packed


def gather_cells(grid, cell, comps, high_total):
    low = jnp.broadcast_to(cell & (LANES - 1), (comps, LANES))
    high = jnp.broadcast_to(cell >> 7, (comps, LANES))
    out = jnp.zeros((comps, LANES), F32)
    for h in range(high_total):
        g = jnp.take_along_axis(
            grid[:, h * LANES : (h + 1) * LANES], low, axis=1, mode="promise_in_bounds"
        )
        out = jnp.where(high == h, g, out)
    return out


def look_by_matmul(cells, cap, onehot, stack, first, count, high_total, wide):
    rows = stack.shape[0] // 2
    comps = rows // high_total
    bits = wide.bit_length() - 1
    part = jnp.dot(
        stack[...], onehot[:, first * LANES : (first + count) * LANES], preferred_element_type=F32
    )
    out = []
    for i in range(count):
        owner, rank = (first + i) // cap, (first + i) % cap
        cell = jnp.maximum(cells[owner, rank : rank + 1, :], 0)
        high = jnp.broadcast_to(cell >> bits, (comps, LANES))
        span = slice(i * LANES, (i + 1) * LANES)
        found = jnp.zeros((comps, LANES), F32)
        for h in range(high_total):
            at = slice(h * comps, (h + 1) * comps)
            at2 = slice(rows + h * comps, rows + (h + 1) * comps)
            found = jnp.where(high == h, part[at, span] + part[at2, span], found)
        out.append(found)
    return out


def in_two(x):
    coarse = x.astype(BF16)
    return coarse, (x - coarse.astype(F32)).astype(BF16)


def stack_grid(grid, stack, wide):
    comps = grid.shape[0]
    rows = stack.shape[0] // 2
    for h in range(grid.shape[1] // wide):
        coarse, fine = in_two(grid[:, h * wide : (h + 1) * wide])
        stack[h * comps : (h + 1) * comps, :] = coarse
        stack[rows + h * comps : rows + (h + 1) * comps, :] = fine


def put_onehot(onehot, at, cell):
    wide = onehot.shape[0]
    row = lax.broadcasted_iota(jnp.int32, (wide, LANES), 0)
    onehot[:, at : at + LANES] = jnp.where(row == (cell & (wide - 1)), 1.0, 0.0).astype(BF16)


def look_first_kernel(groups, cap, cells, grid, kappa, spread, slot, rates, send, onehot, stack):
    comps = grid.shape[0]
    wide = onehot.shape[0]
    high_total = grid.shape[1] // LANES
    by_matmul = onehot.shape[1] // LANES
    row = lax.broadcasted_iota(jnp.int32, (high_total, LANES), 0)
    stack_grid(grid, stack, wide)
    for s in range(by_matmul):
        put_onehot(onehot, s * LANES, cells[s // cap, s % cap : s % cap + 1, :])
    for s in range(cells.shape[0] * cap):
        owner, rank = s // cap, s % cap
        cell = cells[owner, rank : rank + 1, :]
        valid = cell >= 0
        cell = jnp.maximum(cell, 0)
        if s >= by_matmul:
            send[owner, rank * comps : (rank + 1) * comps, :] = gather_cells(
                grid, cell, comps, high_total
            )
        low = jnp.broadcast_to(cell & (LANES - 1), (high_total, LANES))
        k = jnp.take_along_axis(kappa[...], low, axis=1, mode="promise_in_bounds")
        rate = jnp.sum(jnp.where(row == (cell >> 7), k, 0.0), axis=0, keepdims=True)
        rate = jnp.where(valid, rate, 0.0)
        rates[owner, rank : rank + 1, :] = rate
        at = 2 * cap * comps + rank
        send[owner, at : at + 1, :] = rate
    for first in range(0, by_matmul, 4):
        found = look_by_matmul(cells, cap, onehot, stack, first, 4, grid.shape[1] // wide, wide)
        for i in range(4):
            owner, rank = (first + i) // cap, (first + i) % cap
            send[owner, rank * comps : (rank + 1) * comps, :] = found[i]
    for b in range(slot.shape[0]):
        place(send, slot, b, cap, comps, tile(spread, b // groups, comps, b % groups))


def onehot_kernel(cap, cells, order, onehot):
    for owner in range(cells.shape[0]):
        for rank in range(cap):
            put_onehot(onehot, (owner * cap + rank) * LANES, cells[owner, rank : rank + 1, :])


def update_kernel(cap, chunk, cells, got, looked, rates, onehot, grid, grid_out, masked):
    comps = grid.shape[0]
    wide = onehot.shape[0]
    bits = wide.bit_length() - 1
    high_total = grid.shape[1] // wide
    owners_total = cells.shape[0]
    rows = high_total * comps
    width = chunk * cap * LANES
    total = None
    for start in range(0, owners_total, chunk):
        turn = (start // chunk) % masked.shape[0]
        for i in range(chunk):
            owner = start + i
            for rank in range(cap):
                at = (i * cap + rank) * LANES
                cell = cells[owner, rank : rank + 1, :]
                valid = jnp.broadcast_to(cell, (comps, LANES)) >= 0
                cell = jnp.maximum(cell, 0)
                rate = rates[owner, rank : rank + 1, :]
                span = slice(rank * comps, (rank + 1) * comps)
                came = slice((cap + rank) * comps, (cap + rank + 1) * comps)
                flux = jnp.where(valid, rate * (looked[owner, span, :] - got[owner, came, :]), 0.0)
                coarse, fine = in_two(flux)
                high = jnp.broadcast_to((cell >> bits).astype(F32), (comps, LANES)).astype(BF16)
                for h in range(high_total):
                    hit = high == jnp.asarray(h, BF16)
                    masked[turn, h * comps : (h + 1) * comps, at : at + LANES] = jnp.where(
                        hit, coarse, jnp.zeros_like(coarse)
                    )
                    masked[turn, rows + h * comps : rows + (h + 1) * comps, at : at + LANES] = (
                        jnp.where(hit, fine, jnp.zeros_like(fine))
                    )
        first = start * cap * LANES
        part = lax.dot_general(
            masked[turn], onehot[:, first : first + width], (((1,), (1,)), ((), ())),
            preferred_element_type=F32,
        )
        total = part if total is None else total + part
    for h in range(high_total):
        span = slice(h * wide, (h + 1) * wide)
        at = slice(h * comps, (h + 1) * comps)
        at2 = slice(rows + h * comps, rows + (h + 1) * comps)
        grid_out[:, span] = grid[:, span] - 0.25 * (total[at, :] + total[at2, :])


def look_kernel(cap, cells, onehot, grid, looked, stack):
    comps = grid.shape[0]
    wide = onehot.shape[0]
    stack_grid(grid, stack, wide)
    for first in range(0, cells.shape[0] * cap, 4):
        found = look_by_matmul(cells, cap, onehot, stack, first, 4, grid.shape[1] // wide, wide)
        for i in range(4):
            owner, rank = (first + i) // cap, (first + i) % cap
            looked[owner, rank * comps : (rank + 1) * comps, :] = found[i]


def last_kernel(
    lines, comps, groups, cap, chunk,
    spread, came, coupling, slot, cells, looked, rates, onehot, grid,
    conc_out, grid_out, conc, grid_new, masked, done,
):
    for b in range(lines * groups):
        line, group = b // groups, b % groups
        owner, rank = where_slot(slot, b, cap)
        found = came[owner, pl.ds(pl.multiple_of(rank * comps, 8), comps), :]
        s = tile(spread, line, comps, group)
        value = s + coupling[b : b + 1, :] * (found - s)
        conc[line, :, group * LANES : (group + 1) * LANES] = value
    first = pltpu.make_async_copy(conc, conc_out, done.at[0])
    first.start()
    update_kernel(cap, chunk, cells, came, looked, rates, onehot, grid, grid_new, masked)
    second = pltpu.make_async_copy(grid_new, grid_out, done.at[1])
    second.start()
    first.wait()
    second.wait()


def swap(x, segs):
    if segs == 2:
        return lax.ppermute(x, "seg", [(0, 1), (1, 0)])
    return lax.all_gather(x, "seg")


def exchange(x):
    return lax.all_to_all(x, "bundle", split_axis=0, concat_axis=0, tiled=True)


def per_device(conc, slowness, retard, taps, inlet, grid, kappa, owners, cells):
    lines, comps, nodes = conc.shape
    groups = nodes // LANES
    blocks = lines * groups
    segs = lax.axis_size("seg")
    owners_total = lax.axis_size("bundle")
    cap = max(2, 2 * blocks // owners_total)
    rows = lines * comps
    cell_count = grid.shape[1]
    chunk = 4 if owners_total % 4 == 0 else owners_total
    half = cap * comps
    extra = 8 * (-(-cap // 8))
    wide = 256 if cell_count % 256 == 0 else LANES
    matmul_slots = owners_total * cap // 8 * 4

    owners = jnp.swapaxes(owners, 2, 3)
    (cell_send,) = call(
        functools.partial(route_kernel, groups),
        [sds((owners_total, cap, LANES), jnp.int32)],
        [(owners, ANY), (cells, ANY)],
        scratch=[
            pltpu.VMEM((1, lines, 1, groups), jnp.int32), pltpu.VMEM((lines, nodes), jnp.int32),
            pltpu.SMEM((owners_total,), jnp.int32), pltpu.SemaphoreType.DMA((2,)),
        ],
        grant=58,
        flops=1e9,
    )
    cell_recv = exchange(cell_send)

    retain, levels, offset, factor, ends, taps, inlet, slot = call(
        functools.partial(first_kernel, lines, comps, groups, cap, owners_total),
        [
            sds((rows, nodes)), sds((LEVELS + 2, rows, nodes)), sds((rows, nodes)),
            sds((rows, nodes)), sds((2, comps, LANES)), sds((taps.shape[1], comps, LANES)),
            sds((rows, LANES)), sds((blocks, LANES), jnp.int32),
        ],
        [
            (conc, VMEM), (slowness, VMEM), (retard.reshape(1, comps), VMEM), (taps, VMEM),
            (inlet, VMEM), (owners, VMEM),
        ],
        scratch=[pltpu.SMEM((owners_total,), jnp.int32)],
        flops=1e8,
    )
    first_ends = ends
    other = swap(ends, segs)
    if segs == 2:
        other_offset = other_factor = other
    else:
        other_offset, other_factor = other[:, 0], other[:, 1]
    local, carried = call(
        functools.partial(taps_kernel, lines, comps, groups, 2),
        [sds((rows, nodes))] * 2,
        [(taps, VMEM), (offset, VMEM), (factor, VMEM)],
        flops=1e8,
    )

    def finish(looked):
        first = looked is None
        ins = [
            (local, VMEM), (carried, VMEM), (ends, VMEM), (first_ends, VMEM),
            (other_offset, VMEM), (other_factor, VMEM), (taps, VMEM), (inlet, VMEM),
        ]
        outs = [sds((rows, nodes))]
        if not first:
            ins += [(slot, VMEM), (looked, VMEM)]
            outs.append(sds((owners_total, 2 * half, LANES)))
        return call(
            functools.partial(finish_kernel, lines, comps, groups, cap, segs, segs != 2, first),
            outs, ins, flops=1e8 if first else 1,
        )

    (spread,) = finish(None)
    rates, send = call(
        functools.partial(look_first_kernel, groups, cap),
        [
            sds((owners_total, cap, LANES)), sds((owners_total, 2 * half + extra, LANES)),
        ],
        [
            (cell_recv, VMEM), (grid, VMEM), (kappa.reshape(cell_count // LANES, LANES), VMEM),
            (spread, VMEM), (slot, VMEM),
        ],
        scratch=[
            pltpu.VMEM((wide, matmul_slots * LANES), BF16),
            pltpu.VMEM((2 * (cell_count // wide) * comps, wide), BF16),
        ],
        flops=1e8,
    )
    looked = send
    coupling = slowness
    for step in range(STEPS):
        last = step == STEPS - 1
        got = exchange(send)
        masks = pltpu.VMEM(
            (
                min(4, owners_total // chunk), 2 * (cell_count // wide) * comps,
                chunk * cap * LANES,
            ),
            BF16,
        )
        if last:
            conc_out, grid = call(
                functools.partial(last_kernel, lines, comps, groups, cap, chunk),
                [sds(conc.shape), sds(grid.shape)],
                [
                    (spread, VMEM), (got, VMEM), (coupling, VMEM), (slot, VMEM),
                    (cell_recv, VMEM), (looked, VMEM), (rates, VMEM), (onehot, VMEM), (grid, VMEM),
                ],
                out_specs=[ANY, ANY],
                scratch=[
                    pltpu.VMEM(conc.shape, F32), pltpu.VMEM(grid.shape, F32), masks,
                    pltpu.SemaphoreType.DMA((2,)),
                ],
            )
            break
        outs = [sds((rows, nodes)), sds((1, comps, LANES))]
        if step == 0:
            outs.append(sds((blocks, LANES)))
        result = call(
            functools.partial(conc_kernel, lines, comps, groups, cap, step == 0),
            outs,
            [
                (spread, VMEM), (got, VMEM), (coupling, VMEM), (retain, VMEM), (levels, VMEM),
                (slot, VMEM),
            ],
        )
        if step == 0:
            coupling = result[-1]
        offset, ends = result[0], result[1]
        got_ends = swap(ends, segs)
        other_offset = got_ends if segs == 2 else got_ends[:, 0]
        if step == 0:
            (onehot,) = call(
                functools.partial(onehot_kernel, cap),
                [sds((wide, owners_total * cap * LANES), BF16)],
                [(cell_recv, VMEM), (ends, ANY)],
            )
        (grid,) = call(
            functools.partial(update_kernel, cap, chunk),
            [sds(grid.shape)],
            [
                (cell_recv, VMEM), (got, VMEM), (looked, VMEM), (rates, VMEM), (onehot, VMEM),
                (grid, VMEM),
            ],
            scratch=[masks],
        )
        (looked,) = call(
            functools.partial(look_kernel, cap),
            [sds((owners_total, half, LANES))],
            [(cell_recv, VMEM), (onehot, VMEM), (grid, VMEM)],
            scratch=[pltpu.VMEM((2 * (cell_count // wide) * comps, wide), BF16)],
        )
        (local,) = call(
            functools.partial(taps_kernel, lines, comps, groups, 1),
            [sds((rows, nodes))],
            [(taps, VMEM), (offset, VMEM)],
        )
        spread, send = finish(looked)
    return (conc_out, grid)


def solution(mesh):
    return jax.shard_map(
        per_device,
        mesh=mesh,
        in_specs=(
            P("bundle", None, "seg"),
            P("bundle", "seg"),
            P(),
            P(),
            P("bundle", None),
            P(None, ("seg", "bundle")),
            P(("seg", "bundle")),
            P("seg", "bundle", None, None),
            P("bundle", "seg"),
        ),
        out_specs=(P("bundle", None, "seg"), P(None, ("seg", "bundle"))),
        check_vma=False,
    )
```

```python
import functools

import jax
import jax.numpy as jnp
from jax import lax
from jax.experimental import pallas as pl
from jax.experimental.pallas import tpu as pltpu
from jax.sharding import PartitionSpec as P

STEPS = 4
LANES = 128
HALF = 16
RADIX = 4
F32 = jnp.float32
BF16 = jnp.bfloat16

VMEM = pl.BlockSpec(memory_space=pltpu.VMEM)
SMEM = pl.BlockSpec(memory_space=pltpu.SMEM)
ANY = pl.BlockSpec(memory_space=pl.ANY)


def call(kernel, outs, ins, out_specs=None, scratch=(), flops=1, grant=40):
    args = [a for a, _ in ins]
    return pl.pallas_call(
        kernel,
        out_shape=outs,
        in_specs=[s for _, s in ins],
        out_specs=out_specs or [VMEM] * len(outs),
        scratch_shapes=list(scratch),
        cost_estimate=pl.CostEstimate(flops=int(flops), bytes_accessed=1, transcendentals=0),
        compiler_params=pltpu.CompilerParams(vmem_limit_bytes=grant * 1024 * 1024),
    )(*args)


def sds(shape, dtype=F32):
    return jax.ShapeDtypeStruct(shape, dtype)


def slots(owners, count, owners_total, lines, groups):
    for o in range(owners_total):
        count[o] = 0
    out = []
    for line in range(lines):
        for group in range(groups):
            owner = owners[0, line, 0, group]
            rank = count[owner]
            count[owner] = rank + 1
            out.append((owner, rank))
    return out


def route_kernel(groups, owners_in, cells_in, send, owners, cells, count, done):
    copies = [
        pltpu.make_async_copy(owners_in, owners, done.at[0]),
        pltpu.make_async_copy(cells_in, cells, done.at[1]),
    ]
    for copy in copies:
        copy.start()
    send[...] = jnp.full(send.shape, -1, jnp.int32)
    for copy in copies:
        copy.wait()
    for b, (owner, rank) in enumerate(slots(owners, count, send.shape[0], cells.shape[0], groups)):
        line, group = b // groups, b % groups
        send[owner, pl.ds(rank, 1), :] = cells[
            pl.ds(line, 1), group * LANES : (group + 1) * LANES
        ]


def where_slot(slot, b, cap):
    s = slot[b, 0]
    return s // cap, s % cap


def last_lane(x):
    return jnp.broadcast_to(x[:, LANES - 1 : LANES], x.shape)


def column(row, rows):
    square = (rows, rows)
    here = lax.broadcasted_iota(jnp.int32, square, 0) == lax.broadcasted_iota(jnp.int32, square, 1)
    values = jnp.sum(jnp.where(here, jnp.broadcast_to(row, square), 0.0), axis=1, keepdims=True)
    return jnp.broadcast_to(values, (rows, LANES))


def tile(ref, line, comps, group):
    return ref[pl.ds(line * comps, comps), group * LANES : (group + 1) * LANES]


def put(ref, line, comps, group, value):
    ref[pl.ds(line * comps, comps), group * LANES : (group + 1) * LANES] = value


def level_rows(levels, level, line, comps, group):
    return levels[level, pl.ds(line * comps, comps), group * LANES : (group + 1) * LANES]


LEVELS = 7


def scan_lines(levels, retain, values, lines, comps, groups):
    blocks = [(line, group) for line in range(lines) for group in range(groups)]
    offsets = [
        (1.0 - tile(retain, line, comps, group)) * values[line * groups + group]
        for line, group in blocks
    ]
    for level in range(LEVELS):
        offsets = [
            offset
            + level_rows(levels, level, line, comps, group) * pltpu.roll(offset, 1 << level, 1)
            for offset, (line, group) in zip(offsets, blocks)
        ]
    out = []
    for line in range(lines):
        own = offsets[line * groups : (line + 1) * groups]
        carry = last_lane(own[0])
        done = [own[0]]
        for group in range(1, groups):
            done.append(own[group] + level_rows(levels, LEVELS, line, comps, group) * carry)
            if group < groups - 1:
                carry = (
                    last_lane(own[group])
                    + level_rows(levels, LEVELS + 1, line, comps, group) * carry
                )
        out.append(done)
    return out


def tap_columns(wide_taps):
    return [wide_taps[t] for t in range(wide_taps.shape[0])]


def correlate(tiles, columns, lane):
    count = len(tiles)
    shifted = [tiles]
    for b in range(1, RADIX):
        row = []
        for j in range(count):
            x = tiles[j]
            y = jnp.where(lane < b, tiles[j + 1] if j + 1 < count else 0.0, x)
            row.append(pltpu.roll(y, LANES - b, 1))
        shifted.append(row)
    early = [None] + [
        jnp.where(lane >= LANES - b, pltpu.roll(tiles[0], LANES - b, 1), 0.0) for b in range(1, RADIX)
    ]

    def mix(a, values):
        total = None
        for b in range(RADIX):
            t = RADIX * a + b + HALF
            if t < len(columns) and values[b] is not None:
                term = columns[t] * values[b]
                total = term if total is None else total + term
        return total

    spans = range(-(HALF // RADIX), HALF // RADIX + 1)
    outs = [None] * count
    for a in spans:
        parts = [mix(a, [shifted[b][j] for b in range(RADIX)]) for j in range(count)]
        for j in range(count):
            if a == 0:
                y = parts[j]
            elif a > 0:
                after = parts[j + 1] if j + 1 < count else 0.0
                y = pltpu.roll(jnp.where(lane < RADIX * a, after, parts[j]), LANES - RADIX * a, 1)
            else:
                before = parts[j - 1] if j else mix(a, early)
                y = pltpu.roll(
                    jnp.where(lane >= LANES + RADIX * a, before, parts[j]), -RADIX * a, 1
                )
            outs[j] = y if outs[j] is None else outs[j] + y
    return outs


def correlate_ring(x, columns):
    shifted = [x] + [pltpu.roll(x, LANES - b, 1) for b in range(1, RADIX)]
    out = None
    for a in range(-(HALF // RADIX), HALF // RADIX + 1):
        total = None
        for b in range(RADIX):
            t = RADIX * a + b + HALF
            if t < len(columns):
                term = columns[t] * shifted[b]
                total = term if total is None else total + term
        if a:
            total = pltpu.roll(total, (-RADIX * a) % LANES, 1)
        out = total if out is None else out + total
    return out


def pack_ends(line, lane, first, last):
    at = 2 * HALF * line
    both = jnp.where(lane < LANES // 2, first, last)
    both = pltpu.roll(both, (HALF + at) % LANES, 1)
    return both, (lane >= at) & (lane < at + 2 * HALF)


def unpack_ends(line, packed):
    return pltpu.roll(packed, (-(HALF + 2 * HALF * line)) % LANES, 1)


def first_kernel(
    lines, comps, groups, conc, slowness, retard, retain, levels, offset, factor, ends
):
    lane = lax.broadcasted_iota(jnp.int32, (comps, LANES), 1)
    slow_by = column(retard[...], comps)
    packed = [jnp.zeros((comps, LANES), F32)] * 2
    values, wholes = [], []
    for line in range(lines):
        whole = []
        for group in range(groups):
            s = slowness[pl.ds(line, 1), group * LANES : (group + 1) * LANES]
            r = 1.0 / (1.0 + slow_by * s)
            put(retain, line, comps, group, r)
            rows = pl.ds(line * comps, comps)
            span = slice(group * LANES, (group + 1) * LANES)
            f = r
            for level in range(LEVELS):
                inside = lane >= (1 << level)
                levels[level, rows, span] = jnp.where(inside, f, 0.0)
                f = jnp.where(inside, f * pltpu.roll(f, 1 << level, 1), f)
            levels[LEVELS, rows, span] = f
            end = last_lane(f)
            levels[LEVELS + 1, rows, span] = end
            if group:
                f = f * carry
                carry = carry * end
            else:
                carry = end
            put(factor, line, comps, group, f)
            whole.append(f)
            values.append(conc[line, :, span])
        wholes.append(whole)
    for line, offsets in enumerate(scan_lines(levels, retain, values, lines, comps, groups)):
        whole = wholes[line]
        for group in range(groups):
            put(offset, line, comps, group, offsets[group])
        part, inside = pack_ends(line, lane, offsets[0], offsets[-1])
        packed[0] = jnp.where(inside, part, packed[0])
        part, inside = pack_ends(line, lane, whole[0], whole[-1])
        packed[1] = jnp.where(inside, part, packed[1])
    ends[0] = packed[0]
    ends[1] = packed[1]


def taps_kernel(lines, comps, groups, sources, taps, *refs):
    lane = lax.broadcasted_iota(jnp.int32, (comps, LANES), 1)
    columns = tap_columns(taps)
    for source, out in zip(refs[:sources], refs[sources:]):
        for line in range(lines):
            tiles = [tile(source, line, comps, group) for group in range(groups)]
            sums = correlate(tiles, columns, lane)
            for group in range(groups):
                put(out, line, comps, group, tiles[group] + sums[group])


def place(send, slot, b, cap, comps, value):
    owner, rank = where_slot(slot, b, cap)
    send[owner, pl.ds(pl.multiple_of((cap + rank) * comps, 8), comps), :] = value


def first_taps_kernel(
    lines, comps, groups, cap, taps, inlet, owners, offset, factor,
    local, carried, wide_taps, wide_inlet, slot,
):
    for t in range(taps.shape[1]):
        wide_taps[t] = jnp.broadcast_to(taps[:, t : t + 1], (comps, LANES))
    for line in range(lines):
        wide_inlet[pl.ds(line * comps, comps), :] = column(inlet[line : line + 1, :], comps)
    blocks = lines * groups
    square = (blocks, blocks)
    row = jnp.concatenate([owners[0, line].astype(F32) for line in range(lines)], axis=1)
    own = column(row, blocks)[:, :blocks]
    earlier = lax.broadcasted_iota(jnp.int32, square, 1) < lax.broadcasted_iota(jnp.int32, square, 0)
    same = jnp.where(earlier & (own == jnp.broadcast_to(row, square)), 1.0, 0.0)
    at = own[:, :1] * cap + jnp.sum(same, axis=1, keepdims=True)
    slot[...] = jnp.broadcast_to(at, (blocks, LANES)).astype(jnp.int32)
    taps_kernel(lines, comps, groups, 2, wide_taps, offset, factor, local, carried)


def finish_kernel(
    lines, comps, groups, cap, segs, has_gather, first,
    local, carried, end_offset, end_factor, other_offset, other_factor, taps, inlet, *rest,
):
    if first:
        (spread,) = rest
    else:
        slot, looked, spread, send = rest
    me = lax.axis_index("seg")
    lane = lax.broadcasted_iota(jnp.int32, (comps, LANES), 1)
    columns = tap_columns(taps)
    for line in range(lines):
        rows = pl.ds(line * comps, comps)

        def part(s):
            if has_gather:
                pair = other_offset[s], other_factor[s]
            else:
                mine = me == s
                pair = (
                    jnp.where(mine, end_offset[0], other_offset[0]),
                    jnp.where(mine, end_factor[1], other_factor[1]),
                )
            return [unpack_ends(line, x) for x in pair]

        flow = inlet[rows, :]
        zero = jnp.zeros((comps, LANES), F32)
        left, right, inflow = zero, zero, zero
        for s in range(segs):
            inflow = jnp.where(me == s, flow, inflow)
            off, fac = part(s)
            edge = off + fac * flow
            left = jnp.where(me == s + 1, edge, left)
            right = jnp.where(me == s - 1, edge, right)
            if s < segs - 1:
                flow = last_lane(edge)
        ring = jnp.where(lane >= LANES - HALF, left, 0.0)
        ring = jnp.where((lane >= 48) & (lane < 48 + HALF), pltpu.roll(right, 48, 1), ring)
        ring = correlate_ring(ring, columns)
        for group in range(groups):
            total = tile(local, line, comps, group) + tile(carried, line, comps, group) * inflow
            if group == 0:
                total = total + jnp.where(lane < HALF, ring, 0.0)
            if group == groups - 1:
                total = total + jnp.where(lane >= LANES - HALF, pltpu.roll(ring, 80, 1), 0.0)
            put(spread, line, comps, group, total)
    if first:
        return
    send[:, 0 : cap * comps, :] = looked[...]
    for b in range(lines * groups):
        place(send, slot, b, cap, comps, tile(spread, b // groups, comps, b % groups))


def conc_kernel(lines, comps, groups, cap, first, spread, got, coupling, retain, levels, slot, *outs):
    lane = lax.broadcasted_iota(jnp.int32, (comps, LANES), 1)
    values = []
    for b in range(lines * groups):
        line, group = b // groups, b % groups
        owner, rank = where_slot(slot, b, cap)
        looked = got[owner, pl.ds(pl.multiple_of(rank * comps, 8), comps), :]
        if first:
            rate = got[owner, pl.ds(2 * cap * comps + rank, 1), :]
            outs[2][b : b + 1, :] = rate
        else:
            rate = coupling[b : b + 1, :]
        s = tile(spread, line, comps, group)
        values.append(s + rate * (looked - s))
    packed = jnp.zeros((comps, LANES), F32)
    for line, offsets in enumerate(scan_lines(levels, retain, values, lines, comps, groups)):
        for group in range(groups):
            put(outs[0], line, comps, group, offsets[group])
        part, inside = pack_ends(line, lane, offsets[0], offsets[-1])
        packed = jnp.where(inside, part, packed)
    outs[1][0] = packed


def gather_cells(grid, cell, comps, high_total):
    low = jnp.broadcast_to(cell & (LANES - 1), (comps, LANES))
    high = jnp.broadcast_to(cell >> 7, (comps, LANES))
    out = jnp.zeros((comps, LANES), F32)
    for h in range(high_total):
        g = jnp.take_along_axis(
            grid[:, h * LANES : (h + 1) * LANES], low, axis=1, mode="promise_in_bounds"
        )
        out = jnp.where(high == h, g, out)
    return out


def look_by_matmul(cells, cap, onehot, stack, first, count, high_total, wide):
    rows = stack.shape[0] // 2
    comps = rows // high_total
    bits = wide.bit_length() - 1
    part = jnp.dot(
        stack[...], onehot[:, first * LANES : (first + count) * LANES], preferred_element_type=F32
    )
    out = []
    for i in range(count):
        owner, rank = (first + i) // cap, (first + i) % cap
        cell = jnp.maximum(cells[owner, rank : rank + 1, :], 0)
        high = jnp.broadcast_to(cell >> bits, (comps, LANES))
        span = slice(i * LANES, (i + 1) * LANES)
        found = jnp.zeros((comps, LANES), F32)
        for h in range(high_total):
            at = slice(h * comps, (h + 1) * comps)
            at2 = slice(rows + h * comps, rows + (h + 1) * comps)
            found = jnp.where(high == h, part[at, span] + part[at2, span], found)
        out.append(found)
    return out


def in_two(x):
    coarse = x.astype(BF16)
    return coarse, (x - coarse.astype(F32)).astype(BF16)


def stack_grid(grid, stack, wide):
    comps = grid.shape[0]
    rows = stack.shape[0] // 2
    for h in range(grid.shape[1] // wide):
        coarse, fine = in_two(grid[:, h * wide : (h + 1) * wide])
        stack[h * comps : (h + 1) * comps, :] = coarse
        stack[rows + h * comps : rows + (h + 1) * comps, :] = fine


def put_onehot(onehot, at, cell):
    wide = onehot.shape[0]
    row = lax.broadcasted_iota(jnp.int32, (wide, LANES), 0)
    onehot[:, at : at + LANES] = jnp.where(row == (cell & (wide - 1)), 1.0, 0.0).astype(BF16)


def look_first_kernel(groups, cap, cells, grid, kappa, spread, slot, rates, send, onehot, stack):
    comps = grid.shape[0]
    wide = onehot.shape[0]
    high_total = grid.shape[1] // LANES
    by_matmul = onehot.shape[1] // LANES
    row = lax.broadcasted_iota(jnp.int32, (high_total, LANES), 0)
    stack_grid(grid, stack, wide)
    for s in range(by_matmul):
        put_onehot(onehot, s * LANES, cells[s // cap, s % cap : s % cap + 1, :])
    for s in range(cells.shape[0] * cap):
        owner, rank = s // cap, s % cap
        cell = cells[owner, rank : rank + 1, :]
        valid = cell >= 0
        cell = jnp.maximum(cell, 0)
        if s >= by_matmul:
            send[owner, rank * comps : (rank + 1) * comps, :] = gather_cells(
                grid, cell, comps, high_total
            )
        low = jnp.broadcast_to(cell & (LANES - 1), (high_total, LANES))
        k = jnp.take_along_axis(kappa[...], low, axis=1, mode="promise_in_bounds")
        rate = jnp.sum(jnp.where(row == (cell >> 7), k, 0.0), axis=0, keepdims=True)
        rate = jnp.where(valid, rate, 0.0)
        rates[owner, rank : rank + 1, :] = rate
        at = 2 * cap * comps + rank
        send[owner, at : at + 1, :] = rate
    for first in range(0, by_matmul, 4):
        found = look_by_matmul(cells, cap, onehot, stack, first, 4, grid.shape[1] // wide, wide)
        for i in range(4):
            owner, rank = (first + i) // cap, (first + i) % cap
            send[owner, rank * comps : (rank + 1) * comps, :] = found[i]
    for b in range(slot.shape[0]):
        place(send, slot, b, cap, comps, tile(spread, b // groups, comps, b % groups))


def onehot_kernel(cap, cells, order, onehot):
    for owner in range(cells.shape[0]):
        for rank in range(cap):
            put_onehot(onehot, (owner * cap + rank) * LANES, cells[owner, rank : rank + 1, :])


def update_kernel(cap, chunk, cells, got, looked, rates, onehot, grid, grid_out, masked):
    comps = grid.shape[0]
    wide = onehot.shape[0]
    bits = wide.bit_length() - 1
    high_total = grid.shape[1] // wide
    owners_total = cells.shape[0]
    rows = high_total * comps
    width = chunk * cap * LANES
    total = None
    for start in range(0, owners_total, chunk):
        turn = (start // chunk) % masked.shape[0]
        for i in range(chunk):
            owner = start + i
            for rank in range(cap):
                at = (i * cap + rank) * LANES
                cell = cells[owner, rank : rank + 1, :]
                valid = jnp.broadcast_to(cell, (comps, LANES)) >= 0
                cell = jnp.maximum(cell, 0)
                rate = rates[owner, rank : rank + 1, :]
                span = slice(rank * comps, (rank + 1) * comps)
                came = slice((cap + rank) * comps, (cap + rank + 1) * comps)
                flux = jnp.where(valid, rate * (looked[owner, span, :] - got[owner, came, :]), 0.0)
                coarse, fine = in_two(flux)
                high = jnp.broadcast_to((cell >> bits).astype(F32), (comps, LANES)).astype(BF16)
                for h in range(high_total):
                    hit = high == jnp.asarray(h, BF16)
                    masked[turn, h * comps : (h + 1) * comps, at : at + LANES] = jnp.where(
                        hit, coarse, jnp.zeros_like(coarse)
                    )
                    masked[turn, rows + h * comps : rows + (h + 1) * comps, at : at + LANES] = (
                        jnp.where(hit, fine, jnp.zeros_like(fine))
                    )
        first = start * cap * LANES
        part = lax.dot_general(
            masked[turn], onehot[:, first : first + width], (((1,), (1,)), ((), ())),
            preferred_element_type=F32,
        )
        total = part if total is None else total + part
    for h in range(high_total):
        span = slice(h * wide, (h + 1) * wide)
        at = slice(h * comps, (h + 1) * comps)
        at2 = slice(rows + h * comps, rows + (h + 1) * comps)
        grid_out[:, span] = grid[:, span] - 0.25 * (total[at, :] + total[at2, :])


def look_kernel(cap, cells, onehot, grid, looked, stack):
    comps = grid.shape[0]
    wide = onehot.shape[0]
    stack_grid(grid, stack, wide)
    for first in range(0, cells.shape[0] * cap, 4):
        found = look_by_matmul(cells, cap, onehot, stack, first, 4, grid.shape[1] // wide, wide)
        for i in range(4):
            owner, rank = (first + i) // cap, (first + i) % cap
            looked[owner, rank * comps : (rank + 1) * comps, :] = found[i]


def last_kernel(
    lines, comps, groups, cap, chunk,
    spread, came, coupling, slot, cells, looked, rates, onehot, grid,
    conc_out, grid_out, conc, grid_new, masked, done,
):
    for b in range(lines * groups):
        line, group = b // groups, b % groups
        owner, rank = where_slot(slot, b, cap)
        found = came[owner, pl.ds(pl.multiple_of(rank * comps, 8), comps), :]
        s = tile(spread, line, comps, group)
        value = s + coupling[b : b + 1, :] * (found - s)
        conc[line, :, group * LANES : (group + 1) * LANES] = value
    first = pltpu.make_async_copy(conc, conc_out, done.at[0])
    first.start()
    update_kernel(cap, chunk, cells, came, looked, rates, onehot, grid, grid_new, masked)
    second = pltpu.make_async_copy(grid_new, grid_out, done.at[1])
    second.start()
    first.wait()
    second.wait()


def swap(x, segs):
    if segs == 2:
        return lax.ppermute(x, "seg", [(0, 1), (1, 0)])
    return lax.all_gather(x, "seg")


def exchange(x):
    return lax.all_to_all(x, "bundle", split_axis=0, concat_axis=0, tiled=True)


def per_device(conc, slowness, retard, taps, inlet, grid, kappa, owners, cells):
    lines, comps, nodes = conc.shape
    groups = nodes // LANES
    blocks = lines * groups
    segs = lax.axis_size("seg")
    owners_total = lax.axis_size("bundle")
    cap = max(2, 2 * blocks // owners_total)
    rows = lines * comps
    cell_count = grid.shape[1]
    chunk = 4 if owners_total % 4 == 0 else owners_total
    half = cap * comps
    extra = 8 * (-(-cap // 8))
    wide = 256 if cell_count % 256 == 0 else LANES
    matmul_slots = owners_total * cap // 8 * 4

    owners = jnp.swapaxes(owners, 2, 3)
    (cell_send,) = call(
        functools.partial(route_kernel, groups),
        [sds((owners_total, cap, LANES), jnp.int32)],
        [(owners, ANY), (cells, ANY)],
        scratch=[
            pltpu.VMEM((1, lines, 1, groups), jnp.int32), pltpu.VMEM((lines, nodes), jnp.int32),
            pltpu.SMEM((owners_total,), jnp.int32), pltpu.SemaphoreType.DMA((2,)),
        ],
        grant=58,
        flops=1e9,
    )
    cell_recv = exchange(cell_send)

    retain, levels, offset, factor, ends = call(
        functools.partial(first_kernel, lines, comps, groups),
        [
            sds((rows, nodes)), sds((LEVELS + 2, rows, nodes)), sds((rows, nodes)),
            sds((rows, nodes)), sds((2, comps, LANES)),
        ],
        [(conc, VMEM), (slowness, VMEM), (retard.reshape(1, comps), VMEM)],
        flops=1e8,
    )
    first_ends = ends
    other = swap(ends, segs)
    if segs == 2:
        other_offset = other_factor = other
    else:
        other_offset, other_factor = other[:, 0], other[:, 1]
    local, carried, taps, inlet, slot = call(
        functools.partial(first_taps_kernel, lines, comps, groups, cap),
        [
            sds((rows, nodes)), sds((rows, nodes)), sds((taps.shape[1], comps, LANES)),
            sds((rows, LANES)), sds((blocks, LANES), jnp.int32),
        ],
        [(taps, VMEM), (inlet, VMEM), (owners, VMEM), (offset, VMEM), (factor, VMEM)],
        flops=1e8,
    )

    def finish(looked):
        first = looked is None
        ins = [
            (local, VMEM), (carried, VMEM), (ends, VMEM), (first_ends, VMEM),
            (other_offset, VMEM), (other_factor, VMEM), (taps, VMEM), (inlet, VMEM),
        ]
        outs = [sds((rows, nodes))]
        if not first:
            ins += [(slot, VMEM), (looked, VMEM)]
            outs.append(sds((owners_total, 2 * half, LANES)))
        return call(
            functools.partial(finish_kernel, lines, comps, groups, cap, segs, segs != 2, first),
            outs, ins, flops=1e8 if first else 1,
        )

    (spread,) = finish(None)
    rates, send = call(
        functools.partial(look_first_kernel, groups, cap),
        [
            sds((owners_total, cap, LANES)), sds((owners_total, 2 * half + extra, LANES)),
        ],
        [
            (cell_recv, VMEM), (grid, VMEM), (kappa.reshape(cell_count // LANES, LANES), VMEM),
            (spread, VMEM), (slot, VMEM),
        ],
        scratch=[
            pltpu.VMEM((wide, matmul_slots * LANES), BF16),
            pltpu.VMEM((2 * (cell_count // wide) * comps, wide), BF16),
        ],
        flops=1e8,
    )
    looked = send
    coupling = slowness
    for step in range(STEPS):
        last = step == STEPS - 1
        got = exchange(send)
        masks = pltpu.VMEM(
            (
                min(4, owners_total // chunk), 2 * (cell_count // wide) * comps,
                chunk * cap * LANES,
            ),
            BF16,
        )
        if last:
            conc_out, grid = call(
                functools.partial(last_kernel, lines, comps, groups, cap, chunk),
                [sds(conc.shape), sds(grid.shape)],
                [
                    (spread, VMEM), (got, VMEM), (coupling, VMEM), (slot, VMEM),
                    (cell_recv, VMEM), (looked, VMEM), (rates, VMEM), (onehot, VMEM), (grid, VMEM),
                ],
                out_specs=[ANY, ANY],
                scratch=[
                    pltpu.VMEM(conc.shape, F32), pltpu.VMEM(grid.shape, F32), masks,
                    pltpu.SemaphoreType.DMA((2,)),
                ],
            )
            break
        outs = [sds((rows, nodes)), sds((1, comps, LANES))]
        if step == 0:
            outs.append(sds((blocks, LANES)))
        result = call(
            functools.partial(conc_kernel, lines, comps, groups, cap, step == 0),
            outs,
            [
                (spread, VMEM), (got, VMEM), (coupling, VMEM), (retain, VMEM), (levels, VMEM),
                (slot, VMEM),
            ],
        )
        if step == 0:
            coupling = result[-1]
        offset, ends = result[0], result[1]
        got_ends = swap(ends, segs)
        other_offset = got_ends if segs == 2 else got_ends[:, 0]
        if step == 0:
            (onehot,) = call(
                functools.partial(onehot_kernel, cap),
                [sds((wide, owners_total * cap * LANES), BF16)],
                [(cell_recv, VMEM), (ends, ANY)],
            )
        (grid,) = call(
            functools.partial(update_kernel, cap, chunk),
            [sds(grid.shape)],
            [
                (cell_recv, VMEM), (got, VMEM), (looked, VMEM), (rates, VMEM), (onehot, VMEM),
                (grid, VMEM),
            ],
            scratch=[masks],
        )
        (looked,) = call(
            functools.partial(look_kernel, cap),
            [sds((owners_total, half, LANES))],
            [(cell_recv, VMEM), (onehot, VMEM), (grid, VMEM)],
            scratch=[pltpu.VMEM((2 * (cell_count // wide) * comps, wide), BF16)],
        )
        (local,) = call(
            functools.partial(taps_kernel, lines, comps, groups, 1),
            [sds((rows, nodes))],
            [(taps, VMEM), (offset, VMEM)],
        )
        spread, send = finish(looked)
    return (conc_out, grid)


def solution(mesh):
    return jax.shard_map(
        per_device,
        mesh=mesh,
        in_specs=(
            P("bundle", None, "seg"),
            P("bundle", "seg"),
            P(),
            P(),
            P("bundle", None),
            P(None, ("seg", "bundle")),
            P(("seg", "bundle")),
            P("seg", "bundle", None, None),
            P("bundle", "seg"),
        ),
        out_specs=(P("bundle", None, "seg"), P(None, ("seg", "bundle"))),
        check_vma=False,
    )
```

```python
import functools

import jax
import jax.numpy as jnp
from jax import lax
from jax.experimental import pallas as pl
from jax.experimental.pallas import tpu as pltpu
from jax.sharding import PartitionSpec as P

STEPS = 4
LANES = 128
HALF = 16
RADIX = 4
F32 = jnp.float32
BF16 = jnp.bfloat16

VMEM = pl.BlockSpec(memory_space=pltpu.VMEM)
SMEM = pl.BlockSpec(memory_space=pltpu.SMEM)
ANY = pl.BlockSpec(memory_space=pl.ANY)


def call(kernel, outs, ins, out_specs=None, scratch=(), flops=1, grant=40):
    args = [a for a, _ in ins]
    return pl.pallas_call(
        kernel,
        out_shape=outs,
        in_specs=[s for _, s in ins],
        out_specs=out_specs or [VMEM] * len(outs),
        scratch_shapes=list(scratch),
        cost_estimate=pl.CostEstimate(flops=int(flops), bytes_accessed=1, transcendentals=0),
        compiler_params=pltpu.CompilerParams(vmem_limit_bytes=grant * 1024 * 1024),
    )(*args)


def sds(shape, dtype=F32):
    return jax.ShapeDtypeStruct(shape, dtype)


def slots(owners, count, owners_total, lines, groups):
    for o in range(owners_total):
        count[o] = 0
    out = []
    for line in range(lines):
        for group in range(groups):
            owner = owners[0, line, 0, group]
            rank = count[owner]
            count[owner] = rank + 1
            out.append((owner, rank))
    return out


def route_kernel(groups, owners_in, cells_in, send, owners, cells, count, done):
    copies = [
        pltpu.make_async_copy(owners_in, owners, done.at[0]),
        pltpu.make_async_copy(cells_in, cells, done.at[1]),
    ]
    for copy in copies:
        copy.start()
    send[...] = jnp.full(send.shape, -1, jnp.int32)
    for copy in copies:
        copy.wait()
    for b, (owner, rank) in enumerate(slots(owners, count, send.shape[0], cells.shape[0], groups)):
        line, group = b // groups, b % groups
        send[owner, pl.ds(rank, 1), :] = cells[
            pl.ds(line, 1), group * LANES : (group + 1) * LANES
        ]


def where_slot(slot, b, cap):
    s = slot[b, 0]
    return s // cap, s % cap


def last_lane(x):
    return jnp.broadcast_to(x[:, LANES - 1 : LANES], x.shape)


def column(row, rows):
    square = (rows, rows)
    here = lax.broadcasted_iota(jnp.int32, square, 0) == lax.broadcasted_iota(jnp.int32, square, 1)
    values = jnp.sum(jnp.where(here, jnp.broadcast_to(row, square), 0.0), axis=1, keepdims=True)
    return jnp.broadcast_to(values, (rows, LANES))


def tile(ref, line, comps, group):
    return ref[pl.ds(line * comps, comps), group * LANES : (group + 1) * LANES]


def put(ref, line, comps, group, value):
    ref[pl.ds(line * comps, comps), group * LANES : (group + 1) * LANES] = value


def level_rows(levels, level, line, comps, group):
    return levels[level, pl.ds(line * comps, comps), group * LANES : (group + 1) * LANES]


LEVELS = 7


def scan_lines(levels, retain, values, lines, comps, groups):
    blocks = [(line, group) for line in range(lines) for group in range(groups)]
    offsets = [
        (1.0 - tile(retain, line, comps, group)) * values[line * groups + group]
        for line, group in blocks
    ]
    for level in range(LEVELS):
        offsets = [
            offset
            + level_rows(levels, level, line, comps, group) * pltpu.roll(offset, 1 << level, 1)
            for offset, (line, group) in zip(offsets, blocks)
        ]
    out = []
    for line in range(lines):
        own = offsets[line * groups : (line + 1) * groups]
        carry = last_lane(own[0])
        done = [own[0]]
        for group in range(1, groups):
            done.append(own[group] + level_rows(levels, LEVELS, line, comps, group) * carry)
            if group < groups - 1:
                carry = (
                    last_lane(own[group])
                    + level_rows(levels, LEVELS + 1, line, comps, group) * carry
                )
        out.append(done)
    return out


def tap_columns(wide_taps):
    return [wide_taps[t] for t in range(wide_taps.shape[0])]


def correlate(tiles, columns, lane):
    count = len(tiles)
    shifted = [tiles]
    for b in range(1, RADIX):
        row = []
        for j in range(count):
            x = tiles[j]
            y = jnp.where(lane < b, tiles[j + 1] if j + 1 < count else 0.0, x)
            row.append(pltpu.roll(y, LANES - b, 1))
        shifted.append(row)
    early = [None] + [
        jnp.where(lane >= LANES - b, pltpu.roll(tiles[0], LANES - b, 1), 0.0) for b in range(1, RADIX)
    ]

    def mix(a, values):
        total = None
        for b in range(RADIX):
            t = RADIX * a + b + HALF
            if t < len(columns) and values[b] is not None:
                term = columns[t] * values[b]
                total = term if total is None else total + term
        return total

    spans = range(-(HALF // RADIX), HALF // RADIX + 1)
    outs = [None] * count
    for a in spans:
        parts = [mix(a, [shifted[b][j] for b in range(RADIX)]) for j in range(count)]
        for j in range(count):
            if a == 0:
                y = parts[j]
            elif a > 0:
                after = parts[j + 1] if j + 1 < count else 0.0
                y = pltpu.roll(jnp.where(lane < RADIX * a, after, parts[j]), LANES - RADIX * a, 1)
            else:
                before = parts[j - 1] if j else mix(a, early)
                y = pltpu.roll(
                    jnp.where(lane >= LANES + RADIX * a, before, parts[j]), -RADIX * a, 1
                )
            outs[j] = y if outs[j] is None else outs[j] + y
    return outs


def correlate_ring(x, columns):
    shifted = [x] + [pltpu.roll(x, LANES - b, 1) for b in range(1, RADIX)]
    out = None
    for a in range(-(HALF // RADIX), HALF // RADIX + 1):
        total = None
        for b in range(RADIX):
            t = RADIX * a + b + HALF
            if t < len(columns):
                term = columns[t] * shifted[b]
                total = term if total is None else total + term
        if a:
            total = pltpu.roll(total, (-RADIX * a) % LANES, 1)
        out = total if out is None else out + total
    return out


def pack_ends(line, lane, first, last):
    at = 2 * HALF * line
    both = jnp.where(lane < LANES // 2, first, last)
    both = pltpu.roll(both, (HALF + at) % LANES, 1)
    return both, (lane >= at) & (lane < at + 2 * HALF)


def unpack_ends(line, packed):
    return pltpu.roll(packed, (-(HALF + 2 * HALF * line)) % LANES, 1)


def first_kernel(
    lines, comps, groups, conc, slowness, retard, retain, levels, offset, factor, ends
):
    lane = lax.broadcasted_iota(jnp.int32, (comps, LANES), 1)
    slow_by = column(retard[...], comps)
    packed = [jnp.zeros((comps, LANES), F32)] * 2
    values, wholes = [], []
    for line in range(lines):
        whole = []
        for group in range(groups):
            s = slowness[pl.ds(line, 1), group * LANES : (group + 1) * LANES]
            r = 1.0 / (1.0 + slow_by * s)
            put(retain, line, comps, group, r)
            rows = pl.ds(line * comps, comps)
            span = slice(group * LANES, (group + 1) * LANES)
            f = r
            for level in range(LEVELS):
                inside = lane >= (1 << level)
                levels[level, rows, span] = jnp.where(inside, f, 0.0)
                f = jnp.where(inside, f * pltpu.roll(f, 1 << level, 1), f)
            levels[LEVELS, rows, span] = f
            end = last_lane(f)
            levels[LEVELS + 1, rows, span] = end
            if group:
                f = f * carry
                carry = carry * end
            else:
                carry = end
            put(factor, line, comps, group, f)
            whole.append(f)
            values.append(conc[line, :, span])
        wholes.append(whole)
    for line, offsets in enumerate(scan_lines(levels, retain, values, lines, comps, groups)):
        whole = wholes[line]
        for group in range(groups):
            put(offset, line, comps, group, offsets[group])
        part, inside = pack_ends(line, lane, offsets[0], offsets[-1])
        packed[0] = jnp.where(inside, part, packed[0])
        part, inside = pack_ends(line, lane, whole[0], whole[-1])
        packed[1] = jnp.where(inside, part, packed[1])
    ends[0] = packed[0]
    ends[1] = packed[1]


def taps_kernel(lines, comps, groups, sources, taps, *refs):
    lane = lax.broadcasted_iota(jnp.int32, (comps, LANES), 1)
    columns = tap_columns(taps)
    for source, out in zip(refs[:sources], refs[sources:]):
        for line in range(lines):
            tiles = [tile(source, line, comps, group) for group in range(groups)]
            sums = correlate(tiles, columns, lane)
            for group in range(groups):
                put(out, line, comps, group, tiles[group] + sums[group])


def place(send, slot, b, cap, comps, value):
    owner, rank = where_slot(slot, b, cap)
    send[owner, pl.ds(pl.multiple_of((cap + rank) * comps, 8), comps), :] = value


def first_taps_kernel(
    lines, comps, groups, cap, taps, inlet, owners, offset, factor,
    local, carried, wide_taps, wide_inlet, slot,
):
    for t in range(taps.shape[1]):
        wide_taps[t] = jnp.broadcast_to(taps[:, t : t + 1], (comps, LANES))
    for line in range(lines):
        wide_inlet[pl.ds(line * comps, comps), :] = column(inlet[line : line + 1, :], comps)
    blocks = lines * groups
    square = (blocks, blocks)
    row = jnp.concatenate([owners[0, line].astype(F32) for line in range(lines)], axis=1)
    own = column(row, blocks)[:, :blocks]
    earlier = lax.broadcasted_iota(jnp.int32, square, 1) < lax.broadcasted_iota(jnp.int32, square, 0)
    same = jnp.where(earlier & (own == jnp.broadcast_to(row, square)), 1.0, 0.0)
    at = own[:, :1] * cap + jnp.sum(same, axis=1, keepdims=True)
    slot[...] = jnp.broadcast_to(at, (blocks, LANES)).astype(jnp.int32)
    taps_kernel(lines, comps, groups, 2, wide_taps, offset, factor, local, carried)


def finish_kernel(
    lines, comps, groups, cap, segs, has_gather, first,
    local, carried, end_offset, end_factor, other_offset, other_factor, taps, inlet, *rest,
):
    if first:
        (spread,) = rest
    else:
        slot, looked, spread, send = rest
    me = lax.axis_index("seg")
    lane = lax.broadcasted_iota(jnp.int32, (comps, LANES), 1)
    columns = tap_columns(taps)
    for line in range(lines):
        rows = pl.ds(line * comps, comps)

        def part(s):
            if has_gather:
                pair = other_offset[s], other_factor[s]
            else:
                mine = me == s
                pair = (
                    jnp.where(mine, end_offset[0], other_offset[0]),
                    jnp.where(mine, end_factor[1], other_factor[1]),
                )
            return [unpack_ends(line, x) for x in pair]

        flow = inlet[rows, :]
        zero = jnp.zeros((comps, LANES), F32)
        left, right, inflow = zero, zero, zero
        for s in range(segs):
            inflow = jnp.where(me == s, flow, inflow)
            off, fac = part(s)
            edge = off + fac * flow
            left = jnp.where(me == s + 1, edge, left)
            right = jnp.where(me == s - 1, edge, right)
            if s < segs - 1:
                flow = last_lane(edge)
        ring = jnp.where(lane >= LANES - HALF, left, 0.0)
        ring = jnp.where((lane >= 48) & (lane < 48 + HALF), pltpu.roll(right, 48, 1), ring)
        ring = correlate_ring(ring, columns)
        for group in range(groups):
            total = tile(local, line, comps, group) + tile(carried, line, comps, group) * inflow
            if group == 0:
                total = total + jnp.where(lane < HALF, ring, 0.0)
            if group == groups - 1:
                total = total + jnp.where(lane >= LANES - HALF, pltpu.roll(ring, 80, 1), 0.0)
            put(spread, line, comps, group, total)
    if first:
        return
    send[:, 0 : cap * comps, :] = looked[...]
    for b in range(lines * groups):
        place(send, slot, b, cap, comps, tile(spread, b // groups, comps, b % groups))


def conc_kernel(lines, comps, groups, cap, first, spread, got, coupling, retain, levels, slot, *outs):
    lane = lax.broadcasted_iota(jnp.int32, (comps, LANES), 1)
    values = []
    for b in range(lines * groups):
        line, group = b // groups, b % groups
        owner, rank = where_slot(slot, b, cap)
        looked = got[owner, pl.ds(pl.multiple_of(rank * comps, 8), comps), :]
        if first:
            rate = got[owner, pl.ds(2 * cap * comps + rank, 1), :]
            outs[2][b : b + 1, :] = rate
        else:
            rate = coupling[b : b + 1, :]
        s = tile(spread, line, comps, group)
        values.append(s + rate * (looked - s))
    packed = jnp.zeros((comps, LANES), F32)
    for line, offsets in enumerate(scan_lines(levels, retain, values, lines, comps, groups)):
        for group in range(groups):
            put(outs[0], line, comps, group, offsets[group])
        part, inside = pack_ends(line, lane, offsets[0], offsets[-1])
        packed = jnp.where(inside, part, packed)
    outs[1][0] = packed


def look_by_matmul(cells, cap, onehot, stack, first, count, high_total, wide):
    rows = stack.shape[0] // 2
    comps = rows // high_total
    bits = wide.bit_length() - 1
    part = jnp.dot(
        stack[...], onehot[:, first * LANES : (first + count) * LANES], preferred_element_type=F32
    )
    out = []
    for i in range(count):
        owner, rank = (first + i) // cap, (first + i) % cap
        cell = jnp.maximum(cells[owner, rank : rank + 1, :], 0)
        high = jnp.broadcast_to(cell >> bits, (comps, LANES))
        span = slice(i * LANES, (i + 1) * LANES)
        found = jnp.zeros((comps, LANES), F32)
        for h in range(high_total):
            at = slice(h * comps, (h + 1) * comps)
            at2 = slice(rows + h * comps, rows + (h + 1) * comps)
            found = jnp.where(high == h, part[at, span] + part[at2, span], found)
        out.append(found)
    return out


def in_two(x):
    coarse = x.astype(BF16)
    return coarse, (x - coarse.astype(F32)).astype(BF16)


def stack_grid(grid, stack, wide):
    comps = grid.shape[0]
    rows = stack.shape[0] // 2
    for h in range(grid.shape[1] // wide):
        coarse, fine = in_two(grid[:, h * wide : (h + 1) * wide])
        stack[h * comps : (h + 1) * comps, :] = coarse
        stack[rows + h * comps : rows + (h + 1) * comps, :] = fine


def put_onehot(onehot, at, cell):
    wide = onehot.shape[0]
    row = lax.broadcasted_iota(jnp.int32, (wide, LANES), 0)
    onehot[:, at : at + LANES] = jnp.where(row == (cell & (wide - 1)), 1.0, 0.0).astype(BF16)


def look_first_kernel(groups, cap, cells, grid, kappa, spread, slot, rates, send, onehot, stack):
    comps = grid.shape[0]
    wide = onehot.shape[0]
    high_total = grid.shape[1] // LANES
    slots_total = cells.shape[0] * cap
    row = lax.broadcasted_iota(jnp.int32, (high_total, LANES), 0)
    stack_grid(grid, stack, wide)
    for s in range(slots_total):
        put_onehot(onehot, s * LANES, cells[s // cap, s % cap : s % cap + 1, :])
    for s in range(slots_total):
        owner, rank = s // cap, s % cap
        cell = cells[owner, rank : rank + 1, :]
        valid = cell >= 0
        cell = jnp.maximum(cell, 0)
        low = jnp.broadcast_to(cell & (LANES - 1), (high_total, LANES))
        k = jnp.take_along_axis(kappa[...], low, axis=1, mode="promise_in_bounds")
        rate = jnp.sum(jnp.where(row == (cell >> 7), k, 0.0), axis=0, keepdims=True)
        rate = jnp.where(valid, rate, 0.0)
        rates[owner, rank : rank + 1, :] = rate
        at = 2 * cap * comps + rank
        send[owner, at : at + 1, :] = rate
    for first in range(0, slots_total, 4):
        found = look_by_matmul(cells, cap, onehot, stack, first, 4, grid.shape[1] // wide, wide)
        for i in range(4):
            owner, rank = (first + i) // cap, (first + i) % cap
            send[owner, rank * comps : (rank + 1) * comps, :] = found[i]
    for b in range(slot.shape[0]):
        place(send, slot, b, cap, comps, tile(spread, b // groups, comps, b % groups))


def update_kernel(cap, chunk, cells, got, looked, rates, onehot, grid, grid_out, masked):
    comps = grid.shape[0]
    wide = onehot.shape[0]
    bits = wide.bit_length() - 1
    high_total = grid.shape[1] // wide
    owners_total = cells.shape[0]
    rows = high_total * comps
    width = chunk * cap * LANES
    total = None
    for start in range(0, owners_total, chunk):
        turn = (start // chunk) % masked.shape[0]
        for i in range(chunk):
            owner = start + i
            for rank in range(cap):
                at = (i * cap + rank) * LANES
                cell = cells[owner, rank : rank + 1, :]
                valid = jnp.broadcast_to(cell, (comps, LANES)) >= 0
                cell = jnp.maximum(cell, 0)
                rate = rates[owner, rank : rank + 1, :]
                span = slice(rank * comps, (rank + 1) * comps)
                came = slice((cap + rank) * comps, (cap + rank + 1) * comps)
                flux = jnp.where(valid, rate * (looked[owner, span, :] - got[owner, came, :]), 0.0)
                coarse, fine = in_two(flux)
                high = jnp.broadcast_to((cell >> bits).astype(F32), (comps, LANES)).astype(BF16)
                for h in range(high_total):
                    hit = high == jnp.asarray(h, BF16)
                    masked[turn, h * comps : (h + 1) * comps, at : at + LANES] = jnp.where(
                        hit, coarse, jnp.zeros_like(coarse)
                    )
                    masked[turn, rows + h * comps : rows + (h + 1) * comps, at : at + LANES] = (
                        jnp.where(hit, fine, jnp.zeros_like(fine))
                    )
        first = start * cap * LANES
        part = lax.dot_general(
            masked[turn], onehot[:, first : first + width], (((1,), (1,)), ((), ())),
            preferred_element_type=F32,
        )
        total = part if total is None else total + part
    for h in range(high_total):
        span = slice(h * wide, (h + 1) * wide)
        at = slice(h * comps, (h + 1) * comps)
        at2 = slice(rows + h * comps, rows + (h + 1) * comps)
        grid_out[:, span] = grid[:, span] - 0.25 * (total[at, :] + total[at2, :])


def look_kernel(cap, cells, onehot, grid, looked, stack):
    comps = grid.shape[0]
    wide = onehot.shape[0]
    stack_grid(grid, stack, wide)
    for first in range(0, cells.shape[0] * cap, 4):
        found = look_by_matmul(cells, cap, onehot, stack, first, 4, grid.shape[1] // wide, wide)
        for i in range(4):
            owner, rank = (first + i) // cap, (first + i) % cap
            looked[owner, rank * comps : (rank + 1) * comps, :] = found[i]


def last_kernel(
    lines, comps, groups, cap, chunk,
    spread, came, coupling, slot, cells, looked, rates, onehot, grid,
    conc_out, grid_out, conc, grid_new, masked, done,
):
    for b in range(lines * groups):
        line, group = b // groups, b % groups
        owner, rank = where_slot(slot, b, cap)
        found = came[owner, pl.ds(pl.multiple_of(rank * comps, 8), comps), :]
        s = tile(spread, line, comps, group)
        value = s + coupling[b : b + 1, :] * (found - s)
        conc[line, :, group * LANES : (group + 1) * LANES] = value
    first = pltpu.make_async_copy(conc, conc_out, done.at[0])
    first.start()
    update_kernel(cap, chunk, cells, came, looked, rates, onehot, grid, grid_new, masked)
    second = pltpu.make_async_copy(grid_new, grid_out, done.at[1])
    second.start()
    first.wait()
    second.wait()


def swap(x, segs):
    if segs == 2:
        return lax.ppermute(x, "seg", [(0, 1), (1, 0)])
    return lax.all_gather(x, "seg")


def exchange(x):
    return lax.all_to_all(x, "bundle", split_axis=0, concat_axis=0, tiled=True)


def per_device(conc, slowness, retard, taps, inlet, grid, kappa, owners, cells):
    lines, comps, nodes = conc.shape
    groups = nodes // LANES
    blocks = lines * groups
    segs = lax.axis_size("seg")
    owners_total = lax.axis_size("bundle")
    cap = max(2, 2 * blocks // owners_total)
    rows = lines * comps
    cell_count = grid.shape[1]
    chunk = 4 if owners_total % 4 == 0 else owners_total
    half = cap * comps
    extra = 8 * (-(-cap // 8))
    wide = 256 if cell_count % 256 == 0 else LANES

    owners = jnp.swapaxes(owners, 2, 3)
    (cell_send,) = call(
        functools.partial(route_kernel, groups),
        [sds((owners_total, cap, LANES), jnp.int32)],
        [(owners, ANY), (cells, ANY)],
        scratch=[
            pltpu.VMEM((1, lines, 1, groups), jnp.int32), pltpu.VMEM((lines, nodes), jnp.int32),
            pltpu.SMEM((owners_total,), jnp.int32), pltpu.SemaphoreType.DMA((2,)),
        ],
        grant=58,
        flops=1e9,
    )
    cell_recv = exchange(cell_send)

    retain, levels, offset, factor, ends = call(
        functools.partial(first_kernel, lines, comps, groups),
        [
            sds((rows, nodes)), sds((LEVELS + 2, rows, nodes)), sds((rows, nodes)),
            sds((rows, nodes)), sds((2, comps, LANES)),
        ],
        [(conc, VMEM), (slowness, VMEM), (retard.reshape(1, comps), VMEM)],
        flops=1e8,
    )
    first_ends = ends
    other = swap(ends, segs)
    if segs == 2:
        other_offset = other_factor = other
    else:
        other_offset, other_factor = other[:, 0], other[:, 1]
    local, carried, taps, inlet, slot = call(
        functools.partial(first_taps_kernel, lines, comps, groups, cap),
        [
            sds((rows, nodes)), sds((rows, nodes)), sds((taps.shape[1], comps, LANES)),
            sds((rows, LANES)), sds((blocks, LANES), jnp.int32),
        ],
        [(taps, VMEM), (inlet, VMEM), (owners, VMEM), (offset, VMEM), (factor, VMEM)],
        flops=1e8,
    )

    def finish(looked):
        first = looked is None
        ins = [
            (local, VMEM), (carried, VMEM), (ends, VMEM), (first_ends, VMEM),
            (other_offset, VMEM), (other_factor, VMEM), (taps, VMEM), (inlet, VMEM),
        ]
        outs = [sds((rows, nodes))]
        if not first:
            ins += [(slot, VMEM), (looked, VMEM)]
            outs.append(sds((owners_total, 2 * half, LANES)))
        return call(
            functools.partial(finish_kernel, lines, comps, groups, cap, segs, segs != 2, first),
            outs, ins, flops=1e8 if first else 1,
        )

    (spread,) = finish(None)
    rates, send, onehot = call(
        functools.partial(look_first_kernel, groups, cap),
        [
            sds((owners_total, cap, LANES)), sds((owners_total, 2 * half + extra, LANES)),
            sds((wide, owners_total * cap * LANES), BF16),
        ],
        [
            (cell_recv, VMEM), (grid, VMEM), (kappa.reshape(cell_count // LANES, LANES), VMEM),
            (spread, VMEM), (slot, VMEM),
        ],
        scratch=[
            pltpu.VMEM((2 * (cell_count // wide) * comps, wide), BF16),
        ],
        flops=1e8,
    )
    looked = send
    coupling = slowness
    for step in range(STEPS):
        last = step == STEPS - 1
        got = exchange(send)
        masks = pltpu.VMEM(
            (
                min(4, owners_total // chunk), 2 * (cell_count // wide) * comps,
                chunk * cap * LANES,
            ),
            BF16,
        )
        if last:
            conc_out, grid = call(
                functools.partial(last_kernel, lines, comps, groups, cap, chunk),
                [sds(conc.shape), sds(grid.shape)],
                [
                    (spread, VMEM), (got, VMEM), (coupling, VMEM), (slot, VMEM),
                    (cell_recv, VMEM), (looked, VMEM), (rates, VMEM), (onehot, VMEM), (grid, VMEM),
                ],
                out_specs=[ANY, ANY],
                scratch=[
                    pltpu.VMEM(conc.shape, F32), pltpu.VMEM(grid.shape, F32), masks,
                    pltpu.SemaphoreType.DMA((2,)),
                ],
            )
            break
        outs = [sds((rows, nodes)), sds((1, comps, LANES))]
        if step == 0:
            outs.append(sds((blocks, LANES)))
        result = call(
            functools.partial(conc_kernel, lines, comps, groups, cap, step == 0),
            outs,
            [
                (spread, VMEM), (got, VMEM), (coupling, VMEM), (retain, VMEM), (levels, VMEM),
                (slot, VMEM),
            ],
        )
        if step == 0:
            coupling = result[-1]
        offset, ends = result[0], result[1]
        got_ends = swap(ends, segs)
        other_offset = got_ends if segs == 2 else got_ends[:, 0]
        (grid,) = call(
            functools.partial(update_kernel, cap, chunk),
            [sds(grid.shape)],
            [
                (cell_recv, VMEM), (got, VMEM), (looked, VMEM), (rates, VMEM), (onehot, VMEM),
                (grid, VMEM),
            ],
            scratch=[masks],
        )
        (looked,) = call(
            functools.partial(look_kernel, cap),
            [sds((owners_total, half, LANES))],
            [(cell_recv, VMEM), (onehot, VMEM), (grid, VMEM)],
            scratch=[pltpu.VMEM((2 * (cell_count // wide) * comps, wide), BF16)],
        )
        (local,) = call(
            functools.partial(taps_kernel, lines, comps, groups, 1),
            [sds((rows, nodes))],
            [(taps, VMEM), (offset, VMEM)],
        )
        spread, send = finish(looked)
    return (conc_out, grid)


def solution(mesh):
    return jax.shard_map(
        per_device,
        mesh=mesh,
        in_specs=(
            P("bundle", None, "seg"),
            P("bundle", "seg"),
            P(),
            P(),
            P("bundle", None),
            P(None, ("seg", "bundle")),
            P(("seg", "bundle")),
            P("seg", "bundle", None, None),
            P("bundle", "seg"),
        ),
        out_specs=(P("bundle", None, "seg"), P(None, ("seg", "bundle"))),
        check_vma=False,
    )
```

```python
import functools

import jax
import jax.numpy as jnp
from jax import lax
from jax.experimental import pallas as pl
from jax.experimental.pallas import tpu as pltpu
from jax.sharding import PartitionSpec as P

STEPS = 4
LANES = 128
HALF = 16
RADIX = 4
F32 = jnp.float32
BF16 = jnp.bfloat16

VMEM = pl.BlockSpec(memory_space=pltpu.VMEM)
SMEM = pl.BlockSpec(memory_space=pltpu.SMEM)
ANY = pl.BlockSpec(memory_space=pl.ANY)


def call(kernel, outs, ins, out_specs=None, scratch=(), flops=1, grant=40):
    args = [a for a, _ in ins]
    return pl.pallas_call(
        kernel,
        out_shape=outs,
        in_specs=[s for _, s in ins],
        out_specs=out_specs or [VMEM] * len(outs),
        scratch_shapes=list(scratch),
        cost_estimate=pl.CostEstimate(flops=int(flops), bytes_accessed=1, transcendentals=0),
        compiler_params=pltpu.CompilerParams(vmem_limit_bytes=grant * 1024 * 1024),
    )(*args)


def sds(shape, dtype=F32):
    return jax.ShapeDtypeStruct(shape, dtype)


def slots(owners, count, owners_total, lines, groups):
    for o in range(owners_total):
        count[o] = 0
    out = []
    for line in range(lines):
        for group in range(groups):
            owner = owners[0, line, 0, group]
            rank = count[owner]
            count[owner] = rank + 1
            out.append((owner, rank))
    return out


def route_kernel(groups, owners_in, cells_in, send, owners, cells, count, done):
    copies = [
        pltpu.make_async_copy(owners_in, owners, done.at[0]),
        pltpu.make_async_copy(cells_in, cells, done.at[1]),
    ]
    for copy in copies:
        copy.start()
    send[...] = jnp.full(send.shape, -1, jnp.int32)
    for copy in copies:
        copy.wait()
    for b, (owner, rank) in enumerate(slots(owners, count, send.shape[0], cells.shape[0], groups)):
        line, group = b // groups, b % groups
        send[owner, pl.ds(rank, 1), :] = cells[
            pl.ds(line, 1), group * LANES : (group + 1) * LANES
        ]


def where_slot(slot, b, cap):
    s = slot[b, 0]
    return s // cap, s % cap


def last_lane(x):
    return jnp.broadcast_to(x[:, LANES - 1 : LANES], x.shape)


def column(row, rows):
    square = (rows, rows)
    here = lax.broadcasted_iota(jnp.int32, square, 0) == lax.broadcasted_iota(jnp.int32, square, 1)
    values = jnp.sum(jnp.where(here, jnp.broadcast_to(row, square), 0.0), axis=1, keepdims=True)
    return jnp.broadcast_to(values, (rows, LANES))


def tile(ref, line, comps, group):
    return ref[pl.ds(line * comps, comps), group * LANES : (group + 1) * LANES]


def put(ref, line, comps, group, value):
    ref[pl.ds(line * comps, comps), group * LANES : (group + 1) * LANES] = value


def level_rows(levels, level, line, comps, group):
    return levels[level, pl.ds(line * comps, comps), group * LANES : (group + 1) * LANES]


LEVELS = 7
TOGETHER = (
    ((0, 1), (1, 2), (LEVELS + 2, 3)),
    ((2, 4), (3, 8), (LEVELS + 3, 12)),
    ((4, 16), (5, 32), (LEVELS + 4, 48)),
    ((6, 64),),
)


def scan_lines(levels, retain, values, lines, comps, groups):
    blocks = [(line, group) for line in range(lines) for group in range(groups)]
    offsets = [
        (1.0 - tile(retain, line, comps, group)) * values[line * groups + group]
        for line, group in blocks
    ]
    for terms in TOGETHER:
        offsets = [
            offset
            + sum(
                level_rows(levels, at, line, comps, group) * pltpu.roll(offset, shift, 1)
                for at, shift in terms
            )
            for offset, (line, group) in zip(offsets, blocks)
        ]
    out = []
    for line in range(lines):
        own = offsets[line * groups : (line + 1) * groups]
        carry = last_lane(own[0])
        done = [own[0]]
        for group in range(1, groups):
            done.append(own[group] + level_rows(levels, LEVELS, line, comps, group) * carry)
            if group < groups - 1:
                carry = (
                    last_lane(own[group])
                    + level_rows(levels, LEVELS + 1, line, comps, group) * carry
                )
        out.append(done)
    return out


def tap_columns(wide_taps):
    return [wide_taps[t] for t in range(wide_taps.shape[0])]


def correlate(tiles, columns, lane):
    count = len(tiles)
    shifted = [tiles]
    for b in range(1, RADIX):
        row = []
        for j in range(count):
            x = tiles[j]
            y = jnp.where(lane < b, tiles[j + 1] if j + 1 < count else 0.0, x)
            row.append(pltpu.roll(y, LANES - b, 1))
        shifted.append(row)
    early = [None] + [
        jnp.where(lane >= LANES - b, pltpu.roll(tiles[0], LANES - b, 1), 0.0) for b in range(1, RADIX)
    ]

    def mix(a, values):
        total = None
        for b in range(RADIX):
            t = RADIX * a + b + HALF
            if t < len(columns) and values[b] is not None:
                term = columns[t] * values[b]
                total = term if total is None else total + term
        return total

    spans = range(-(HALF // RADIX), HALF // RADIX + 1)
    outs = [None] * count
    for a in spans:
        parts = [mix(a, [shifted[b][j] for b in range(RADIX)]) for j in range(count)]
        for j in range(count):
            if a == 0:
                y = parts[j]
            elif a > 0:
                after = parts[j + 1] if j + 1 < count else 0.0
                y = pltpu.roll(jnp.where(lane < RADIX * a, after, parts[j]), LANES - RADIX * a, 1)
            else:
                before = parts[j - 1] if j else mix(a, early)
                y = pltpu.roll(
                    jnp.where(lane >= LANES + RADIX * a, before, parts[j]), -RADIX * a, 1
                )
            outs[j] = y if outs[j] is None else outs[j] + y
    return outs


def correlate_ring(x, columns):
    shifted = [x] + [pltpu.roll(x, LANES - b, 1) for b in range(1, RADIX)]
    out = None
    for a in range(-(HALF // RADIX), HALF // RADIX + 1):
        total = None
        for b in range(RADIX):
            t = RADIX * a + b + HALF
            if t < len(columns):
                term = columns[t] * shifted[b]
                total = term if total is None else total + term
        if a:
            total = pltpu.roll(total, (-RADIX * a) % LANES, 1)
        out = total if out is None else out + total
    return out


def pack_ends(line, lane, first, last):
    at = 2 * HALF * line
    both = jnp.where(lane < LANES // 2, first, last)
    both = pltpu.roll(both, (HALF + at) % LANES, 1)
    return both, (lane >= at) & (lane < at + 2 * HALF)


def unpack_ends(line, packed):
    return pltpu.roll(packed, (-(HALF + 2 * HALF * line)) % LANES, 1)


def first_kernel(
    lines, comps, groups, conc, slowness, retard, retain, levels, offset, factor, ends
):
    lane = lax.broadcasted_iota(jnp.int32, (comps, LANES), 1)
    slow_by = column(retard[...], comps)
    packed = [jnp.zeros((comps, LANES), F32)] * 2
    values, wholes = [], []
    for line in range(lines):
        whole = []
        for group in range(groups):
            s = slowness[pl.ds(line, 1), group * LANES : (group + 1) * LANES]
            r = 1.0 / (1.0 + slow_by * s)
            put(retain, line, comps, group, r)
            rows = pl.ds(line * comps, comps)
            span = slice(group * LANES, (group + 1) * LANES)
            f = r
            for level in range(LEVELS):
                inside = lane >= (1 << level)
                masked = jnp.where(inside, f, 0.0)
                levels[level, rows, span] = masked
                if level % 2:
                    levels[LEVELS + 2 + level // 2, rows, span] = masked * pltpu.roll(
                        shorter, 1 << level, 1
                    )
                shorter = masked
                f = jnp.where(inside, f * pltpu.roll(f, 1 << level, 1), f)
            levels[LEVELS, rows, span] = f
            end = last_lane(f)
            levels[LEVELS + 1, rows, span] = end
            if group:
                f = f * carry
                carry = carry * end
            else:
                carry = end
            put(factor, line, comps, group, f)
            whole.append(f)
            values.append(conc[line, :, span])
        wholes.append(whole)
    for line, offsets in enumerate(scan_lines(levels, retain, values, lines, comps, groups)):
        whole = wholes[line]
        for group in range(groups):
            put(offset, line, comps, group, offsets[group])
        part, inside = pack_ends(line, lane, offsets[0], offsets[-1])
        packed[0] = jnp.where(inside, part, packed[0])
        part, inside = pack_ends(line, lane, whole[0], whole[-1])
        packed[1] = jnp.where(inside, part, packed[1])
    ends[0] = packed[0]
    ends[1] = packed[1]


def taps_kernel(lines, comps, groups, sources, taps, *refs):
    lane = lax.broadcasted_iota(jnp.int32, (comps, LANES), 1)
    columns = tap_columns(taps)
    for source, out in zip(refs[:sources], refs[sources:]):
        for line in range(lines):
            tiles = [tile(source, line, comps, group) for group in range(groups)]
            sums = correlate(tiles, columns, lane)
            for group in range(groups):
                put(out, line, comps, group, tiles[group] + sums[group])


def place(send, slot, b, cap, comps, value):
    owner, rank = where_slot(slot, b, cap)
    send[owner, pl.ds(pl.multiple_of((cap + rank) * comps, 8), comps), :] = value


def first_taps_kernel(
    lines, comps, groups, cap, taps, inlet, owners, offset, factor,
    local, carried, wide_taps, wide_inlet, slot,
):
    for t in range(taps.shape[1]):
        wide_taps[t] = jnp.broadcast_to(taps[:, t : t + 1], (comps, LANES))
    for line in range(lines):
        wide_inlet[pl.ds(line * comps, comps), :] = column(inlet[line : line + 1, :], comps)
    blocks = lines * groups
    square = (blocks, blocks)
    row = jnp.concatenate([owners[0, line].astype(F32) for line in range(lines)], axis=1)
    own = column(row, blocks)[:, :blocks]
    earlier = lax.broadcasted_iota(jnp.int32, square, 1) < lax.broadcasted_iota(jnp.int32, square, 0)
    same = jnp.where(earlier & (own == jnp.broadcast_to(row, square)), 1.0, 0.0)
    at = own[:, :1] * cap + jnp.sum(same, axis=1, keepdims=True)
    slot[...] = jnp.broadcast_to(at, (blocks, LANES)).astype(jnp.int32)
    taps_kernel(lines, comps, groups, 2, wide_taps, offset, factor, local, carried)


def finish_kernel(
    lines, comps, groups, cap, segs, has_gather, first,
    local, carried, end_offset, end_factor, other_offset, other_factor, taps, inlet, *rest,
):
    if first:
        (spread,) = rest
    else:
        slot, looked, spread, send = rest
    me = lax.axis_index("seg")
    lane = lax.broadcasted_iota(jnp.int32, (comps, LANES), 1)
    columns = tap_columns(taps)
    for line in range(lines):
        rows = pl.ds(line * comps, comps)

        def part(s):
            if has_gather:
                pair = other_offset[s], other_factor[s]
            else:
                mine = me == s
                pair = (
                    jnp.where(mine, end_offset[0], other_offset[0]),
                    jnp.where(mine, end_factor[1], other_factor[1]),
                )
            return [unpack_ends(line, x) for x in pair]

        flow = inlet[rows, :]
        zero = jnp.zeros((comps, LANES), F32)
        left, right, inflow = zero, zero, zero
        for s in range(segs):
            inflow = jnp.where(me == s, flow, inflow)
            off, fac = part(s)
            edge = off + fac * flow
            left = jnp.where(me == s + 1, edge, left)
            right = jnp.where(me == s - 1, edge, right)
            if s < segs - 1:
                flow = last_lane(edge)
        ring = jnp.where(lane >= LANES - HALF, left, 0.0)
        ring = jnp.where((lane >= 48) & (lane < 48 + HALF), pltpu.roll(right, 48, 1), ring)
        ring = correlate_ring(ring, columns)
        for group in range(groups):
            total = tile(local, line, comps, group) + tile(carried, line, comps, group) * inflow
            if group == 0:
                total = total + jnp.where(lane < HALF, ring, 0.0)
            if group == groups - 1:
                total = total + jnp.where(lane >= LANES - HALF, pltpu.roll(ring, 80, 1), 0.0)
            put(spread, line, comps, group, total)
    if first:
        return
    send[:, 0 : cap * comps, :] = looked[...]
    for b in range(lines * groups):
        place(send, slot, b, cap, comps, tile(spread, b // groups, comps, b % groups))


def conc_kernel(lines, comps, groups, cap, first, spread, got, coupling, retain, levels, slot, *outs):
    lane = lax.broadcasted_iota(jnp.int32, (comps, LANES), 1)
    values = []
    for b in range(lines * groups):
        line, group = b // groups, b % groups
        owner, rank = where_slot(slot, b, cap)
        looked = got[owner, pl.ds(pl.multiple_of(rank * comps, 8), comps), :]
        if first:
            rate = got[owner, pl.ds(2 * cap * comps + rank, 1), :]
            outs[2][b : b + 1, :] = rate
        else:
            rate = coupling[b : b + 1, :]
        s = tile(spread, line, comps, group)
        values.append(s + rate * (looked - s))
    packed = jnp.zeros((comps, LANES), F32)
    for line, offsets in enumerate(scan_lines(levels, retain, values, lines, comps, groups)):
        for group in range(groups):
            put(outs[0], line, comps, group, offsets[group])
        part, inside = pack_ends(line, lane, offsets[0], offsets[-1])
        packed = jnp.where(inside, part, packed)
    outs[1][0] = packed


def look_by_matmul(cells, cap, onehot, stack, first, count, high_total, wide):
    rows = stack.shape[0] // 2
    comps = rows // high_total
    bits = wide.bit_length() - 1
    part = jnp.dot(
        stack[...], onehot[:, first * LANES : (first + count) * LANES], preferred_element_type=F32
    )
    out = []
    for i in range(count):
        owner, rank = (first + i) // cap, (first + i) % cap
        cell = jnp.maximum(cells[owner, rank : rank + 1, :], 0)
        high = jnp.broadcast_to(cell >> bits, (comps, LANES))
        span = slice(i * LANES, (i + 1) * LANES)
        found = jnp.zeros((comps, LANES), F32)
        for h in range(high_total):
            at = slice(h * comps, (h + 1) * comps)
            at2 = slice(rows + h * comps, rows + (h + 1) * comps)
            found = jnp.where(high == h, part[at, span] + part[at2, span], found)
        out.append(found)
    return out


def in_two(x):
    coarse = x.astype(BF16)
    return coarse, (x - coarse.astype(F32)).astype(BF16)


def stack_grid(grid, stack, wide):
    comps = grid.shape[0]
    rows = stack.shape[0] // 2
    for h in range(grid.shape[1] // wide):
        coarse, fine = in_two(grid[:, h * wide : (h + 1) * wide])
        stack[h * comps : (h + 1) * comps, :] = coarse
        stack[rows + h * comps : rows + (h + 1) * comps, :] = fine


def put_onehot(onehot, at, cell):
    wide = onehot.shape[0]
    row = lax.broadcasted_iota(jnp.int32, (wide, LANES), 0)
    onehot[:, at : at + LANES] = jnp.where(row == (cell & (wide - 1)), 1.0, 0.0).astype(BF16)


def look_first_kernel(groups, cap, cells, grid, kappa, spread, slot, rates, send, onehot, stack):
    comps = grid.shape[0]
    wide = onehot.shape[0]
    high_total = grid.shape[1] // LANES
    slots_total = cells.shape[0] * cap
    row = lax.broadcasted_iota(jnp.int32, (high_total, LANES), 0)
    stack_grid(grid, stack, wide)
    for s in range(slots_total):
        put_onehot(onehot, s * LANES, cells[s // cap, s % cap : s % cap + 1, :])
    for s in range(slots_total):
        owner, rank = s // cap, s % cap
        cell = cells[owner, rank : rank + 1, :]
        valid = cell >= 0
        cell = jnp.maximum(cell, 0)
        low = jnp.broadcast_to(cell & (LANES - 1), (high_total, LANES))
        k = jnp.take_along_axis(kappa[...], low, axis=1, mode="promise_in_bounds")
        rate = jnp.sum(jnp.where(row == (cell >> 7), k, 0.0), axis=0, keepdims=True)
        rate = jnp.where(valid, rate, 0.0)
        rates[owner, rank : rank + 1, :] = rate
        at = 2 * cap * comps + rank
        send[owner, at : at + 1, :] = rate
    for first in range(0, slots_total, 4):
        found = look_by_matmul(cells, cap, onehot, stack, first, 4, grid.shape[1] // wide, wide)
        for i in range(4):
            owner, rank = (first + i) // cap, (first + i) % cap
            send[owner, rank * comps : (rank + 1) * comps, :] = found[i]
    for b in range(slot.shape[0]):
        place(send, slot, b, cap, comps, tile(spread, b // groups, comps, b % groups))


def update_kernel(cap, chunk, cells, got, looked, rates, onehot, grid, grid_out, masked):
    comps = grid.shape[0]
    wide = onehot.shape[0]
    bits = wide.bit_length() - 1
    high_total = grid.shape[1] // wide
    owners_total = cells.shape[0]
    rows = high_total * comps
    width = chunk * cap * LANES
    total = None
    for start in range(0, owners_total, chunk):
        turn = (start // chunk) % masked.shape[0]
        for i in range(chunk):
            owner = start + i
            for rank in range(cap):
                at = (i * cap + rank) * LANES
                cell = cells[owner, rank : rank + 1, :]
                valid = jnp.broadcast_to(cell, (comps, LANES)) >= 0
                cell = jnp.maximum(cell, 0)
                rate = rates[owner, rank : rank + 1, :]
                span = slice(rank * comps, (rank + 1) * comps)
                came = slice((cap + rank) * comps, (cap + rank + 1) * comps)
                flux = jnp.where(valid, rate * (looked[owner, span, :] - got[owner, came, :]), 0.0)
                coarse, fine = in_two(flux)
                high = jnp.broadcast_to((cell >> bits).astype(F32), (comps, LANES)).astype(BF16)
                for h in range(high_total):
                    hit = high == jnp.asarray(h, BF16)
                    masked[turn, h * comps : (h + 1) * comps, at : at + LANES] = jnp.where(
                        hit, coarse, jnp.zeros_like(coarse)
                    )
                    masked[turn, rows + h * comps : rows + (h + 1) * comps, at : at + LANES] = (
                        jnp.where(hit, fine, jnp.zeros_like(fine))
                    )
        first = start * cap * LANES
        part = lax.dot_general(
            masked[turn], onehot[:, first : first + width], (((1,), (1,)), ((), ())),
            preferred_element_type=F32,
        )
        total = part if total is None else total + part
    for h in range(high_total):
        span = slice(h * wide, (h + 1) * wide)
        at = slice(h * comps, (h + 1) * comps)
        at2 = slice(rows + h * comps, rows + (h + 1) * comps)
        grid_out[:, span] = grid[:, span] - 0.25 * (total[at, :] + total[at2, :])


def look_kernel(cap, cells, onehot, grid, looked, stack):
    comps = grid.shape[0]
    wide = onehot.shape[0]
    stack_grid(grid, stack, wide)
    for first in range(0, cells.shape[0] * cap, 4):
        found = look_by_matmul(cells, cap, onehot, stack, first, 4, grid.shape[1] // wide, wide)
        for i in range(4):
            owner, rank = (first + i) // cap, (first + i) % cap
            looked[owner, rank * comps : (rank + 1) * comps, :] = found[i]


def last_kernel(
    lines, comps, groups, cap, chunk,
    spread, came, coupling, slot, cells, looked, rates, onehot, grid,
    conc_out, grid_out, conc, grid_new, masked, done,
):
    for b in range(lines * groups):
        line, group = b // groups, b % groups
        owner, rank = where_slot(slot, b, cap)
        found = came[owner, pl.ds(pl.multiple_of(rank * comps, 8), comps), :]
        s = tile(spread, line, comps, group)
        value = s + coupling[b : b + 1, :] * (found - s)
        conc[line, :, group * LANES : (group + 1) * LANES] = value
    first = pltpu.make_async_copy(conc, conc_out, done.at[0])
    first.start()
    update_kernel(cap, chunk, cells, came, looked, rates, onehot, grid, grid_new, masked)
    second = pltpu.make_async_copy(grid_new, grid_out, done.at[1])
    second.start()
    first.wait()
    second.wait()


def swap(x, segs):
    if segs == 2:
        return lax.ppermute(x, "seg", [(0, 1), (1, 0)])
    return lax.all_gather(x, "seg")


def exchange(x):
    return lax.all_to_all(x, "bundle", split_axis=0, concat_axis=0, tiled=True)


def per_device(conc, slowness, retard, taps, inlet, grid, kappa, owners, cells):
    lines, comps, nodes = conc.shape
    groups = nodes // LANES
    blocks = lines * groups
    segs = lax.axis_size("seg")
    owners_total = lax.axis_size("bundle")
    cap = max(2, 2 * blocks // owners_total)
    rows = lines * comps
    cell_count = grid.shape[1]
    chunk = 4 if owners_total % 4 == 0 else owners_total
    half = cap * comps
    extra = 8 * (-(-cap // 8))
    wide = 256 if cell_count % 256 == 0 else LANES

    owners = jnp.swapaxes(owners, 2, 3)
    (cell_send,) = call(
        functools.partial(route_kernel, groups),
        [sds((owners_total, cap, LANES), jnp.int32)],
        [(owners, ANY), (cells, ANY)],
        scratch=[
            pltpu.VMEM((1, lines, 1, groups), jnp.int32), pltpu.VMEM((lines, nodes), jnp.int32),
            pltpu.SMEM((owners_total,), jnp.int32), pltpu.SemaphoreType.DMA((2,)),
        ],
        grant=58,
        flops=1e9,
    )
    cell_recv = exchange(cell_send)

    retain, levels, offset, factor, ends = call(
        functools.partial(first_kernel, lines, comps, groups),
        [
            sds((rows, nodes)), sds((LEVELS + 5, rows, nodes)), sds((rows, nodes)),
            sds((rows, nodes)), sds((2, comps, LANES)),
        ],
        [(conc, VMEM), (slowness, VMEM), (retard.reshape(1, comps), VMEM)],
        flops=1e8,
    )
    first_ends = ends
    other = swap(ends, segs)
    if segs == 2:
        other_offset = other_factor = other
    else:
        other_offset, other_factor = other[:, 0], other[:, 1]
    local, carried, taps, inlet, slot = call(
        functools.partial(first_taps_kernel, lines, comps, groups, cap),
        [
            sds((rows, nodes)), sds((rows, nodes)), sds((taps.shape[1], comps, LANES)),
            sds((rows, LANES)), sds((blocks, LANES), jnp.int32),
        ],
        [(taps, VMEM), (inlet, VMEM), (owners, VMEM), (offset, VMEM), (factor, VMEM)],
        flops=1e8,
    )

    def finish(looked):
        first = looked is None
        ins = [
            (local, VMEM), (carried, VMEM), (ends, VMEM), (first_ends, VMEM),
            (other_offset, VMEM), (other_factor, VMEM), (taps, VMEM), (inlet, VMEM),
        ]
        outs = [sds((rows, nodes))]
        if not first:
            ins += [(slot, VMEM), (looked, VMEM)]
            outs.append(sds((owners_total, 2 * half, LANES)))
        return call(
            functools.partial(finish_kernel, lines, comps, groups, cap, segs, segs != 2, first),
            outs, ins, flops=1e8 if first else 1,
        )

    (spread,) = finish(None)
    rates, send, onehot = call(
        functools.partial(look_first_kernel, groups, cap),
        [
            sds((owners_total, cap, LANES)), sds((owners_total, 2 * half + extra, LANES)),
            sds((wide, owners_total * cap * LANES), BF16),
        ],
        [
            (cell_recv, VMEM), (grid, VMEM), (kappa.reshape(cell_count // LANES, LANES), VMEM),
            (spread, VMEM), (slot, VMEM),
        ],
        scratch=[
            pltpu.VMEM((2 * (cell_count // wide) * comps, wide), BF16),
        ],
        flops=1e8,
    )
    looked = send
    coupling = slowness
    for step in range(STEPS):
        last = step == STEPS - 1
        got = exchange(send)
        masks = pltpu.VMEM(
            (
                min(4, owners_total // chunk), 2 * (cell_count // wide) * comps,
                chunk * cap * LANES,
            ),
            BF16,
        )
        if last:
            conc_out, grid = call(
                functools.partial(last_kernel, lines, comps, groups, cap, chunk),
                [sds(conc.shape), sds(grid.shape)],
                [
                    (spread, VMEM), (got, VMEM), (coupling, VMEM), (slot, VMEM),
                    (cell_recv, VMEM), (looked, VMEM), (rates, VMEM), (onehot, VMEM), (grid, VMEM),
                ],
                out_specs=[ANY, ANY],
                scratch=[
                    pltpu.VMEM(conc.shape, F32), pltpu.VMEM(grid.shape, F32), masks,
                    pltpu.SemaphoreType.DMA((2,)),
                ],
            )
            break
        outs = [sds((rows, nodes)), sds((1, comps, LANES))]
        if step == 0:
            outs.append(sds((blocks, LANES)))
        result = call(
            functools.partial(conc_kernel, lines, comps, groups, cap, step == 0),
            outs,
            [
                (spread, VMEM), (got, VMEM), (coupling, VMEM), (retain, VMEM), (levels, VMEM),
                (slot, VMEM),
            ],
        )
        if step == 0:
            coupling = result[-1]
        offset, ends = result[0], result[1]
        got_ends = swap(ends, segs)
        other_offset = got_ends if segs == 2 else got_ends[:, 0]
        (grid,) = call(
            functools.partial(update_kernel, cap, chunk),
            [sds(grid.shape)],
            [
                (cell_recv, VMEM), (got, VMEM), (looked, VMEM), (rates, VMEM), (onehot, VMEM),
                (grid, VMEM),
            ],
            scratch=[masks],
        )
        (looked,) = call(
            functools.partial(look_kernel, cap),
            [sds((owners_total, half, LANES))],
            [(cell_recv, VMEM), (onehot, VMEM), (grid, VMEM)],
            scratch=[pltpu.VMEM((2 * (cell_count // wide) * comps, wide), BF16)],
        )
        (local,) = call(
            functools.partial(taps_kernel, lines, comps, groups, 1),
            [sds((rows, nodes))],
            [(taps, VMEM), (offset, VMEM)],
        )
        spread, send = finish(looked)
    return (conc_out, grid)


def solution(mesh):
    return jax.shard_map(
        per_device,
        mesh=mesh,
        in_specs=(
            P("bundle", None, "seg"),
            P("bundle", "seg"),
            P(),
            P(),
            P("bundle", None),
            P(None, ("seg", "bundle")),
            P(("seg", "bundle")),
            P("seg", "bundle", None, None),
            P("bundle", "seg"),
        ),
        out_specs=(P("bundle", None, "seg"), P(None, ("seg", "bundle"))),
        check_vma=False,
    )
```
